32 devices in a mesh: seq: 8 (over z, x), dp: 4 (over y, core).
Axes of the slice: x: 2, y: 2, z: 4, core: 2. Of those that a mesh axis runs over, the one named last changes fastest.
Arguments:
- tokens: bfloat16 [4, 2048, 1024], P('dp', 'seq'), may hold values from -6 to 6
- attn_gain: bfloat16 [1024], P(('seq', 'dp')), may hold values from 0.099609375 to 1.8984375
- query_weight: bfloat16 [1024, 256], P(('seq', 'dp')), may hold values from -0.1875 to 0.1875
- key_weight: bfloat16 [1024, 256], P(('seq', 'dp')), may hold values from -0.1875 to 0.1875
- value_weight: bfloat16 [1024, 1024], P(('seq', 'dp')), may hold values from -0.1875 to 0.1875
- out_weight: bfloat16 [1024, 1024], P(None, ('seq', 'dp')), may hold values from -3 to 3
- ffn_gain: bfloat16 [1024], P(('seq', 'dp')), may hold values from 0.099609375 to 1.8984375
- gate_weight: bfloat16 [1024, 2752], P(('seq', 'dp')), may hold values from -0.1875 to 0.1875
- up_weight: bfloat16 [1024, 2752], P(('seq', 'dp')), may hold values from -0.1875 to 0.1875
- down_weight: bfloat16 [2752, 1024], P(None, ('seq', 'dp')), may hold values from -0.109375 to 0.109375
- cotangent: bfloat16 [4, 2048, 1024], P('dp', 'seq'), may hold values from -6 to 6
Outputs:
- output: bfloat16 [4, 2048, 1024], P('dp', 'seq')
- input_grad: float32 [4, 2048, 1024], P('dp', 'seq')
- attn_gain_grad: float32 [1024], P(('seq', 'dp'))
- query_grad: float32 [1024, 256], P(('seq', 'dp'))
- key_grad: float32 [1024, 256], P(('seq', 'dp'))
- value_grad: float32 [1024, 1024], P(('seq', 'dp'))
- out_grad: float32 [1024, 1024], P(None, ('seq', 'dp'))
- ffn_gain_grad: float32 [1024], P(('seq', 'dp'))
- gate_grad: float32 [1024, 2752], P(('seq', 'dp'))
- up_grad: float32 [1024, 2752], P(('seq', 'dp'))
- down_grad: float32 [2752, 1024], P(None, ('seq', 'dp'))
The draws below stay inside these ranges and needn't reach their ends.
All inputs are finite; a program needn't handle non-finite values.
Results may differ from the reference program's by a relative error of at most 0.017.
Values may be sent and summed in bfloat16 or wider, within the bound.
A program may use at most 320 MiB of HBM per device.

```python
import jax
import jax.numpy as jnp
from jax import lax

D = 1024
FF = 2752
HEADS = 16
FDIM = 16
VDIM = 64
BLOCK = 256
FEAT = 273
QK_WIDTH = 256
V_WIDTH = 1024
BATCH = 4
LENGTH = 2048


def strengthened(entries, key, source, target, parts, factor):
    def block_of(axis_at):
        return (jnp.arange(entries.shape[axis_at]) // (entries.shape[axis_at] // parts)).reshape((-1,) + (1,) * (entries.ndim - 1 - axis_at))

    first = jax.random.permutation(key, parts)[block_of(target)]
    second = (block_of(target) + parts // 2) % parts
    return jnp.where((block_of(source) == first) | (block_of(source) == second), factor * entries, entries)


def shard_levels(key, shape, cuts, low, top_value):
    factor_of = 1.0
    for position, parts in cuts:
        steps = jax.random.uniform(jax.random.fold_in(jax.random.fold_in(key, 6), position), (parts,), jnp.float32, low / len(cuts), top_value / len(cuts))
        factor_of = factor_of * jnp.repeat(jnp.exp(steps), shape[position] // parts).reshape((-1,) + (1,) * (len(shape) - 1 - position))
    return factor_of


def scatter_about(key, extent, spread, reach, split=(), kind=jnp.bfloat16):
    array = spread * jax.random.normal(key, extent, jnp.float32)
    if split:
        array = array * shard_levels(key, extent, split, -0.22, 0.18)
    return jnp.clip(array, -reach, reach).astype(kind)


def gaussian_with(own_key, shape, spread, limit, shards, heavy, held_as=jnp.bfloat16):
    drawn = spread * jax.random.normal(own_key, shape, jnp.float32)
    if shards:
        drawn = drawn * shard_levels(own_key, shape, shards, -0.22, 0.18)
    return jnp.clip(strengthened(drawn, jax.random.fold_in(own_key, 3), *heavy), -limit, limit).astype(held_as)


def setup_inputs(seed: int = 0) -> dict:
    seeds = jax.random.split(jax.random.key(seed), 12)
    return {
        "tokens": scatter_about(seeds[0], (BATCH, LENGTH, D), 1.0, 6.0, ((0, 4), (1, 8))),
        "attn_gain": jnp.clip(1.0 + 0.18 * jax.random.normal(seeds[1], (D,), jnp.float32), 0.099609375, 1.8984375).astype(jnp.bfloat16),
        "query_weight": scatter_about(seeds[2], (D, QK_WIDTH), D ** -0.5, 0.1875, ((0, 32),)),
        "key_weight": scatter_about(seeds[3], (D, QK_WIDTH), D ** -0.5, 0.1875, ((0, 32),)),
        "value_weight": scatter_about(seeds[4], (D, V_WIDTH), D ** -0.5, 0.1875, ((0, 32),)),
        "out_weight": scatter_about(seeds[5], (V_WIDTH, D), (max(V_WIDTH // 256, 1)) ** -0.5, 3.0, ((1, 32),)),
        "ffn_gain": jnp.clip(1.0 + 0.18 * jax.random.normal(seeds[6], (D,), jnp.float32), 0.099609375, 1.8984375).astype(jnp.bfloat16),
        "gate_weight": scatter_about(seeds[7], (D, FF), D ** -0.5, 0.1875, ((0, 32),)),
        "up_weight": scatter_about(seeds[8], (D, FF), D ** -0.5, 0.1875, ((0, 32),)),
        "down_weight": scatter_about(seeds[9], (FF, D), FF ** -0.5, 0.109375, ((1, 32),)),
        "cotangent": gaussian_with(seeds[10], (BATCH, LENGTH, D), 1.0, 6.0, ((0, 4), (1, 8)), (1, 2, 8, 2.0)),
    }


epsilon = 1e-05
highest = lax.Precision.HIGHEST

@jax.custom_vjp
def low(v):
    return lax.optimization_barrier(v.astype(jnp.bfloat16)).astype(jnp.float32)

@jax.custom_vjp
def low_back(v):
    return v

def low_keep(v):
    return (low(v), None)

def low_pass(kept, grad):
    return (grad,)

def back_keep(v):
    return (v, None)

def back_low(kept, grad):
    return (low(grad),)
low.defvjp(low_keep, low_pass)
low_back.defvjp(back_keep, back_low)

def matmul(left, right):
    return jnp.dot(left, right, precision=highest, preferred_element_type=jnp.float32)

def taylor(vector):
    feature_dim = vector.shape[-1]
    leading = vector.shape[:-1]
    constant = jnp.ones(leading + (1,), vector.dtype)
    product = (vector[..., :, None] * vector[..., None, :]).reshape(leading + (feature_dim * feature_dim,))
    return jnp.concatenate([constant, vector * feature_dim ** (-0.25), product * (2.0 * feature_dim) ** (-0.5)], axis=-1)

def exclusive(series):
    return jnp.concatenate([jnp.zeros_like(series[:1]), jnp.cumsum(series[:-1], axis=0)], axis=0)

def layer(source, params):
    attn_gain, query_weight, key_weight, value_weight, out_weight, ffn_gain, gate_weight, up_weight, down_weight = params
    blocks = LENGTH // BLOCK
    scale_one = lax.rsqrt(lax.optimization_barrier(jnp.mean(source * source, axis=-1, keepdims=True)) + epsilon)
    normed = low(source * scale_one * attn_gain)
    query = low_back(matmul(normed, query_weight)).reshape(LENGTH, HEADS, FDIM)
    keyvec = low_back(matmul(normed, key_weight)).reshape(LENGTH, HEADS, FDIM)
    values = low(low_back(matmul(normed, value_weight))).reshape(blocks, BLOCK, HEADS, VDIM)
    feat_q = low(taylor(query)).reshape(blocks, BLOCK, HEADS, FEAT)
    feat_k = low(taylor(keyvec)).reshape(blocks, BLOCK, HEADS, FEAT)
    scores = low(low_back(jnp.einsum('nihf,njhf->nhij', feat_q, feat_k, precision=highest)))
    units = low_back(jnp.einsum('njhf,njhd->nhfd', feat_k, values, precision=highest))
    counts = lax.optimization_barrier(jnp.sum(feat_k, axis=1))
    prefix = low(exclusive(units))
    prior = low(exclusive(counts))
    numer = jnp.einsum('nhij,njhd->nihd', scores, values, precision=highest)
    numer = low_back(numer + jnp.einsum('nihf,nhfd->nihd', feat_q, prefix, precision=highest))
    denom = jnp.transpose(lax.optimization_barrier(jnp.sum(scores, axis=-1)), (0, 2, 1))
    denom = low_back(denom + jnp.einsum('nihf,nhf->nih', feat_q, prior, precision=highest))
    attended = low(numer / denom[..., None]).reshape(LENGTH, V_WIDTH)
    middle = source + low_back(matmul(attended, out_weight))
    scale_two = lax.rsqrt(lax.optimization_barrier(jnp.mean(middle * middle, axis=-1, keepdims=True)) + epsilon)
    normed_two = low(middle * scale_two * ffn_gain)
    gate = low_back(matmul(normed_two, gate_weight))
    upper = low_back(matmul(normed_two, up_weight))
    hidden = low(jax.nn.silu(gate) * upper)
    return middle + low_back(matmul(hidden, down_weight))

def reference(tokens, attn_gain, query_weight, key_weight, value_weight, out_weight, ffn_gain, gate_weight, up_weight, down_weight, cotangent):
    params = (attn_gain.astype(jnp.float32), query_weight.astype(jnp.float32), key_weight.astype(jnp.float32), value_weight.astype(jnp.float32), out_weight.astype(jnp.float32), ffn_gain.astype(jnp.float32), gate_weight.astype(jnp.float32), up_weight.astype(jnp.float32), down_weight.astype(jnp.float32))

    def one_sequence(totals, pair):
        source, grad_out = pair
        result, pullback = jax.vjp(layer, source, params)
        grad_source, grad_params = pullback(grad_out)
        totals = jax.tree.map(lambda left, right: left + right, totals, grad_params)
        return (totals, (result.astype(jnp.bfloat16), grad_source))
    start_totals = jax.tree.map(jnp.zeros_like, params)
    totals, outputs = lax.scan(one_sequence, start_totals, (tokens.astype(jnp.float32), cotangent.astype(jnp.float32)))
    return (outputs[0], outputs[1], totals[0], totals[1], totals[2], totals[3], totals[4], totals[5], totals[6], totals[7], totals[8])
```

```python
import jax
import jax.numpy as jnp
from jax import lax
from jax.experimental import pallas as pl
from jax.experimental.pallas import tpu as pltpu
from jax.sharding import PartitionSpec as P

HEADS = 16
FDIM = 16
VDIM = 64
EPS = 1e-05
LIN = FDIM**-0.25
QUAD = (2.0 * FDIM) ** -0.5
SHIFTS = FDIM // 2 + 1
FEATS = FDIM * (SHIFTS + 2)
HALF_HEADS = HEADS // 2
QH = HALF_HEADS * FDIM
VH = HALF_HEADS * VDIM
PAIRS = HALF_HEADS // 2
SLOTS = 2 * PAIRS + 1
LANES = 128
PIECE = 512
RING = 6
MESH = pl.DeviceIdType.MESH
F32 = jnp.float32
BF16 = jnp.bfloat16


def pieces_of(width):
    out, at = [], 0
    while at < width:
        out.append((at, min(PIECE, width - at)))
        at += PIECE
    return out


def tiles_of(width):
    out, at = [], 0
    while at < width:
        out.append((at, min(256, width - at)))
        at += 256
    return out


def nn(a, b):
    return jnp.dot(a, b, preferred_element_type=F32)


def nt(a, b):
    return lax.dot_general(a, b, (((1,), (1,)), ((), ())), preferred_element_type=F32)


def tn(a, b):
    return lax.dot_general(a, b, (((0,), (0,)), ((), ())), preferred_element_type=F32)


def ahead(t, d):
    return t if d == 0 else pltpu.roll(t, FDIM - d, 0)


def behind(t, d):
    return t if d == 0 else pltpu.roll(t, d, 0)


def times(d):
    return 1.0 if d in (0, FDIM // 2) else 2.0


def features(u):
    rows = [u * ahead(u, d) * QUAD for d in range(SHIFTS)]
    first = lax.broadcasted_iota(jnp.int32, u.shape, 0) == 0
    rows += [u * LIN, jnp.where(first, 1.0, 0.0)]
    return jnp.concatenate(rows, axis=0).astype(BF16)


def weighted(f):
    lo, hi = FDIM, FDIM * (SHIFTS - 1)
    return jnp.concatenate([f[:lo], f[lo:hi] * 2, f[hi:]], axis=0)


def features_back(u, df):
    at = FDIM * SHIFTS
    total = df[at : at + FDIM] * LIN
    for d in range(SHIFTS):
        t = df[FDIM * d : FDIM * (d + 1)] * (QUAD * times(d))
        total = total + t * ahead(u, d) + behind(t * u, d)
    return total


def split_low(u):
    high = u.astype(BF16)
    return high, (u - high.astype(F32)).astype(BF16)


def plan(ff_half):
    parts = pieces_of(ff_half)
    gather = [("gain", LANES), ("qkv", 2 * QH + VH), ("out", VH)]
    gather += [(f"gu{j}", 2 * w) for j, (_, w) in enumerate(parts)]
    gather += [(f"d{j}", w) for j, (_, w) in enumerate(parts)]
    reduce = [(f"d{j}", w) for j, (_, w) in enumerate(parts)]
    for j, (_, w) in enumerate(parts):
        reduce += [(f"g{j}", w), (f"u{j}", w)]
    reduce += [("out", VH), ("qk", 2 * QH), ("v", VH), ("gain", LANES)]
    return gather, reduce


def make_kernel(seq_size, block, width, ff_half):
    gather, reduce = plan(ff_half)
    parts = pieces_of(ff_half)
    n_parts = len(parts)
    gi = {name: i for i, (name, _) in enumerate(gather)}
    ri = {name: i for i, (name, _) in enumerate(reduce)}
    members = seq_size // 8
    n_hi = seq_size // 2
    rows = width // 32
    rows2 = 2 * rows
    quarter = width // 4
    offsets = []
    total_width = 0
    for _, w in reduce:
        offsets.append(total_width)
        total_width += w
    n_hops = 4

    def kernel(*refs):
        it = iter(refs)
        take = lambda n: [next(it) for _ in range(n)]
        tok, cot = take(2)
        wp = take(len(gather))
        out_ref, din_ref = take(2)
        go = take(len(reduce))
        W = take(len(gather))
        G = take(len(reduce))
        (R1, R2, R3, FS, X, DY, NB, N1T, N2T, DYT, HID, CA, CB, X1, SND, RCV, OWN) = take(17)
        (NUM, DATT, QK, VT, ATT, DEN, DNUM, DDEN, DQK, DV, DQKV) = take(11)
        (ST, STXS, STSS, STO, PB, PX, WACC, TG, TU, GROW, GACC) = take(11)
        ss, rs, ls, bar2 = take(4)
        del bar2

        s, dp = lax.axis_index("seq"), lax.axis_index("dp")
        hi, x = s // 2, lax.rem(s, 2)
        y, c = dp // 2, lax.rem(dp, 2)
        g, m = hi // members, lax.rem(hi, members)
        o = 1 - c
        ax, ay = x + o * (1 - 2 * x), y + c * (1 - 2 * y)
        bx, by = x + c * (1 - 2 * x), y + o * (1 - 2 * y)
        p, pa = 2 * x + y, 2 * ax + ay
        pb, pab = 2 * bx + by, 2 * (1 - x) + (1 - y)

        def dev(hi_, x_, y_, c_):
            return (hi_ * 2 + x_, y_ * 2 + c_)

        partner = dev(hi, x, y, o)
        dev_a, dev_b = dev(hi, ax, ay, c), dev(hi, bx, by, c)
        dev_x = dev(hi, 1 - x, y, c)
        ups = [lax.rem(g + j, 4) for j in range(4)]
        downs = [lax.rem(g + 4 - j, 4) for j in range(4)]
        dev_up = [dev(u * members + m, x, y, c) for u in ups]
        right = dev(jnp.minimum(hi + 1, n_hi - 1), x, y, c)
        left = dev(jnp.maximum(hi - 1, 0), x, y, c)

        barrier = pltpu.get_barrier_semaphore()
        greet = [partner, dev_a, dev_b] + dev_up[1:]
        for d in greet:
            pl.semaphore_signal(barrier, inc=1, device_id=d, device_id_type=MESH)
        if members > 1:

            @pl.when(hi < n_hi - 1)
            def _():
                pl.semaphore_signal(barrier, inc=1, device_id=right, device_id_type=MESH)

            @pl.when(hi > 0)
            def _():
                pl.semaphore_signal(barrier, inc=1, device_id=left, device_id_type=MESH)

        pl.semaphore_wait(barrier, len(greet))
        if members > 1:

            @pl.when(hi < n_hi - 1)
            def _():
                pl.semaphore_wait(barrier, 1)

            @pl.when(hi > 0)
            def _():
                pl.semaphore_wait(barrier, 1)

        numbers = {}
        pending = []

        def number(key):
            return numbers.setdefault(key, len(numbers))

        def remote(key, src, dst, to):
            i = number(key)
            return pltpu.make_async_remote_copy(
                src_ref=src, dst_ref=dst, send_sem=ss.at[i], recv_sem=rs.at[i], device_id=to, device_id_type=MESH
            )

        def send(key, src, dst, to):
            d = remote(key, src, dst, to)
            d.start()
            pending.append((key, d))

        def sent(key):
            for k, d in list(pending):
                if k == key:
                    d.wait_send()
                    pending.remove((k, d))

        def got(key, ref):
            remote(key, ref, ref, partner).wait_recv()

        n_local = [0]
        local_pending = []

        def local(src, dst):
            d = pltpu.make_async_copy(src, dst, ls.at[n_local[0]])
            n_local[0] += 1
            d.start()
            return d

        started = {}

        def e0(i):
            r = wp[i].shape[1]
            mine = W[i].at[g, p, pl.ds(r * c, r)]
            started[i] = local(wp[i].at[c], mine)
            send(("e0", i), wp[i].at[o], mine, partner)

        def e1(i):
            r = wp[i].shape[1]
            started[i].wait()
            got(("e0", i), W[i].at[g, p, pl.ds(r * o, r)])
            for j in (1, 2, 3):
                send(("e1", i, j), W[i].at[g, p], W[i].at[g, p], dev_up[j])

        def e2(i):
            for j in (1, 2, 3):
                got(("e1", i, j), W[i].at[downs[j], p])
            send(("e2b", i), W[i].at[:, p], W[i].at[:, p], dev_b)
            send(("e2a", i), W[i].at[:, p], W[i].at[:, p], dev_a)

        def e3(i):
            got(("e2a", i), W[i].at[:, pa])
            send(("e3", i), W[i].at[:, pa], W[i].at[:, pa], dev_b)

        def e4(i):
            got(("e2b", i), W[i].at[:, pb])
            got(("e3", i), W[i].at[:, pab])

        done = {1: -1, 2: -1, 3: -1, 4: -1}

        def f1(i):
            w = reduce[i][1]
            k = i % RING
            for n, col in ((0, pab), (1, pb)):
                send(("f1", i, n), G[i].at[:, col], R1.at[k, n, :, :, 0:w], dev_b)

        def f2(i):
            w = reduce[i][1]
            k = i % RING
            got(("f1", i, 0), R1.at[k, 0, :, :, 0:w])
            G[i][:, pa] = G[i][:, pa] + R1[k, 0, :, :, 0:w]
            send(("f2", i), G[i].at[:, pa], R2.at[k, :, :, 0:w], dev_a)
            got(("f1", i, 1), R1.at[k, 1, :, :, 0:w])
            G[i][:, p] = G[i][:, p] + R1[k, 1, :, :, 0:w]

        def f3(i):
            w = reduce[i][1]
            k = i % RING
            got(("f2", i), R2.at[k, :, :, 0:w])
            G[i][:, p] = G[i][:, p] + R2[k, :, :, 0:w]
            for j in (1, 2, 3):
                send(("f3", i, j), G[i].at[ups[j], p], R3.at[k, j - 1, :, 0:w], dev_up[j])

        def f4(i):
            w, at = reduce[i][1], offsets[i]
            k = i % RING
            total = G[i][g, p].astype(F32)
            for j in (1, 2, 3):
                got(("f3", i, j), R3.at[k, j - 1, :, 0:w])
                total = total + R3[k, j - 1, :, 0:w].astype(F32)
            FS[:, :, at : at + w] = total.reshape(2, rows, w)
            local_pending.append(local(FS.at[c, :, at : at + w], go[i].at[c]))
            send(("f4", i), FS.at[o, :, at : at + w], go[i].at[c], partner)

        stages = {1: f1, 2: f2, 3: f3, 4: f4}

        def go_to(stage, last):
            while done[stage] < last:
                i = done[stage] + 1
                if stage < 4 and i >= RING // 2:
                    go_to(stage + 1, i - RING // 2)
                if stage > 1:
                    go_to(stage - 1, i)
                stages[stage](i)
                done[stage] = i

        def reduce_to(a, b=-1, cc=-1, dd=-1):
            if dd >= 0:
                go_to(4, dd)
            if cc >= 0:
                go_to(3, cc)
            if b >= 0:
                go_to(2, b)
            if a >= 0:
                go_to(1, a)

        def loop(n, body):
            def step(i, carry):
                body(i)
                return carry

            lax.fori_loop(0, n, step, 0)

        def put_grad(i, lhs_t, rhs):
            w = reduce[i][1]

            def one(k):
                a = lhs_t[pl.ds(pl.multiple_of(k * quarter, quarter), quarter), :]
                G[i][k] = nn(a, rhs()).astype(BF16).reshape(4, rows2, w)

            loop(4, one)

        def weight(i, at, w):
            return W[i][:, :, :, at : at + w].reshape(width, w)

        def transpose_in(src, dst, b):
            def one(k):
                at = pl.multiple_of(k * quarter, quarter)
                dst[pl.ds(at, quarter), pl.ds(pl.multiple_of(b * block, block), block)] = (
                    src[b, :, pl.ds(at, quarter)].astype(F32).T.astype(BF16)
                )

            loop(4, one)

        for i in range(len(gather)):
            e0(i)
        cx = local(tok, X.at[c])
        send("x", tok, X.at[c], partner)
        cy = local(cot, DY.at[c])
        send("dy", cot, DY.at[c], partner)
        e1(0)
        e1(1)
        e1(2)
        e1(3)
        cx.wait()
        cy.wait()
        got("x", X.at[o])
        got("dy", DY.at[o])
        e2(0)
        e2(1)
        e3(0)
        e1(4)
        transpose_in(DY, DYT, 0)
        transpose_in(DY, DYT, 1)
        e2(2)
        e4(0)
        e3(1)

        for k in range(8):
            kg, kx = k // 2, k % 2
            acc = None
            for ky in range(2):
                for kc in range(2):
                    t = W[0][kg, 2 * kx + ky, 16 * kc : 16 * kc + 16, :].astype(F32)
                    acc = t if acc is None else acc + t
            GROW[:, LANES * k : LANES * (k + 1)] = acc[:8]
        GACC[...] = jnp.zeros_like(GACC)

        step_rows = 16

        def norm_one(r):
            at = pl.multiple_of(r * step_rows, step_rows)
            for b in range(2):
                xs = X[b, pl.ds(at, step_rows), :].astype(F32)
                r1 = lax.rsqrt(jnp.mean(xs * xs, axis=-1, keepdims=True) + EPS)
                NB[b, pl.ds(at, step_rows), :] = (xs * r1 * GROW[0:1, :]).astype(BF16)

        loop(block // step_rows, norm_one)
        transpose_in(NB, N1T, 0)
        transpose_in(NB, N1T, 1)
        e2(3)
        e3(2)
        e1(5)
        e4(1)

        iq = gi["qkv"]
        both = NB[...].reshape(2 * block, width)
        t = nn(both, weight(iq, 0, 2 * QH))
        for b in range(2):
            QK[b] = t[block * b : block * (b + 1)].T
        for at, w in tiles_of(VH):
            t = nn(NB[...].reshape(2 * block, width), weight(iq, 2 * QH + at, w))
            for b in range(2):
                VT[b, at : at + w, :] = t[block * b : block * (b + 1)].T.astype(BF16)
        WACC[...] = jnp.zeros_like(WACC)
        lane = lax.broadcasted_iota(jnp.int32, (FEATS, LANES), 1)

        def place(i):
            b = i // PAIRS
            hp = lax.rem(i, PAIRS)
            return b, hp

        def q_rows(b, hp, e):
            return QK[b, pl.ds(pl.multiple_of(hp * 2 * FDIM + e * FDIM, FDIM), FDIM), :]

        def k_rows(b, hp, e):
            return QK[b, pl.ds(pl.multiple_of(QH + hp * 2 * FDIM + e * FDIM, FDIM), FDIM), :]

        def v_slice(hp):
            return pl.ds(pl.multiple_of(hp * 2 * VDIM, 2 * VDIM), 2 * VDIM)

        def head_slice(hp, e):
            return pl.ds(pl.multiple_of(hp * 2 * VDIM + e * VDIM, VDIM), VDIM)

        def put_state(i, f0, f1, right_side, w0, w1):
            low = nt(f0, right_side)
            high = nt(f1, right_side)
            ST[1 + i] = jnp.where(lane < VDIM, low, high).astype(BF16)
            WACC[...] += jnp.where(lane == 2 * i, w0, 0.0) + jnp.where(lane == 2 * i + 1, w1, 0.0)

        def state_step(i):
            b, hp = place(i)
            fs = [features(k_rows(b, hp, e)) for e in range(2)]
            ws = [jnp.sum(f.astype(F32), axis=1, keepdims=True) for f in fs]
            put_state(i, fs[0], fs[1], VT[b, v_slice(hp), :], ws[0], ws[1])

        loop(2 * PAIRS, state_step)
        ST[0] = WACC[...].astype(BF16)

        spans = ((0, PAIRS + 1), (PAIRS + 1, SLOTS))

        def state_exchange(n):
            for k, (lo, up) in enumerate(spans):
                send(("sx", n, k), ST.at[lo:up], STXS.at[n, lo:up], dev_x)

        def chain(n, hop, back):
            rank = n_hi - 1 - hi if back else hi
            to = left if back else right
            STX, STS = STXS.at[n], STSS.at[n]
            mine = rank == hop if hop < n_hops - 1 else rank >= hop

            @pl.when(mine)
            def _():
                for k, (lo, up) in enumerate(spans):
                    number(("sc", n, k))
                    d = remote(("sc", n, k), STO.at[lo:up], STS.at[lo:up], to)

                    if hop > 0:
                        got(("sc", n, k), STS.at[lo:up])
                    else:
                        STS[lo:up] = jnp.zeros((up - lo, FEATS, LANES), BF16)

                    @pl.when(rank < n_hi - 1)
                    def _():
                        def add(j):
                            STO[j] = (
                                STS[j].astype(F32) + (ST[j].astype(F32) + STX[j].astype(F32))
                            ).astype(BF16)

                        lax.fori_loop(lo, up, lambda j, z: (add(j), z)[1], 0)
                        d.start()

        def chain_sent(n, back):
            rank = n_hi - 1 - hi if back else hi

            @pl.when(rank < n_hi - 1)
            def _():
                for k, (lo, up) in enumerate(spans):
                    remote(("sc", n, k), STO.at[lo:up], STSS.at[n, lo:up], partner).wait_send()

        def chain_end(n, dst, near):
            def add(j):
                keep = jnp.where(near, STXS[n, j].astype(F32), 0.0)
                dst[j] = (STSS[n, j].astype(F32) + keep).astype(BF16)

            loop(SLOTS, add)

        def state_got(n):
            for k, (lo, up) in enumerate(spans):
                got(("sx", n, k), STXS.at[n, lo:up])

        state_exchange(0)
        e3(3)
        e2(4)
        e1(6)
        e4(2)
        state_got(0)
        chain(0, 0, False)
        e2(5)
        e3(4)
        e1(7)
        e4(3)
        chain(0, 1, False)
        e1(8)
        e2(6)
        e3(5)
        chain(0, 2, False)
        e2(7)
        e3(6)
        chain(0, 3, False)
        chain_end(0, PB, x == 1)

        def score_z(b, hp, e):
            qh, ql = split_low(q_rows(b, hp, e))
            kh, kl = split_low(k_rows(b, hp, e))
            return tn(jnp.concatenate([kh, kh, kl], axis=0), jnp.concatenate([qh, ql, qh], axis=0))

        def column(buf, at):
            return jnp.sum(jnp.where(lane == at, buf[0].astype(F32), 0.0), axis=1, keepdims=True)

        def att_step(i):
            b, hp = place(i)
            turned = PB[1 + i].astype(F32).T.astype(BF16)
            tops = []
            for e in range(2):
                z = score_z(b, hp, e)
                st = (1.0 + z * FDIM**-0.5 + z * z * (0.5 / FDIM)).astype(BF16)
                fq = weighted(features(q_rows(b, hp, e)))
                num = nn(VT[b, head_slice(hp, e), :], st) + nn(turned[VDIM * e : VDIM * (e + 1)], fq)
                den = jnp.sum(st.astype(F32), axis=0, keepdims=True) + jnp.sum(
                    fq.astype(F32) * column(PB, 2 * i + e), axis=0, keepdims=True
                )
                NUM[b, head_slice(hp, e), :] = num
                DEN[i, e : e + 1, :] = den
                tops.append(num / den)
            ATT[b, :, v_slice(hp)] = jnp.concatenate(tops, axis=0).T.astype(BF16)

        loop(2 * PAIRS, att_step)
        e2(8)
        e3(7)

        io = gi["out"]

        def col(k):
            return pl.ds(pl.multiple_of(k * quarter, quarter), quarter)

        def wrow(i, k, at, w):
            return W[i][k, :, :, at : at + w].reshape(quarter, w)

        def out_proj(dst, b):
            def one(k):
                dst[:, col(k)] = nt(ATT[b], wrow(io, k, 0, VH))

            loop(4, one)

        out_proj(SND.at[0], o)
        send("x1", SND.at[0], RCV.at[0], partner)
        out_proj(OWN, c)
        got("x1", RCV.at[0])

        def norm_two(r):
            at = pl.multiple_of(r * step_rows, step_rows)
            rr = pl.ds(at, step_rows)
            x1 = X[c, rr, :].astype(F32) + (OWN[rr, :] + RCV[0, rr, :])
            X1[rr, :] = x1
            r2 = lax.rsqrt(jnp.mean(x1 * x1, axis=-1, keepdims=True) + EPS)
            NB[c, rr, :] = (x1 * r2 * GROW[1:2, :]).astype(BF16)

        loop(block // step_rows, norm_two)
        send("n2", NB.at[c], NB.at[c], partner)
        transpose_in(NB, N2T, c)
        got("n2", NB.at[o])
        transpose_in(NB, N2T, o)

        def ffn_in(j):
            base, w = parts[j]
            i = gi[f"gu{j}"]
            for at, tw in tiles_of(w):
                TG[:, 0:tw] = nn(NB[...].reshape(2 * block, width), weight(i, at, tw))
                TU[:, 0:tw] = nn(NB[...].reshape(2 * block, width), weight(i, w + at, tw))
                lo = base + at

                def one(r):
                    rr = pl.ds(pl.multiple_of(r * 64, 64), 64)
                    gate, up = TG[rr, 0:tw], TU[rr, 0:tw]
                    sg = 1.0 / (1.0 + jnp.exp(-gate))
                    silu = gate * sg
                    HID[rr, lo : lo + tw] = (silu * up).astype(BF16)
                    CA[rr, lo : lo + tw] = (up * sg * (1.0 + gate * (1.0 - sg))).astype(BF16)
                    CB[rr, lo : lo + tw] = silu.astype(BF16)

                loop(2 * block // 64, one)
            put_grad(ri[f"d{j}"], DYT, lambda: HID[:, base : base + w])
            reduce_to(ri[f"d{j}"])

        for j in range(n_parts):
            if j:
                e4(gi[f"gu{j}"])
            ffn_in(j)
        e3(8)
        e4(6)
        e4(7)
        e4(8)

        def ffn_back(j):
            base, w = parts[j]
            i = gi[f"d{j}"]
            for at, tw in tiles_of(w):
                TG[:, 0:tw] = nn(DY[...].reshape(2 * block, width), weight(i, at, tw))
                lo = base + at

                def one(r):
                    rr = pl.ds(pl.multiple_of(r * 64, 64), 64)
                    dh = TG[rr, 0:tw]
                    CA[rr, lo : lo + tw] = (dh * CA[rr, lo : lo + tw].astype(F32)).astype(BF16)
                    CB[rr, lo : lo + tw] = (dh * CB[rr, lo : lo + tw].astype(F32)).astype(BF16)

                loop(2 * block // 64, one)

        for j in range(n_parts):
            ffn_back(j)
        reduce_to(-1, 0)

        def tokens_of(b):
            return pl.ds(pl.multiple_of(b * block, block), block)

        def dn2(dst, b):
            def one(k):
                acc = None
                for j, (base, w) in enumerate(parts):
                    i = gi[f"gu{j}"]
                    for buf, at in ((CA, 0), (CB, w)):
                        t = nt(buf[tokens_of(b), base : base + w], wrow(i, k, at, w))
                        acc = t if acc is None else acc + t
                dst[:, col(k)] = acc

            loop(4, one)

        sent("x1")
        dn2(SND.at[0], o)
        send("dn2", SND.at[0], RCV.at[1], partner)
        dn2(OWN, c)
        reduce_to(-1, 1, 0)
        put_grad(ri["g0"], N2T, lambda: CA[:, parts[0][0] : parts[0][0] + parts[0][1]])
        reduce_to(ri["g0"])
        got("dn2", RCV.at[1])
        sent("n2")

        def norm_two_back(r):
            at = pl.multiple_of(r * step_rows, step_rows)
            rr = pl.ds(at, step_rows)
            d = OWN[rr, :] + RCV[1, rr, :]
            x1 = X1[rr, :]
            r2 = lax.rsqrt(jnp.mean(x1 * x1, axis=-1, keepdims=True) + EPS)
            t = d * (x1 * r2)
            GACC[8:16, :] += t[:8] + t[8:]
            a2 = d * GROW[1:2, :]
            dx = DY[c, rr, :].astype(F32) + (
                r2 * a2 - x1 * (r2 * r2 * r2) * jnp.mean(a2 * x1, axis=-1, keepdims=True)
            )
            din_ref[rr, :] = dx
            NB[c, rr, :] = dx.astype(BF16)

        loop(block // step_rows, norm_two_back)
        send("dx1", NB.at[c], NB.at[c], partner)
        transpose_in(NB, DYT, c)
        put_grad(ri["u0"], N2T, lambda: CB[:, parts[0][0] : parts[0][0] + parts[0][1]])
        reduce_to(ri["u0"], 2)
        got("dx1", NB.at[o])
        transpose_in(NB, DYT, o)

        for at, tw in tiles_of(VH):
            t = nn(NB[...].reshape(2 * block, width), weight(io, at, tw))
            for b in range(2):
                DATT[b, at : at + tw, :] = t[block * b : block * (b + 1)].T
        WACC[...] = jnp.zeros_like(WACC)
        for k in range(len(spans)):
            sent(("sx", 0, k))
        chain_sent(0, False)

        def back_state_step(i):
            b, hp = place(i)
            fs, ws = [], []
            for e in range(2):
                hs = head_slice(hp, e)
                datt, num, den = DATT[b, hs, :], NUM[b, hs, :], DEN[i, e : e + 1, :]
                dd = (-jnp.sum(datt * num, axis=0, keepdims=True) / (den * den)).astype(BF16)
                DNUM[b, hs, :] = (datt / den).astype(BF16)
                DDEN[i, e : e + 1, :] = dd.astype(F32)
                f = features(q_rows(b, hp, e))
                fs.append(f)
                ws.append(jnp.sum(f.astype(F32) * dd.astype(F32), axis=1, keepdims=True))
            put_state(i, fs[0], fs[1], DNUM[b, v_slice(hp), :], ws[0], ws[1])

        loop(2 * PAIRS, back_state_step)
        ST[0] = WACC[...].astype(BF16)
        state_exchange(1)
        put_grad(ri["g1"], N2T, lambda: CA[:, parts[1][0] : parts[1][0] + parts[1][1]])
        reduce_to(ri["g1"], 3, 1)
        state_got(1)
        chain(1, 0, True)

        zeros_head = jnp.zeros((VDIM, block), BF16)

        def masked(t, e):
            return jnp.concatenate([zeros_head, t] if e else [t, zeros_head], axis=0)

        def back_step(i):
            b, hp = place(i)
            for e in range(2):
                hs = head_slice(hp, e)
                q, kk = q_rows(b, hp, e), k_rows(b, hp, e)
                qh, ql = split_low(q)
                kh, kl = split_low(kk)
                z = tn(jnp.concatenate([kh, kh, kl], axis=0), jnp.concatenate([qh, ql, qh], axis=0))
                st = (1.0 + z * FDIM**-0.5 + z * z * (0.5 / FDIM)).astype(BF16)
                dnum, dden = DNUM[b, hs, :], DDEN[i, e : e + 1, :]
                ds = (tn(VT[b, hs, :], dnum) + dden).astype(BF16).astype(F32)
                dz = (ds * (FDIM**-0.5 + z * (1.0 / FDIM))).astype(BF16)
                t = nn(jnp.concatenate([kh, kl], axis=0), dz)
                dq = t[:FDIM] + t[FDIM:]
                t = nt(jnp.concatenate([qh, ql], axis=0), dz)
                dk = t[:FDIM] + t[FDIM:]
                DV[b, hs, :] = nt(dnum, st)
                df = nn(PB[1 + i], masked(dnum, e)) + column(PB, 2 * i + e) * dden
                DQK[b, pl.ds(pl.multiple_of(hp * 2 * FDIM + e * FDIM, FDIM), FDIM), :] = dq + features_back(q, df)
                DQK[b, pl.ds(pl.multiple_of(QH + hp * 2 * FDIM + e * FDIM, FDIM), FDIM), :] = dk

        loop(2 * PAIRS, back_step)
        chain(1, 1, True)
        put_grad(ri["u1"], N2T, lambda: CB[:, parts[1][0] : parts[1][0] + parts[1][1]])
        reduce_to(ri["u1"], 4, 2)

        def y_part(dst, b):
            def one(k):
                acc = None
                for j, (base, w) in enumerate(parts):
                    t = nt(HID[tokens_of(b), base : base + w], wrow(gi[f"d{j}"], k, 0, w))
                    acc = t if acc is None else acc + t
                dst[:, col(k)] = acc

            loop(4, one)

        y_part(SND.at[1], o)
        send("y", SND.at[1], RCV.at[2], partner)
        y_part(OWN, c)
        chain(1, 2, True)
        for j in range(2, n_parts):
            put_grad(ri[f"g{j}"], N2T, lambda: CA[:, parts[j][0] : parts[j][0] + parts[j][1]])
            reduce_to(ri[f"g{j}"], ri[f"g{j}"] - 2, ri[f"g{j}"] - 4)
            put_grad(ri[f"u{j}"], N2T, lambda: CB[:, parts[j][0] : parts[j][0] + parts[j][1]])
        got("y", RCV.at[2])

        def finish(r):
            rr = pl.ds(pl.multiple_of(r * step_rows, step_rows), step_rows)
            out_ref[rr, :] = (X1[rr, :] + (OWN[rr, :] + RCV[2, rr, :])).astype(BF16)

        loop(block // step_rows, finish)
        chain(1, 3, True)
        chain_end(1, PX, x == 0)

        def key_step(i):
            b, hp = place(i)
            turned = PX[1 + i].astype(F32).T.astype(BF16)
            for e in range(2):
                hs = head_slice(hp, e)
                kk = k_rows(b, hp, e)
                df = nn(PX[1 + i], masked(VT[b, hs, :], e)) + column(PX, 2 * i + e)
                kr = pl.ds(pl.multiple_of(QH + hp * 2 * FDIM + e * FDIM, FDIM), FDIM)
                DQK[b, kr, :] += features_back(kk, df)
                DV[b, hs, :] += nn(turned[VDIM * e : VDIM * (e + 1)], weighted(features(kk)))

        loop(2 * PAIRS, key_step)
        for b in range(2):
            DQKV[b, :, 0 : 2 * QH] = DQK[b].T.astype(BF16)
            for at, tw in tiles_of(VH):
                DQKV[b, :, 2 * QH + at : 2 * QH + at + tw] = DV[b, at : at + tw, :].T.astype(BF16)

        def dn1(dst, b):
            def one(k):
                dst[:, col(k)] = nt(DQKV[b], wrow(iq, k, 0, 2 * QH + VH))

            loop(4, one)

        sent("dn2")
        dn1(SND.at[0], o)
        send("dn1", SND.at[0], RCV.at[0], partner)
        u_last = ri[f"u{n_parts - 1}"]
        reduce_to(u_last, u_last - 2, u_last - 4)
        put_grad(ri["out"], DYT, lambda: ATT[...].reshape(2 * block, VH))
        reduce_to(ri["out"], ri["out"] - 2, ri["out"] - 4)
        put_grad(ri["qk"], N1T, lambda: DQKV[:, :, 0 : 2 * QH].reshape(2 * block, 2 * QH))
        put_grad(ri["v"], N1T, lambda: DQKV[:, :, 2 * QH :].reshape(2 * block, VH))
        reduce_to(ri["qk"], ri["qk"] - 2, ri["qk"] - 4)
        dn1(OWN, c)
        got("dn1", RCV.at[0])

        def norm_one_back(r):
            rr = pl.ds(pl.multiple_of(r * step_rows, step_rows), step_rows)
            d = OWN[rr, :] + RCV[0, rr, :]
            xs = X[c, rr, :].astype(F32)
            r1 = lax.rsqrt(jnp.mean(xs * xs, axis=-1, keepdims=True) + EPS)
            t = d * (xs * r1)
            GACC[0:8, :] += t[:8] + t[8:]
            a1 = d * GROW[0:1, :]
            din_ref[rr, :] += r1 * a1 - xs * (r1 * r1 * r1) * jnp.mean(a1 * xs, axis=-1, keepdims=True)

        loop(block // step_rows, norm_one_back)
        ga = jnp.sum(GACC[0:8, :], axis=0, keepdims=True)
        gf = jnp.sum(GACC[8:16, :], axis=0, keepdims=True)
        last = ri["gain"]
        for k in range(4):
            row = lax.broadcasted_iota(jnp.int32, (LANES, quarter), 0)
            sl = slice(quarter * k, quarter * (k + 1))
            mat = jnp.where(row == 0, ga[:, sl], 0.0) + jnp.where(row == 1, gf[:, sl], 0.0)
            G[last][k] = mat.T.astype(BF16).reshape(4, rows2, LANES)
        n = len(reduce)
        reduce_to(n - 1, n - 3, n - 5)
        for k in range(n):
            go_to(2, min(n - 1, n - 3 + k))
            go_to(3, min(n - 1, n - 4 + k))
            go_to(4, min(n - 1, n - 5 + k))
        for i in range(n):
            got(("f4", i), go[i].at[o])
        for d in local_pending:
            d.wait()
        chain_sent(1, True)
        for _, d in pending:
            d.wait_send()

    return kernel


def call_kernel(tok, cot, packed, seq_size, ff_half):
    block, width = tok.shape
    gather, reduce = plan(ff_half)
    rows = width // 32
    quarter = width // 4
    vmem = pltpu.VMEM
    any_spec = pl.BlockSpec(memory_space=pl.ANY)
    total_width = sum(w for _, w in reduce)
    state = vmem((SLOTS, FEATS, LANES), BF16)
    scratch = [vmem((4, 4, 2 * a.shape[1], w), BF16) for a, (_, w) in zip(packed, gather)]
    scratch += [vmem((4, 4, 2 * rows, w), BF16) for _, w in reduce]
    scratch += [
        vmem((RING, 2, 4, 2 * rows, PIECE), BF16),
        vmem((RING, 4, 2 * rows, PIECE), BF16),
        vmem((RING, 3, 2 * rows, PIECE), BF16),
        vmem((2, rows, total_width), F32),
        vmem((2, block, width), BF16),
        vmem((2, block, width), BF16),
        vmem((2, block, width), BF16),
        vmem((width, 2 * block), BF16),
        vmem((width, 2 * block), BF16),
        vmem((width, 2 * block), BF16),
        vmem((2 * block, ff_half), BF16),
        vmem((2 * block, ff_half), BF16),
        vmem((2 * block, ff_half), BF16),
        vmem((block, width), F32),
        vmem((2, block, width), F32),
        vmem((3, block, width), F32),
        vmem((block, width), F32),
        vmem((2, VH, block), F32),
        vmem((2, VH, block), F32),
        vmem((2, 2 * QH, block), F32),
        vmem((2, VH, block), BF16),
        vmem((2, block, VH), BF16),
        vmem((2 * PAIRS, 8, block), F32),
        vmem((2, VH, block), BF16),
        vmem((2 * PAIRS, 8, block), F32),
        vmem((2, 2 * QH, block), F32),
        vmem((2, VH, block), F32),
        vmem((2, block, 2 * QH + VH), BF16),
        state,
        vmem((2, SLOTS, FEATS, LANES), BF16),
        vmem((2, SLOTS, FEATS, LANES), BF16),
        state,
        state,
        state,
        vmem((FEATS, LANES), F32),
        vmem((2 * block, 256), F32),
        vmem((2 * block, 256), F32),
        vmem((8, width), F32),
        vmem((16, width), F32),
        pltpu.SemaphoreType.DMA((256,)),
        pltpu.SemaphoreType.DMA((256,)),
        pltpu.SemaphoreType.DMA((64,)),
        pltpu.SemaphoreType.REGULAR,
    ]
    out_shape = [
        jax.ShapeDtypeStruct((block, width), BF16),
        jax.ShapeDtypeStruct((block, width), F32),
    ] + [jax.ShapeDtypeStruct((2, rows, w), F32) for _, w in reduce]
    return pl.pallas_call(
        make_kernel(seq_size, block, width, ff_half),
        out_shape=out_shape,
        in_specs=[any_spec] * (2 + len(packed)),
        out_specs=[pl.BlockSpec(memory_space=vmem)] * 2 + [any_spec] * len(reduce),
        scratch_shapes=scratch,
        compiler_params=pltpu.CompilerParams(
            collective_id=0, has_side_effects=True, vmem_limit_bytes=62 * 2**20
        ),
    )(tok, cot, *packed)


def body(
    tokens, attn_gain, query_weight, key_weight, value_weight, out_weight, ffn_gain, gate_weight, up_weight, down_weight, cotangent
):
    seq_size = lax.axis_size("seq")
    members = seq_size // 8
    _, block, width = tokens.shape
    ff = gate_weight.shape[1]
    ff_half = LANES * ((ff + 2 * LANES - 1) // (2 * LANES))
    few = attn_gain.shape[0]
    groups = [[(g * members + m) * 2 + x for m in range(members)] for g in range(4) for x in range(2)]

    def halves(w):
        return w.reshape(w.shape[0], 2, w.shape[1] // 2).transpose(1, 0, 2)

    def ff_halves(w):
        return halves(jnp.pad(w, ((0, 0), (0, 2 * ff_half - ff))))

    gates, ups, downs = ff_halves(gate_weight), ff_halves(up_weight), ff_halves(down_weight.T)
    parts = pieces_of(ff_half)
    packed = [jnp.concatenate([halves(query_weight), halves(key_weight), halves(value_weight)], axis=2), halves(out_weight.T)]
    packed += [jnp.concatenate([gates[:, :, a : a + w], ups[:, :, a : a + w]], axis=2) for a, w in parts]
    packed += [downs[:, :, a : a + w] for a, w in parts]
    gains = jnp.stack([attn_gain, ffn_gain])
    if members > 1:
        packed = [lax.all_gather(a, "seq", axis_index_groups=groups, axis=1, tiled=True) for a in packed]
        gains = lax.all_gather(gains, "seq", axis_index_groups=groups, axis=1, tiled=True)
    rows = members * few
    spot = lax.broadcasted_iota(jnp.int32, (2, 4 * rows), 1) // rows == lax.axis_index("dp")
    gain_rows = jnp.where(spot, jnp.tile(gains, (1, 4)), jnp.zeros((), BF16))
    gain_block = jnp.pad(gain_rows, ((0, 14), (0, 0)))
    packed = [jnp.stack([gain_block, gain_block])] + packed

    def turn(t):
        if members == 1:
            return t
        return t.reshape(block, 4, members, 2, 4, few).transpose(0, 1, 3, 4, 2, 5).reshape(block, width)

    def turn_back(t):
        if members == 1:
            return t
        return t.reshape(block, 4, 2, 4, members, few).transpose(0, 1, 4, 2, 3, 5).reshape(block, width)

    results = call_kernel(turn(tokens[0]), turn(cotangent[0]), packed, seq_size, ff_half)
    output, input_grad, grads = results[0], results[1], results[2:]
    if members > 1:
        grads = [
            lax.psum_scatter(a, "seq", scatter_dimension=1, axis_index_groups=groups, tiled=True) for a in grads
        ]
    _, reduce = plan(ff_half)
    by = {name: a for (name, _), a in zip(reduce, grads)}

    def joined(a):
        return jnp.concatenate([a[0], a[1]], axis=1)

    def ff_joined(letter):
        return joined(jnp.concatenate([by[f"{letter}{j}"] for j in range(len(parts))], axis=2))[:, :ff]

    gain = by["gain"][0] + by["gain"][1]
    return (
        turn_back(output)[None],
        turn_back(input_grad)[None],
        gain[:, 0],
        joined(by["qk"][:, :, :QH]),
        joined(by["qk"][:, :, QH:]),
        joined(by["v"]),
        joined(by["out"]).T,
        gain[:, 1],
        ff_joined("g"),
        ff_joined("u"),
        ff_joined("d").T,
    )


def solution(mesh):
    both = ("seq", "dp")
    row, column, whole = P(both, None), P(None, both), P("dp", "seq", None)
    return jax.shard_map(
        body,
        mesh=mesh,
        in_specs=(whole, P(both), row, row, row, column, P(both), row, row, column, whole),
        out_specs=(whole, whole, P(both), row, row, row, column, P(both), row, row, column),
        check_vma=False,
    )
```

```python
import jax
import jax.numpy as jnp
from jax import lax
from jax.experimental import pallas as pl
from jax.experimental.pallas import tpu as pltpu
from jax.sharding import PartitionSpec as P

HEADS = 16
FDIM = 16
VDIM = 64
EPS = 1e-05
LIN = FDIM**-0.25
QUAD = (2.0 * FDIM) ** -0.5
SHIFTS = FDIM // 2
HALF = FDIM // 2
FEATS = FDIM * (SHIFTS + 2)
HALF_HEADS = HEADS // 2
QH = HALF_HEADS * FDIM
VH = HALF_HEADS * VDIM
PAIRS = HALF_HEADS // 2
COUNTS = PAIRS * FEATS
STATE = COUNTS + 16
STATE_STEPS = STATE // 16
LANES = 128
PIECE = 512
RING = 6
MESH = pl.DeviceIdType.MESH
F32 = jnp.float32
BF16 = jnp.bfloat16


def pieces_of(width):
    out, at = [], 0
    while at < width:
        out.append((at, min(PIECE, width - at)))
        at += PIECE
    return out


def tiles_of(width):
    out, at = [], 0
    while at < width:
        out.append((at, min(256, width - at)))
        at += 256
    return out


def nn(a, b):
    return jnp.dot(a, b, preferred_element_type=F32)


def nt(a, b):
    return lax.dot_general(a, b, (((1,), (1,)), ((), ())), preferred_element_type=F32)


def tn(a, b):
    return lax.dot_general(a, b, (((0,), (0,)), ((), ())), preferred_element_type=F32)


def ahead(t, d):
    return t if d == 0 else pltpu.roll(t, FDIM - d, 0)


def behind(t, d):
    return t if d == 0 else pltpu.roll(t, d, 0)


def features(u):
    rows = [u * ahead(u, d) * QUAD for d in range(SHIFTS)]
    spot = lax.broadcasted_iota(jnp.int32, u.shape, 0)
    last = jnp.where(spot < HALF, u * ahead(u, HALF) * QUAD, jnp.where(spot == HALF, 1.0, 0.0))
    return jnp.concatenate(rows + [last, u * LIN], axis=0).astype(BF16)


def weighted(f):
    at = FDIM * SHIFTS
    scale = jnp.where(lax.broadcasted_iota(jnp.int32, (FDIM, f.shape[1]), 0) < HALF, 2.0, 1.0).astype(BF16)
    return jnp.concatenate([f[:FDIM], f[FDIM:at] * 2, f[at : at + FDIM] * scale, f[at + FDIM :]], axis=0)


def features_back(u, df):
    at = FDIM * SHIFTS
    total = df[at + FDIM :] * LIN
    for d in range(SHIFTS + 1):
        t = df[FDIM * d : FDIM * (d + 1)] * (QUAD * (2.0 if d else 1.0))
        if d == HALF:
            t = jnp.where(lax.broadcasted_iota(jnp.int32, t.shape, 0) < HALF, t, 0.0)
        total = total + t * ahead(u, d) + behind(t * u, d)
    return total


def split_low(u):
    high = u.astype(BF16)
    return high, (u - high.astype(F32)).astype(BF16)


def plan(ff_half):
    parts = pieces_of(ff_half)
    gather = [("gain", LANES), ("qk", 2 * QH), ("v", VH), ("out", VH)]
    for j, (_, w) in enumerate(parts):
        gather += [(f"g{j}", w), (f"u{j}", w)]
    gather += [(f"d{j}", w) for j, (_, w) in enumerate(parts)][1:]
    gather += [("d0", parts[0][1])]
    reduce = [(f"d{j}", w) for j, (_, w) in enumerate(parts)]
    for j, (_, w) in enumerate(parts):
        reduce += [(f"g{j}", w), (f"u{j}", w)]
    reduce += [("out", VH), ("qk", 2 * QH), ("v", VH), ("gain", LANES)]
    return gather, reduce


def offsets_of(chunks):
    out, at = [], 0
    for _, w in chunks:
        out.append(at)
        at += w
    return out


def make_kernel(seq_size, block, width, ff, ff_half):
    gather, reduce = plan(ff_half)
    parts = pieces_of(ff_half)
    n_parts = len(parts)
    gi = {name: i for i, (name, _) in enumerate(gather)}
    ri = {name: i for i, (name, _) in enumerate(reduce)}
    members = seq_size // 8
    n_hi = seq_size // 2
    rows = width // 32
    rows2 = 2 * rows
    quarter = width // 4
    offsets = offsets_of(reduce)
    pack_at = offsets_of(gather)

    def kernel(*refs):
        it = iter(refs)
        take = lambda n: [next(it) for _ in range(n)]
        tok, cot = take(2)
        attn_in, q_in, k_in, v_in, o_in, ffn_in_gain, g_in, u_in, d_in = take(9)
        out_ref, din_ref, go = take(3)
        W = take(len(gather))
        G = take(len(reduce))
        (PK, R1, R2, R3, RZ, RY, FS, X, DY, NB, N1T, N2T, DYT, HID, CA, CB, X1, SND, RCV, OWN) = take(20)
        (NUM, DATT, QK, VT, ATT, DEN, DNUM, DDEN, DQK, DV, DQKV) = take(11)
        (ST, SA, SZ, TZ, TY, SB, PB, PX, WACC, TG, TU, GROW, GACC) = take(13)
        ss, rs, ls = take(3)

        s, dp = lax.axis_index("seq"), lax.axis_index("dp")
        hi, x = s // 2, lax.rem(s, 2)
        y, c = dp // 2, lax.rem(dp, 2)
        g, m = hi // members, lax.rem(hi, members)
        o = 1 - c
        ax, ay = x + o * (1 - 2 * x), y + c * (1 - 2 * y)
        bx, by = x + c * (1 - 2 * x), y + o * (1 - 2 * y)
        p, pa = 2 * x + y, 2 * ax + ay
        pb, pab = 2 * bx + by, 2 * (1 - x) + (1 - y)

        def dev(hi_, x_, y_, c_):
            return (hi_ * 2 + x_, y_ * 2 + c_)

        partner = dev(hi, x, y, o)
        dev_a, dev_b = dev(hi, ax, ay, c), dev(hi, bx, by, c)
        dev_x = dev(hi, 1 - x, y, c)
        ups = [lax.rem(g + j, 4) for j in range(4)]
        downs = [lax.rem(g + 4 - j, 4) for j in range(4)]
        dev_up = [dev(u * members + m, x, y, c) for u in ups]
        right = dev(jnp.minimum(hi + 1, n_hi - 1), x, y, c)
        left = dev(jnp.maximum(hi - 1, 0), x, y, c)

        n_local = [0]
        local_pending = []

        def local(src, dst):
            d = pltpu.make_async_copy(src, dst, ls.at[n_local[0]])
            n_local[0] += 1
            d.start()
            return d

        barrier = pltpu.get_barrier_semaphore()
        greet = [partner, dev_a, dev_b] + dev_up[1:]
        for d in greet:
            pl.semaphore_signal(barrier, inc=1, device_id=d, device_id_type=MESH)
        if members > 1:

            @pl.when(hi < n_hi - 1)
            def _():
                pl.semaphore_signal(barrier, inc=1, device_id=right, device_id_type=MESH)

            @pl.when(hi > 0)
            def _():
                pl.semaphore_signal(barrier, inc=1, device_id=left, device_id_type=MESH)

        cx = local(tok, X.at[c])
        cy = local(cot, DY.at[c])
        cx.wait()
        cy.wait()
        pl.semaphore_wait(barrier, len(greet))
        if members > 1:

            @pl.when(hi < n_hi - 1)
            def _():
                pl.semaphore_wait(barrier, 1)

            @pl.when(hi > 0)
            def _():
                pl.semaphore_wait(barrier, 1)

        numbers = {}
        pending = {}

        def number(key):
            return numbers.setdefault(key, len(numbers))

        def remote(key, src, dst, to):
            i = number(key)
            return pltpu.make_async_remote_copy(
                src_ref=src, dst_ref=dst, send_sem=ss.at[i], recv_sem=rs.at[i], device_id=to, device_id_type=MESH
            )

        def send(key, src, dst, to):
            if key in pending:
                sent(key)
            d = remote(key, src, dst, to)
            d.start()
            pending[key] = d

        def sent(key):
            pending.pop(key).wait_send()

        def got(key, ref):
            remote(key, ref, ref, partner).wait_recv()

        def pack(i, lower, upper):
            w = gather[i][1]
            r = 16 if i == 0 else rows
            mine = W[i].at[g, p, pl.ds(pl.multiple_of(r * c, r), r)]
            stage = PK.at[0:r, pack_at[i] : pack_at[i] + w]

            @pl.when(c == 0)
            def _():
                mine[...] = lower()
                stage[...] = upper()

            @pl.when(c == 1)
            def _():
                mine[...] = upper()
                stage[...] = lower()

            send(("e0", i), stage, mine, partner)

        def ff_piece(ref, at, w):
            have = min(w, ff - at)
            if have == w:
                return ref[:, at : at + w]
            return jnp.concatenate([ref[:, at : at + have], jnp.zeros((ref.shape[0], w - have), BF16)], axis=1)

        def gain_block():
            out = jnp.zeros((16, LANES), F32)
            lanes = lax.broadcasted_iota(jnp.int32, (16, LANES), 1) // rows
            row = lax.broadcasted_iota(jnp.int32, (16, LANES), 0)
            for n, ref in enumerate((attn_in, ffn_in_gain)):
                t = jnp.concatenate([ref[...].astype(F32)] * (LANES // rows), axis=1)
                out = jnp.where((lanes == dp) & (row == n), t, out)
            return out.astype(BF16)

        def e0(i):
            name, w = gather[i]
            if name == "gain":
                pack(i, gain_block, gain_block)
            elif name == "qk":
                pack(
                    i,
                    lambda: jnp.concatenate([q_in[:, :QH], k_in[:, :QH]], axis=1),
                    lambda: jnp.concatenate([q_in[:, QH:], k_in[:, QH:]], axis=1),
                )
            elif name == "v":
                pack(i, lambda: v_in[:, :VH], lambda: v_in[:, VH:])
            elif name == "out":
                pack(i, lambda: o_in[:, :VH], lambda: o_in[:, VH:])
            else:
                at = parts[int(name[1:])][0]
                ref = {"g": g_in, "u": u_in, "d": d_in}[name[0]]
                pack(i, lambda: ff_piece(ref, at, w), lambda: ff_piece(ref, ff_half + at, w))

        def e1(i):
            r = 16 if i == 0 else rows
            got(("e0", i), W[i].at[g, p, pl.ds(pl.multiple_of(r * o, r), r)])
            for j in (1, 2, 3):
                send(("e1", i, j), W[i].at[g, p], W[i].at[g, p], dev_up[j])

        def e2(i):
            for j in (1, 2, 3):
                got(("e1", i, j), W[i].at[downs[j], p])
            send(("e2b", i), W[i].at[:, p], W[i].at[:, p], dev_b)
            send(("e2a", i), W[i].at[:, p], W[i].at[:, p], dev_a)

        def e3(i):
            got(("e2a", i), W[i].at[:, pa])
            send(("e3", i), W[i].at[:, pa], W[i].at[:, pa], dev_b)

        def e4(i):
            got(("e2b", i), W[i].at[:, pb])
            got(("e3", i), W[i].at[:, pab])

        iz = len(gather) - 1

        def z1():
            r = rows
            got(("e0", iz), W[iz].at[g, p, pl.ds(pl.multiple_of(r * o, r), r)])
            send(("e2b", iz), W[iz].at[g, p], W[iz].at[g, p], dev_b)
            send(("e2a", iz), W[iz].at[g, p], W[iz].at[g, p], dev_a)

        def z2():
            got(("e2a", iz), W[iz].at[g, pa])
            send(("e3", iz), W[iz].at[g, pa], W[iz].at[g, pa], dev_b)

        def z3():
            got(("e2b", iz), W[iz].at[g, pb])
            got(("e3", iz), W[iz].at[g, pab])
            for j in (1, 2, 3):
                send(("e1", iz, j), W[iz].at[g], W[iz].at[g], dev_up[j])

        def z4():
            for j in (1, 2, 3):
                got(("e1", iz, j), W[iz].at[downs[j]])

        gathered = {1: -1, 2: -1, 3: -1, 4: -1}

        def ga(step, last):
            while gathered[step] < min(last, iz - 1):
                gathered[step] += 1
                (e1, e2, e3, e4)[step - 1](gathered[step])

        def gstep(k, l1=1, l2=1):
            ga(1, k + l1 + l2)
            ga(2, k + l2)
            ga(3, k)
            ga(4, k - 1)

        done = {1: 0, 2: 0, 3: 0, 4: 0}

        def zf1():
            w = reduce[0][1]
            for j in (1, 2, 3):
                send(("z1", j), G[0].at[ups[j]], RZ.at[j - 1, :, :, 0:w], dev_up[j])

        def zf2():
            w = reduce[0][1]
            for j in (1, 2, 3):
                got(("z1", j), RZ.at[j - 1, :, :, 0:w])

            def one(k):
                total = G[0][g, k].astype(F32)
                for j in range(3):
                    total = total + RZ[j, k, :, 0:w].astype(F32)
                G[0][g, k] = total.astype(BF16)

            loop(4, one)
            for n, q in ((0, pab), (1, pb)):
                send(("z2", n), G[0].at[g, q], RY.at[n, :, 0:w], dev_b)

        def zf3():
            w = reduce[0][1]
            got(("z2", 0), RY.at[0, :, 0:w])
            G[0][g, pa] = G[0][g, pa] + RY[0, :, 0:w]
            send(("z3", 0), G[0].at[g, pa], RY.at[2, :, 0:w], dev_a)
            got(("z2", 1), RY.at[1, :, 0:w])
            G[0][g, p] = G[0][g, p] + RY[1, :, 0:w]

        def zf4():
            w = reduce[0][1]
            got(("z3", 0), RY.at[2, :, 0:w])
            finish_chunk(0, G[0][g, p].astype(F32) + RY[2, :, 0:w].astype(F32))

        def f1(i):
            w = reduce[i][1]
            k = i % RING
            for n, col in ((0, pab), (1, pb)):
                send(("f1", k, n), G[i].at[:, col], R1.at[k, n, :, :, 0:w], dev_b)

        def f2(i):
            w = reduce[i][1]
            k = i % RING
            got(("f1", k, 0), R1.at[k, 0, :, :, 0:w])
            G[i][:, pa] = G[i][:, pa] + R1[k, 0, :, :, 0:w]
            send(("f2", k), G[i].at[:, pa], R2.at[k, :, :, 0:w], dev_a)
            got(("f1", k, 1), R1.at[k, 1, :, :, 0:w])
            G[i][:, p] = G[i][:, p] + R1[k, 1, :, :, 0:w]

        def f3(i):
            w = reduce[i][1]
            k = i % RING
            got(("f2", k), R2.at[k, :, :, 0:w])
            G[i][:, p] = G[i][:, p] + R2[k, :, :, 0:w]
            for j in (1, 2, 3):
                send(("f3", k, j), G[i].at[ups[j], p], R3.at[k, j - 1, :, 0:w], dev_up[j])

        def f4(i):
            w = reduce[i][1]
            k = i % RING
            total = G[i][g, p].astype(F32)
            for j in (1, 2, 3):
                got(("f3", k, j), R3.at[k, j - 1, :, 0:w])
                total = total + R3[k, j - 1, :, 0:w].astype(F32)
            finish_chunk(i, total)

        def finish_chunk(i, total):
            w, at = reduce[i][1], offsets[i]
            FS[:, :, at : at + w] = total.reshape(2, rows, w)
            local_pending.append(local(FS.at[c, :, at : at + w], go.at[c, :, at : at + w]))
            send(("f4", i), FS.at[o, :, at : at + w], go.at[c, :, at : at + w], partner)

        stages = {1: f1, 2: f2, 3: f3, 4: f4}

        def go_to(stage, last):
            while done[stage] < last:
                i = done[stage] + 1
                if stage < 4 and i >= RING // 2:
                    go_to(stage + 1, i - RING // 2)
                if stage > 1:
                    go_to(stage - 1, i)
                stages[stage](i)
                done[stage] = i

        def loop(n, body):
            def step(i, carry):
                body(i)
                return carry

            lax.fori_loop(0, n, step, 0)

        def put_grad(i, lhs_t, rhs):
            w = reduce[i][1]

            def one(k):
                a = lhs_t[pl.ds(pl.multiple_of(k * quarter, quarter), quarter), :]
                G[i][k] = nn(a, rhs()).astype(BF16).reshape(4, rows2, w)

            loop(4, one)

        def weight(i, at, w):
            return W[i][:, :, :, at : at + w].reshape(width, w)

        def transpose_in(src, dst, b):
            def one(k):
                at = pl.multiple_of(k * quarter, quarter)
                dst[pl.ds(at, quarter), pl.ds(pl.multiple_of(b * block, block), block)] = (
                    src[b, :, pl.ds(at, quarter)].astype(F32).T.astype(BF16)
                )

            loop(4, one)

        step_rows = 16
        iq, iv, io = gi["qk"], gi["v"], gi["out"]

        def gains():
            for k in range(8):
                kg, kx = k // 2, k % 2
                acc = None
                for ky in range(2):
                    for kc in range(2):
                        t = W[0][kg, 2 * kx + ky, 16 * kc : 16 * kc + 16, :].astype(F32)
                        acc = t if acc is None else acc + t
                GROW[:, LANES * k : LANES * (k + 1)] = acc[:8]
            GACC[...] = jnp.zeros_like(GACC)

            GACC[...] = jnp.zeros_like(GACC)

        def norm_one(r):
            at = pl.multiple_of(r * step_rows, step_rows)
            for b in range(2):
                xs = X[b, pl.ds(at, step_rows), :].astype(F32)
                r1 = lax.rsqrt(jnp.mean(xs * xs, axis=-1, keepdims=True) + EPS)
                NB[b, pl.ds(at, step_rows), :] = (xs * r1 * GROW[0:1, :]).astype(BF16)

        def first_norm():
            loop(block // step_rows, norm_one)
            transpose_in(NB, N1T, 0)
            transpose_in(NB, N1T, 1)

        def qkv():
            both = NB[...].reshape(2 * block, width)
            t = nn(both, weight(iq, 0, 2 * QH))
            for b in range(2):
                QK[b] = t[block * b : block * (b + 1)].T
            for at, w in tiles_of(VH):
                t = nn(both, weight(iv, at, w))
                for b in range(2):
                    VT[b, at : at + w, :] = t[block * b : block * (b + 1)].T.astype(BF16)

        lane = lax.broadcasted_iota(jnp.int32, (FEATS, LANES), 1)

        def place(i):
            b = i // PAIRS
            hp = lax.rem(i, PAIRS)
            return b, hp

        def slot(hp):
            return pl.ds(pl.multiple_of(FEATS * hp, FEATS), FEATS)

        def q_rows(b, hp, e):
            return QK[b, pl.ds(pl.multiple_of(hp * 2 * FDIM + e * FDIM, FDIM), FDIM), :]

        def k_rows(b, hp, e):
            return QK[b, pl.ds(pl.multiple_of(QH + hp * 2 * FDIM + e * FDIM, FDIM), FDIM), :]

        def v_slice(hp):
            return pl.ds(pl.multiple_of(hp * 2 * VDIM, 2 * VDIM), 2 * VDIM)

        def head_slice(hp, e):
            return pl.ds(pl.multiple_of(hp * 2 * VDIM + e * VDIM, VDIM), VDIM)

        def put_state(i, f0, f1, right_side, w0, w1):
            low = nt(f0, right_side)
            high = nt(f1, right_side)
            b, hp = place(i)
            ST[b, slot(hp), :] = jnp.where(lane < VDIM, low, high).astype(BF16)
            for e, t in ((0, w0), (1, w1)):
                WACC[b, pl.ds(2 * hp + e, 1), :] = t[0:1, :LANES]
                WACC[b, pl.ds(HALF_HEADS + 2 * hp + e, 1), 0 : FEATS - LANES] = t[0:1, LANES:]

        def state_step(i):
            b, hp = place(i)
            fs = [features(k_rows(b, hp, e)) for e in range(2)]
            ws = [nt(jnp.ones((8, block), BF16), f) for f in fs]
            put_state(i, fs[0], fs[1], VT[b, v_slice(hp), :], ws[0], ws[1])

        def states():
            WACC[...] = jnp.zeros_like(WACC)
            loop(2 * PAIRS, state_step)
            ST[:, COUNTS:, :] = WACC[...].astype(BF16)

        ranks = (hi, n_hi - 1 - hi)
        firsts = (x == 0, x == 1)
        doubling = n_hi == 4

        def away(n, j):
            t = hi + j if n == 0 else hi - j
            return dev(jnp.clip(t, 0, n_hi - 1), x, y, c)

        def state_rows(body):
            def step(i, z):
                body(pl.ds(pl.multiple_of(i * 16, 16), 16))
                return z

            lax.fori_loop(0, STATE_STEPS, step, 0)

        def state_x(n):
            send(("sx", n), ST.at[1 - x], SA.at[n], dev_x)

        def near(n):
            return remote(("sz", n, 0), TZ, SZ.at[n, 0], away(n, 1))

        def far(n, j):
            return remote(("sz", n, j), TY, SZ.at[n, 1], away(n, j))

        def near_sends(n):
            return lax.rem(ranks[n], 2) == 0 if doubling else ranks[n] < n_hi - 1

        def near_gets(n):
            return lax.rem(ranks[n], 2) == 1 if doubling else ranks[n] > 0

        def state_z(n):
            got(("sx", n), SA.at[n])
            for j in range(3):
                number(("sz", n, j))

            @pl.when(jnp.logical_not(near_gets(n)))
            def _():
                SZ[n, 0] = jnp.zeros((STATE, LANES), BF16)

            @pl.when(ranks[n] < 2 if doubling else ranks[n] >= 0)
            def _():
                SZ[n, 1] = jnp.zeros((STATE, LANES), BF16)

            if not doubling:

                @pl.when(near_gets(n))
                def _():
                    got(("sz", n, 0), SZ.at[n, 0])

            def add(r):
                t = ST[x, r, :].astype(F32) + SA[n, r, :].astype(F32)
                if not doubling:
                    t = t + SZ[n, 0, r, :].astype(F32)
                TZ[r, :] = t.astype(BF16)

            state_rows(add)
            pl.when(near_sends(n))(lambda: near(n).start())

        def state_far(n):
            if not doubling:
                return

            @pl.when(ranks[n] == 1)
            def _():
                got(("sz", n, 0), SZ.at[n, 0])

                def add(r):
                    TY[r, :] = (TZ[r, :].astype(F32) + SZ[n, 0, r, :].astype(F32)).astype(BF16)

                state_rows(add)
                far(n, 1).start()
                far(n, 2).start()

        def state_end(n, dst):
            if doubling:

                @pl.when(ranks[n] == 3)
                def _():
                    got(("sz", n, 0), SZ.at[n, 0])
                    got(("sz", n, 2), SZ.at[n, 1])

                @pl.when(ranks[n] == 2)
                def _():
                    got(("sz", n, 1), SZ.at[n, 1])

            def add(r):
                total = SZ[n, 0, r, :].astype(F32) + SZ[n, 1, r, :].astype(F32)
                mine = ST[x, r, :].astype(F32)
                other = SA[n, r, :].astype(F32)
                dst[x, r, :] = (total + jnp.where(firsts[n], 0.0, other)).astype(BF16)
                SB[r, :] = (total + jnp.where(firsts[n], mine, 0.0)).astype(BF16)

            state_rows(add)
            send(("sy", n), SB, dst.at[x], dev_x)

        def state_got(n, dst):
            got(("sy", n), dst.at[1 - x])

        def state_sent(n):
            sent(("sx", n))
            sent(("sy", n))
            pl.when(near_sends(n))(lambda: near(n).wait_send())
            if doubling:

                @pl.when(ranks[n] == 1)
                def _():
                    far(n, 1).wait_send()
                    far(n, 2).wait_send()

        def score_z(b, hp, e):
            qh, ql = split_low(q_rows(b, hp, e))
            kh, kl = split_low(k_rows(b, hp, e))
            return tn(jnp.concatenate([kh, kh, kl], axis=0), jnp.concatenate([qh, ql, qh], axis=0))

        def counts(buf, b):
            return buf[b, COUNTS:, :]

        def count_dot(t, f, at):
            r = nn(t[:HALF_HEADS], f[:LANES]) + nn(t[HALF_HEADS:, : FEATS - LANES], f[LANES:])
            spot = lax.broadcasted_iota(jnp.int32, r.shape, 0)
            return jnp.sum(jnp.where(spot == at, r, 0.0), axis=0, keepdims=True)

        def count_outer(t, row, at):
            spot = lax.broadcasted_iota(jnp.int32, (16, block), 0)
            first = jnp.where(spot == at, row, 0.0).astype(BF16)
            second = jnp.where(spot == HALF_HEADS + at, row, 0.0).astype(BF16)
            return jnp.concatenate([tn(t, first), tn(t[:, : FEATS - LANES], second)], axis=0)

        def att_step(i):
            b, hp = place(i)
            turned = PB[b, slot(hp), :].astype(F32).T.astype(BF16)
            tops = []
            for e in range(2):
                z = score_z(b, hp, e)
                st = (1.0 + z * FDIM**-0.5 + z * z * (0.5 / FDIM)).astype(BF16)
                fq = weighted(features(q_rows(b, hp, e)))
                num = nn(VT[b, head_slice(hp, e), :], st) + nn(turned[VDIM * e : VDIM * (e + 1)], fq)
                den = jnp.sum(st.astype(F32), axis=0, keepdims=True) + count_dot(counts(PB, b), fq, 2 * hp + e)
                NUM[b, head_slice(hp, e), :] = num
                DEN[i, e : e + 1, :] = den
                tops.append(num / den)
            ATT[b, :, v_slice(hp)] = jnp.concatenate(tops, axis=0).T.astype(BF16)

        def attention():
            loop(2 * PAIRS, att_step)

        def col(k):
            return pl.ds(pl.multiple_of(k * quarter, quarter), quarter)

        def wrow(i, k, at, w):
            return W[i][k, :, :, at : at + w].reshape(quarter, w)

        def out_proj(dst, b):
            def one(k):
                dst[:, col(k)] = nt(ATT[b], wrow(io, k, 0, VH))

            loop(4, one)

        def proj_send():
            out_proj(SND.at[0], o)
            send("x1", SND.at[0], RCV.at[0], partner)

        def norm_two(r):
            at = pl.multiple_of(r * step_rows, step_rows)
            rr = pl.ds(at, step_rows)
            x1 = X[c, rr, :].astype(F32) + (OWN[rr, :] + RCV[0, rr, :])
            X1[rr, :] = x1
            r2 = lax.rsqrt(jnp.mean(x1 * x1, axis=-1, keepdims=True) + EPS)
            NB[c, rr, :] = (x1 * r2 * GROW[1:2, :]).astype(BF16)

        def second_norm():
            out_proj(OWN, c)
            got("x1", RCV.at[0])
            loop(block // step_rows, norm_two)
            send("n2", NB.at[c], NB.at[c], partner)
            transpose_in(NB, N2T, c)
            got("n2", NB.at[o])
            transpose_in(NB, N2T, o)

        def ffn_in(j):
            base, w = parts[j]
            for at, tw in tiles_of(w):
                TG[:, 0:tw] = nn(NB[...].reshape(2 * block, width), weight(gi[f"g{j}"], at, tw))
                TU[:, 0:tw] = nn(NB[...].reshape(2 * block, width), weight(gi[f"u{j}"], at, tw))
                lo = base + at

                def one(r):
                    rr = pl.ds(pl.multiple_of(r * 64, 64), 64)
                    gate, up = TG[rr, 0:tw], TU[rr, 0:tw]
                    sg = 1.0 / (1.0 + jnp.exp(-gate))
                    silu = gate * sg
                    HID[rr, lo : lo + tw] = (silu * up).astype(BF16)
                    CA[rr, lo : lo + tw] = (up * sg * (1.0 + gate * (1.0 - sg))).astype(BF16)
                    CB[rr, lo : lo + tw] = silu.astype(BF16)

                loop(2 * block // 64, one)
        def ffn_back(j):
            base, w = parts[j]
            i = gi[f"d{j}"]
            for at, tw in tiles_of(w):
                TG[:, 0:tw] = nn(DY[...].reshape(2 * block, width), weight(i, at, tw))
                lo = base + at

                def one(r):
                    rr = pl.ds(pl.multiple_of(r * 64, 64), 64)
                    dh = TG[rr, 0:tw]
                    CA[rr, lo : lo + tw] = (dh * CA[rr, lo : lo + tw].astype(F32)).astype(BF16)
                    CB[rr, lo : lo + tw] = (dh * CB[rr, lo : lo + tw].astype(F32)).astype(BF16)

                loop(2 * block // 64, one)

        def tokens_of(b):
            return pl.ds(pl.multiple_of(b * block, block), block)

        def dn2(dst, b):
            def one(k):
                acc = None
                for j, (base, w) in enumerate(parts):
                    for buf, i in ((CA, gi[f"g{j}"]), (CB, gi[f"u{j}"])):
                        t = nt(buf[tokens_of(b), base : base + w], wrow(i, k, 0, w))
                        acc = t if acc is None else acc + t
                dst[:, col(k)] = acc

            loop(4, one)

        def dn2_send():
            sent("x1")
            dn2(SND.at[0], o)
            send("dn2", SND.at[0], RCV.at[1], partner)
            dn2(OWN, c)

        def norm_two_back(r):
            at = pl.multiple_of(r * step_rows, step_rows)
            rr = pl.ds(at, step_rows)
            d = OWN[rr, :] + RCV[1, rr, :]
            x1 = X1[rr, :]
            r2 = lax.rsqrt(jnp.mean(x1 * x1, axis=-1, keepdims=True) + EPS)
            t = d * (x1 * r2)
            GACC[8:16, :] += t[:8] + t[8:]
            a2 = d * GROW[1:2, :]
            dx = DY[c, rr, :].astype(F32) + (
                r2 * a2 - x1 * (r2 * r2 * r2) * jnp.mean(a2 * x1, axis=-1, keepdims=True)
            )
            din_ref[rr, :] = dx
            NB[c, rr, :] = dx.astype(BF16)

        def second_norm_back():
            got("dn2", RCV.at[1])
            sent("n2")
            loop(block // step_rows, norm_two_back)
            send("dx1", NB.at[c], NB.at[c], partner)
            transpose_in(NB, DYT, c)

        def datt():
            got("dx1", NB.at[o])
            transpose_in(NB, DYT, o)
            for at, tw in tiles_of(VH):
                t = nn(NB[...].reshape(2 * block, width), weight(io, at, tw))
                for b in range(2):
                    DATT[b, at : at + tw, :] = t[block * b : block * (b + 1)].T

        def back_state_step(i):
            b, hp = place(i)
            fs, ws = [], []
            for e in range(2):
                hs = head_slice(hp, e)
                datt, num, den = DATT[b, hs, :], NUM[b, hs, :], DEN[i, e : e + 1, :]
                dd = (-jnp.sum(datt * num, axis=0, keepdims=True) / (den * den)).astype(BF16)
                DNUM[b, hs, :] = (datt / den).astype(BF16)
                DDEN[i, e : e + 1, :] = dd.astype(F32)
                f = features(q_rows(b, hp, e))
                fs.append(f)
                ws.append(nt(jnp.broadcast_to(dd, (8, block)), f))
            put_state(i, fs[0], fs[1], DNUM[b, v_slice(hp), :], ws[0], ws[1])

        def back_states():
            WACC[...] = jnp.zeros_like(WACC)
            state_sent(0)
            loop(2 * PAIRS, back_state_step)
            ST[:, COUNTS:, :] = WACC[...].astype(BF16)

        zeros_head = jnp.zeros((VDIM, block), BF16)

        def masked(t, e):
            return jnp.concatenate([zeros_head, t] if e else [t, zeros_head], axis=0)

        def back_step(i):
            b, hp = place(i)
            for e in range(2):
                hs = head_slice(hp, e)
                q, kk = q_rows(b, hp, e), k_rows(b, hp, e)
                qh, ql = split_low(q)
                kh, kl = split_low(kk)
                z = tn(jnp.concatenate([kh, kh, kl], axis=0), jnp.concatenate([qh, ql, qh], axis=0))
                st = (1.0 + z * FDIM**-0.5 + z * z * (0.5 / FDIM)).astype(BF16)
                dnum, dden = DNUM[b, hs, :], DDEN[i, e : e + 1, :]
                ds = (tn(VT[b, hs, :], dnum) + dden).astype(BF16).astype(F32)
                dz = (ds * (FDIM**-0.5 + z * (1.0 / FDIM))).astype(BF16)
                t = nn(jnp.concatenate([kh, kl], axis=0), dz)
                dq = t[:FDIM] + t[FDIM:]
                t = nt(jnp.concatenate([qh, ql], axis=0), dz)
                dk = t[:FDIM] + t[FDIM:]
                DV[b, hs, :] = nt(dnum, st)
                df = nn(PB[b, slot(hp), :], masked(dnum, e)) + count_outer(counts(PB, b), dden, 2 * hp + e)
                DQK[b, pl.ds(pl.multiple_of(hp * 2 * FDIM + e * FDIM, FDIM), FDIM), :] = dq + features_back(q, df)
                DQK[b, pl.ds(pl.multiple_of(QH + hp * 2 * FDIM + e * FDIM, FDIM), FDIM), :] = dk

        def back_rows(lo, n):
            def step(i, z):
                back_step(lo + i)
                return z

            lax.fori_loop(0, n, step, 0)

        def y_part(dst, b):
            def one(k):
                acc = None
                for j, (base, w) in enumerate(parts):
                    t = nt(HID[tokens_of(b), base : base + w], wrow(gi[f"d{j}"], k, 0, w))
                    acc = t if acc is None else acc + t
                dst[:, col(k)] = acc

            loop(4, one)

        def finish(r):
            rr = pl.ds(pl.multiple_of(r * step_rows, step_rows), step_rows)
            out_ref[rr, :] = (X1[rr, :] + (OWN[rr, :] + RCV[2, rr, :])).astype(BF16)

        def y_send():
            y_part(SND.at[1], o)
            send("y", SND.at[1], RCV.at[2], partner)
            y_part(OWN, c)

        def y_end():
            got("y", RCV.at[2])
            loop(block // step_rows, finish)

        def key_step(i):
            b, hp = place(i)
            turned = PX[b, slot(hp), :].astype(F32).T.astype(BF16)
            for e in range(2):
                hs = head_slice(hp, e)
                kk = k_rows(b, hp, e)
                df = nn(PX[b, slot(hp), :], masked(VT[b, hs, :], e)) + count_outer(
                    counts(PX, b), jnp.ones((1, block), F32), 2 * hp + e
                )
                kr = pl.ds(pl.multiple_of(QH + hp * 2 * FDIM + e * FDIM, FDIM), FDIM)
                DQK[b, kr, :] += features_back(kk, df)
                DV[b, hs, :] += nn(turned[VDIM * e : VDIM * (e + 1)], weighted(features(kk)))

        def keys_back():
            loop(2 * PAIRS, key_step)
            for b in range(2):
                DQKV[b, :, 0 : 2 * QH] = DQK[b].T.astype(BF16)
                for at, tw in tiles_of(VH):
                    DQKV[b, :, 2 * QH + at : 2 * QH + at + tw] = DV[b, at : at + tw, :].T.astype(BF16)

        def dn1(dst, b):
            def one(k):
                dst[:, col(k)] = nt(DQKV[b, :, : 2 * QH], wrow(iq, k, 0, 2 * QH)) + nt(
                    DQKV[b, :, 2 * QH :], wrow(iv, k, 0, VH)
                )

            loop(4, one)

        def dn1_send():
            sent("dn2")
            dn1(SND.at[0], o)
            send("dn1", SND.at[0], RCV.at[0], partner)
            dn1(OWN, c)

        def norm_one_back(r):
            rr = pl.ds(pl.multiple_of(r * step_rows, step_rows), step_rows)
            d = OWN[rr, :] + RCV[0, rr, :]
            xs = X[c, rr, :].astype(F32)
            r1 = lax.rsqrt(jnp.mean(xs * xs, axis=-1, keepdims=True) + EPS)
            t = d * (xs * r1)
            GACC[0:8, :] += t[:8] + t[8:]
            a1 = d * GROW[0:1, :]
            din_ref[rr, :] += r1 * a1 - xs * (r1 * r1 * r1) * jnp.mean(a1 * xs, axis=-1, keepdims=True)

        def first_norm_back():
            got("dn1", RCV.at[0])
            loop(block // step_rows, norm_one_back)
            sum_a = jnp.sum(GACC[0:8, :], axis=0, keepdims=True)
            gf = jnp.sum(GACC[8:16, :], axis=0, keepdims=True)
            last = ri["gain"]
            for k in range(4):
                row = lax.broadcasted_iota(jnp.int32, (LANES, quarter), 0)
                sl = slice(quarter * k, quarter * (k + 1))
                mat = jnp.where(row == 0, sum_a[:, sl], 0.0) + jnp.where(row == 1, gf[:, sl], 0.0)
                G[last][k] = mat.T.astype(BF16).reshape(4, rows2, LANES)
        def part_of(buf, j):
            base, w = parts[j]
            return lambda: buf[:, base : base + w]

        def grad(name):
            kind = name.rstrip("0123456789")
            if kind == "d":
                put_grad(ri[name], DYT, part_of(HID, int(name[1:])))
            elif kind == "g":
                put_grad(ri[name], N2T, part_of(CA, int(name[1:])))
            elif kind == "u":
                put_grad(ri[name], N2T, part_of(CB, int(name[1:])))
            elif name == "out":
                put_grad(ri[name], DYT, lambda: ATT[...].reshape(2 * block, VH))
            elif name == "qk":
                put_grad(ri[name], N1T, lambda: DQKV[:, :, 0 : 2 * QH].reshape(2 * block, 2 * QH))
            elif name == "v":
                put_grad(ri[name], N1T, lambda: DQKV[:, :, 2 * QH :].reshape(2 * block, VH))

        def adv(st, name):
            go_to(st, ri[name])

        for i in range(len(gather)):
            e0(i)
        send("x", X.at[c], X.at[c], partner)
        send("dy", DY.at[c], DY.at[c], partner)
        ga(1, 0)
        gstep(-1)
        gstep(0)
        transpose_in(DY, DYT, c)
        got("x", X.at[o])
        got("dy", DY.at[o])
        transpose_in(DY, DYT, o)
        gstep(1, 2, 1)
        z1()
        gains()
        first_norm()
        gstep(2, 2, 1)
        ga(2, 4)
        ga(4, 2)
        qkv()
        states()
        state_x(0)
        gstep(3, 2, 1)
        z2()
        gstep(4, 2, 1)
        state_z(0)
        gstep(5, 4, 1)
        state_far(0)
        z3()
        gstep(6, 5, 1)
        state_end(0, PB)
        gstep(7, 5, 1)
        state_got(0, PB)
        gstep(8, 5, 2)
        attention()
        gstep(9, 5, 2)
        proj_send()
        second_norm()
        gstep(10, 5, 2)
        ffn_in(0)
        grad("d0")
        zf1()
        ffn_in(1)
        grad("d1")
        adv(1, "d1")
        ga(3, 11)
        ga(4, 9)
        ffn_in(2)
        grad("d2")
        adv(1, "d2")
        z4()
        ffn_back(0)
        adv(2, "d1")
        grad("g0")
        adv(1, "g0")
        ga(4, 10)
        ffn_back(1)
        adv(2, "d2")
        adv(3, "d1")
        ga(4, 11)
        ffn_back(2)
        dn2_send()
        grad("u0")
        adv(1, "u0")
        second_norm_back()
        adv(4, "d1")
        datt()
        back_states()
        state_x(1)
        grad("g1")
        adv(2, "g0")
        adv(3, "d2")
        adv(1, "g1")
        state_z(1)
        zf2()
        adv(4, "d2")
        grad("u1")
        adv(2, "u0")
        adv(3, "g0")
        adv(1, "u1")
        back_rows(0, 4)
        state_far(1)
        grad("g2")
        adv(2, "g1")
        adv(3, "u0")
        adv(4, "g0")
        adv(1, "g2")
        zf3()
        state_end(1, PX)
        back_rows(4, 4)
        grad("u2")
        adv(2, "u1")
        adv(3, "g1")
        adv(4, "u0")
        adv(1, "u2")
        zf4()
        y_send()
        grad("out")
        state_got(1, PX)
        keys_back()
        grad("qk")
        adv(2, "g2")
        adv(3, "u1")
        adv(4, "g1")
        adv(1, "out")
        y_end()
        adv(2, "u2")
        adv(3, "g2")
        adv(4, "u1")
        adv(1, "qk")
        grad("v")
        adv(1, "v")
        dn1_send()
        adv(2, "out")
        adv(3, "u2")
        adv(4, "g2")
        first_norm_back()
        adv(1, "gain")
        adv(2, "qk")
        adv(3, "out")
        adv(4, "u2")
        adv(2, "v")
        adv(3, "qk")

        n = len(reduce)
        for k in range(n, n + 4):
            for st in (1, 2, 3, 4):
                go_to(st, min(n - 1, k - st))
        for i in range(n):
            got(("f4", i), go.at[o, :, offsets[i] : offsets[i] + reduce[i][1]])
        for d in local_pending:
            d.wait()
        state_sent(1)
        for d in pending.values():
            d.wait_send()

    return kernel


def call_kernel(tok, cot, shards, seq_size, ff, ff_half):
    block, width = tok.shape
    gather, reduce = plan(ff_half)
    rows = width // 32
    vmem = pltpu.VMEM
    any_spec = pl.BlockSpec(memory_space=pl.ANY)
    vmem_spec = pl.BlockSpec(memory_space=vmem)
    total_width = sum(w for _, w in reduce)
    pack_width = sum(w for _, w in gather)
    state = vmem((2, STATE, LANES), BF16)
    scratch = [vmem((4, 4, 2 * (16 if name == "gain" else rows), w), BF16) for name, w in gather]
    scratch += [vmem((4, 4, 2 * rows, w), BF16) for _, w in reduce]
    scratch += [
        vmem((rows, pack_width), BF16),
        vmem((RING, 2, 4, 2 * rows, PIECE), BF16),
        vmem((RING, 4, 2 * rows, PIECE), BF16),
        vmem((RING, 3, 2 * rows, PIECE), BF16),
        vmem((3, 4, 2 * rows, PIECE), BF16),
        vmem((3, 2 * rows, PIECE), BF16),
        vmem((2, rows, total_width), F32),
        vmem((2, block, width), BF16),
        vmem((2, block, width), BF16),
        vmem((2, block, width), BF16),
        vmem((width, 2 * block), BF16),
        vmem((width, 2 * block), BF16),
        vmem((width, 2 * block), BF16),
        vmem((2 * block, ff_half), BF16),
        vmem((2 * block, ff_half), BF16),
        vmem((2 * block, ff_half), BF16),
        vmem((block, width), F32),
        vmem((2, block, width), F32),
        vmem((3, block, width), F32),
        vmem((block, width), F32),
        vmem((2, VH, block), F32),
        vmem((2, VH, block), F32),
        vmem((2, 2 * QH, block), F32),
        vmem((2, VH, block), BF16),
        vmem((2, block, VH), BF16),
        vmem((2 * PAIRS, 8, block), F32),
        vmem((2, VH, block), BF16),
        vmem((2 * PAIRS, 8, block), F32),
        vmem((2, 2 * QH, block), F32),
        vmem((2, VH, block), F32),
        vmem((2, block, 2 * QH + VH), BF16),
        state,
        vmem((2, STATE, LANES), BF16),
        vmem((2, 2, STATE, LANES), BF16),
        vmem((STATE, LANES), BF16),
        vmem((STATE, LANES), BF16),
        vmem((STATE, LANES), BF16),
        state,
        state,
        vmem((2, 16, LANES), F32),
        vmem((2 * block, 256), F32),
        vmem((2 * block, 256), F32),
        vmem((8, width), F32),
        vmem((16, width), F32),
        pltpu.SemaphoreType.DMA((n_messages(gather, reduce),)),
        pltpu.SemaphoreType.DMA((n_messages(gather, reduce),)),
        pltpu.SemaphoreType.DMA((2 + len(reduce),)),
    ]
    out_shape = [
        jax.ShapeDtypeStruct((block, width), BF16),
        jax.ShapeDtypeStruct((block, width), F32),
        jax.ShapeDtypeStruct((2, rows, total_width), F32),
    ]
    return pl.pallas_call(
        make_kernel(seq_size, block, width, ff, ff_half),
        out_shape=out_shape,
        in_specs=[any_spec] * 2 + [vmem_spec] * len(shards),
        out_specs=[vmem_spec] * 2 + [any_spec],
        scratch_shapes=scratch,
        compiler_params=pltpu.CompilerParams(
            collective_id=0, has_side_effects=True, vmem_limit_bytes=62 * 2**20
        ),
    )(tok, cot, *shards)


def n_messages(gather, reduce):
    return 7 * len(gather) + 6 * RING + len(reduce) + 24


def call_finish(output, input_grad, grads, ff, ff_half):
    block, width = output.shape
    rows = grads.shape[1]
    _, reduce = plan(ff_half)
    at = dict(zip([name for name, _ in reduce], offsets_of(reduce)))
    parts = pieces_of(ff_half)
    vmem_spec = pl.BlockSpec(memory_space=pltpu.VMEM)
    hbm_spec = pl.BlockSpec(memory_space=pltpu.HBM)

    def kernel(o_in, i_in, g_hbm, o_out, i_out, ag, qg, kg, vg, og, fg, gg, ug, dg, g_in, sems):
        c2 = pltpu.make_async_copy(g_hbm, g_in, sems.at[2])
        c2.start()
        c0 = pltpu.make_async_copy(o_in, o_out, sems.at[0])
        c1 = pltpu.make_async_copy(i_in, i_out, sems.at[1])
        c0.start()
        c1.start()
        c2.wait()
        gain = (g_in[0, :, at["gain"] : at["gain"] + LANES] + g_in[1, :, at["gain"] : at["gain"] + LANES]).T
        ag[...] = gain[0:1, :rows]
        fg[...] = gain[1:2, :rows]
        for h in range(2):
            qg[:, QH * h : QH * (h + 1)] = g_in[h, :, at["qk"] : at["qk"] + QH]
            kg[:, QH * h : QH * (h + 1)] = g_in[h, :, at["qk"] + QH : at["qk"] + 2 * QH]
            vg[:, VH * h : VH * (h + 1)] = g_in[h, :, at["v"] : at["v"] + VH]
            og[:, VH * h : VH * (h + 1)] = g_in[h, :, at["out"] : at["out"] + VH]
            for j, (base, w) in enumerate(parts):
                lo = ff_half * h + base
                have = min(w, ff - lo)
                for ref, letter in ((gg, "g"), (ug, "u"), (dg, "d")):
                    a = at[f"{letter}{j}"]
                    ref[:, lo : lo + have] = g_in[h, :, a : a + have]
        c0.wait()
        c1.wait()

    shapes = [(1, rows), (rows, 2 * QH), (rows, 2 * QH), (rows, 2 * VH), (rows, 2 * VH), (1, rows)] + [(rows, ff)] * 3
    return pl.pallas_call(
        kernel,
        out_shape=[jax.ShapeDtypeStruct(output.shape, BF16), jax.ShapeDtypeStruct(input_grad.shape, F32)]
        + [jax.ShapeDtypeStruct(n, F32) for n in shapes],
        in_specs=[hbm_spec] * 3,
        out_specs=[hbm_spec] * 2 + [vmem_spec] * len(shapes),
        scratch_shapes=[pltpu.VMEM(grads.shape, F32), pltpu.SemaphoreType.DMA((3,))],
        compiler_params=pltpu.CompilerParams(vmem_limit_bytes=32 * 2**20),
    )(output, input_grad, grads)


def body(
    tokens, attn_gain, query_weight, key_weight, value_weight, out_weight, ffn_gain, gate_weight, up_weight, down_weight, cotangent
):
    seq_size = lax.axis_size("seq")
    members = seq_size // 8
    _, block, width = tokens.shape
    ff = gate_weight.shape[1]
    ff_half = LANES * ((ff + 2 * LANES - 1) // (2 * LANES))
    few = attn_gain.shape[0]
    groups = [[(g * members + m) * 2 + x for m in range(members)] for g in range(4) for x in range(2)]

    shards = [attn_gain, query_weight, key_weight, value_weight, out_weight.T, ffn_gain, gate_weight, up_weight, down_weight.T]
    if members > 1:
        shards = [
            lax.all_gather(a, "seq", axis_index_groups=groups, axis=0, tiled=True) for a in shards
        ]
    shards = [a.reshape(1, -1) if a.ndim == 1 else a for a in shards]

    def turn(t):
        if members == 1:
            return t
        return t.reshape(block, 4, members, 2, 4, few).transpose(0, 1, 3, 4, 2, 5).reshape(block, width)

    def turn_back(t):
        if members == 1:
            return t
        return t.reshape(block, 4, 2, 4, members, few).transpose(0, 1, 4, 2, 3, 5).reshape(block, width)

    output, input_grad, grads = call_kernel(turn(tokens[0]), turn(cotangent[0]), shards, seq_size, ff, ff_half)
    if members == 1:
        o, i, ag, qg, kg, vg, og, fg, gg, ug, dg = call_finish(output, input_grad, grads, ff, ff_half)
        return o[None], i[None], ag[0], qg, kg, vg, og.T, fg[0], gg, ug, dg.T
    grads = lax.psum_scatter(grads, "seq", scatter_dimension=1, axis_index_groups=groups, tiled=True)
    _, reduce = plan(ff_half)
    by = {name: grads[:, :, a : a + w] for (name, w), a in zip(reduce, offsets_of(reduce))}
    n_parts = len(pieces_of(ff_half))

    def joined(a):
        return jnp.concatenate([a[0], a[1]], axis=1)

    def ff_joined(letter):
        return joined(jnp.concatenate([by[f"{letter}{j}"] for j in range(n_parts)], axis=2))[:, :ff]

    gain = by["gain"][0] + by["gain"][1]
    return (
        turn_back(output)[None],
        turn_back(input_grad)[None],
        gain[:, 0],
        joined(by["qk"][:, :, :QH]),
        joined(by["qk"][:, :, QH:]),
        joined(by["v"]),
        joined(by["out"]).T,
        gain[:, 1],
        ff_joined("g"),
        ff_joined("u"),
        ff_joined("d").T,
    )


def solution(mesh):
    both = ("seq", "dp")
    row, column, whole = P(both, None), P(None, both), P("dp", "seq", None)
    return jax.shard_map(
        body,
        mesh=mesh,
        in_specs=(whole, P(both), row, row, row, column, P(both), row, row, column, whole),
        out_specs=(whole, whole, P(both), row, row, row, column, P(both), row, row, column),
        check_vma=False,
    )
```

```python
import jax
import jax.numpy as jnp
from jax import lax
from jax.experimental import pallas as pl
from jax.experimental.pallas import tpu as pltpu
from jax.sharding import PartitionSpec as P

HEADS = 16
FDIM = 16
VDIM = 64
EPS = 1e-05
LIN = FDIM**-0.25
QUAD = (2.0 * FDIM) ** -0.5
SHIFTS = FDIM // 2
HALF = FDIM // 2
FEATS = FDIM * (SHIFTS + 2)
HALF_HEADS = HEADS // 2
QH = HALF_HEADS * FDIM
VH = HALF_HEADS * VDIM
PAIRS = HALF_HEADS // 2
COUNTS = PAIRS * FEATS
STATE = COUNTS + 16
STATE_STEPS = STATE // 16
SPLIT = 96
LANES = 128
ALIKE = (("g0",), ())
PIECE = 512
RING = 6
MESH = pl.DeviceIdType.MESH
F32 = jnp.float32
BF16 = jnp.bfloat16


def pieces_of(width):
    out, at = [], 0
    while at < width:
        out.append((at, min(PIECE, width - at)))
        at += PIECE
    return out


def tiles_of(width):
    out, at = [], 0
    while at < width:
        out.append((at, min(256, width - at)))
        at += 256
    return out


def nn(a, b):
    return jnp.dot(a, b, preferred_element_type=F32)


def nt(a, b):
    return lax.dot_general(a, b, (((1,), (1,)), ((), ())), preferred_element_type=F32)


def tn(a, b):
    return lax.dot_general(a, b, (((0,), (0,)), ((), ())), preferred_element_type=F32)


def ahead(t, d):
    return t if d == 0 else pltpu.roll(t, FDIM - d, 0)


def behind(t, d):
    return t if d == 0 else pltpu.roll(t, d, 0)


def features(u):
    rows = [u * ahead(u, d) * QUAD for d in range(SHIFTS)]
    spot = lax.broadcasted_iota(jnp.int32, u.shape, 0)
    last = jnp.where(spot < HALF, u * ahead(u, HALF) * QUAD, jnp.where(spot == HALF, 1.0, 0.0))
    return jnp.concatenate(rows + [last, u * LIN], axis=0).astype(BF16)


def weighted(f):
    at = FDIM * SHIFTS
    scale = jnp.where(lax.broadcasted_iota(jnp.int32, (FDIM, f.shape[1]), 0) < HALF, 2.0, 1.0).astype(BF16)
    return jnp.concatenate([f[:FDIM], f[FDIM:at] * 2, f[at : at + FDIM] * scale, f[at + FDIM :]], axis=0)


def features_back(u, df):
    at = FDIM * SHIFTS
    total = df[at + FDIM :] * LIN
    for d in range(SHIFTS + 1):
        t = df[FDIM * d : FDIM * (d + 1)] * (QUAD * (2.0 if d else 1.0))
        if d == HALF:
            t = jnp.where(lax.broadcasted_iota(jnp.int32, t.shape, 0) < HALF, t, 0.0)
        total = total + t * ahead(u, d) + behind(t * u, d)
    return total


def split_low(u):
    high = u.astype(BF16)
    return high, (u - high.astype(F32)).astype(BF16)


def plan(ff_half):
    parts = pieces_of(ff_half)
    gather = [("gain", LANES), ("qk", 2 * QH), ("v", VH), ("out", VH)]
    for j, (_, w) in enumerate(parts):
        gather += [(f"g{j}", w), (f"u{j}", w)]
    gather += [(f"d{j}", w) for j, (_, w) in enumerate(parts)][1:]
    gather += [("d0", parts[0][1])]
    reduce = [(f"d{j}", w) for j, (_, w) in enumerate(parts)]
    for j, (_, w) in enumerate(parts):
        reduce += [(f"g{j}", w), (f"u{j}", w)]
    reduce += [("out", VH), ("qk", 2 * QH), ("v", VH), ("gain", LANES)]
    return gather, reduce


def offsets_of(chunks):
    out, at = [], 0
    for _, w in chunks:
        out.append(at)
        at += w
    return out


def make_kernel(seq_size, block, width, ff, ff_half):
    gather, reduce = plan(ff_half)
    parts = pieces_of(ff_half)
    n_parts = len(parts)
    gi = {name: i for i, (name, _) in enumerate(gather)}
    ri = {name: i for i, (name, _) in enumerate(reduce)}
    members = seq_size // 8
    n_hi = seq_size // 2
    rows = width // 32
    rows2 = 2 * rows
    quarter = width // 4
    offsets = offsets_of(reduce)
    pack_at = offsets_of(gather)

    def kernel(*refs):
        it = iter(refs)
        take = lambda n: [next(it) for _ in range(n)]
        tok, cot = take(2)
        attn_in, q_in, k_in, v_in, o_in, ffn_in_gain, g_in, u_in, d_in = take(9)
        out_ref, din_ref, go = take(3)
        W = take(len(gather))
        G = take(len(reduce))
        (PK, R1, R2, R3, RZ, RY, FS, X, DY, NB, N1T, N2T, DYT, HID, CA, CB, X1, SND, RCV, OWN) = take(20)
        (NUM, DATT, QK, VT, ATT, DEN, DNUM, DDEN, DQK, DV, DQKV) = take(11)
        (ST, SA, SZ, TZ, TY, SB, PB, PX, WACC, TG, TU, GROW, GACC) = take(13)
        ss, rs, ls = take(3)

        s, dp = lax.axis_index("seq"), lax.axis_index("dp")
        hi, x = s // 2, lax.rem(s, 2)
        y, c = dp // 2, lax.rem(dp, 2)
        g, m = hi // members, lax.rem(hi, members)
        o = 1 - c
        p, pab = 2 * x + y, 2 * (1 - x) + (1 - y)

        def dev(hi_, x_, y_, c_):
            return (hi_ * 2 + x_, y_ * 2 + c_)

        partner = dev(hi, x, y, o)
        dev_x, dev_y = dev(hi, 1 - x, y, c), dev(hi, x, 1 - y, c)

        def roles(flip):
            nx, ny = x + flip * (1 - 2 * x), y + (1 - flip) * (1 - 2 * y)
            return dev(hi, nx, ny, c), 2 * nx + ny

        mixed = roles(o) + roles(c)
        alike = roles(1) + roles(0)

        def way(name, phase):
            return alike if name in ALIKE[phase] else mixed

        ups = [lax.rem(g + j, 4) for j in range(4)]
        downs = [lax.rem(g + 4 - j, 4) for j in range(4)]
        dev_up = [dev(u * members + m, x, y, c) for u in ups]
        right = dev(jnp.minimum(hi + 1, n_hi - 1), x, y, c)
        left = dev(jnp.maximum(hi - 1, 0), x, y, c)

        n_local = [0]
        local_pending = []

        def local(src, dst):
            d = pltpu.make_async_copy(src, dst, ls.at[n_local[0]])
            n_local[0] += 1
            d.start()
            return d

        barrier = pltpu.get_barrier_semaphore()
        greet = [partner, dev_x, dev_y] + dev_up[1:]
        for d in greet:
            pl.semaphore_signal(barrier, inc=1, device_id=d, device_id_type=MESH)
        if members > 1:

            @pl.when(hi < n_hi - 1)
            def _():
                pl.semaphore_signal(barrier, inc=1, device_id=right, device_id_type=MESH)

            @pl.when(hi > 0)
            def _():
                pl.semaphore_signal(barrier, inc=1, device_id=left, device_id_type=MESH)

        numbers = {}
        pending = {}

        def number(key):
            return numbers.setdefault(key, len(numbers))

        def remote(key, src, dst, to):
            i = number(key)
            return pltpu.make_async_remote_copy(
                src_ref=src, dst_ref=dst, send_sem=ss.at[i], recv_sem=rs.at[i], device_id=to, device_id_type=MESH
            )

        def send(key, src, dst, to):
            if key in pending:
                sent(key)
            d = remote(key, src, dst, to)
            d.start()
            pending[key] = d

        def sent(key):
            pending.pop(key).wait_send()

        def got(key, ref):
            remote(key, ref, ref, partner).wait_recv()

        def pack(i, lower, upper):
            w = gather[i][1]
            r = 16 if i == 0 else rows
            mine = W[i].at[g, p, pl.ds(pl.multiple_of(r * c, r), r)]
            stage = PK.at[0:r, pack_at[i] : pack_at[i] + w]

            @pl.when(c == 0)
            def _():
                mine[...] = lower()
                stage[...] = upper()

            @pl.when(c == 1)
            def _():
                mine[...] = upper()
                stage[...] = lower()

        def e0_send(i):
            w = gather[i][1]
            r = 16 if i == 0 else rows
            mine = W[i].at[g, p, pl.ds(pl.multiple_of(r * c, r), r)]
            send(("e0", i), PK.at[0:r, pack_at[i] : pack_at[i] + w], mine, partner)

        def ff_piece(ref, at, w):
            have = min(w, ff - at)
            if have == w:
                return ref[:, at : at + w]
            return jnp.concatenate([ref[:, at : at + have], jnp.zeros((ref.shape[0], w - have), BF16)], axis=1)

        def gain_block():
            out = jnp.zeros((16, LANES), F32)
            lanes = lax.broadcasted_iota(jnp.int32, (16, LANES), 1) // rows
            row = lax.broadcasted_iota(jnp.int32, (16, LANES), 0)
            for n, ref in enumerate((attn_in, ffn_in_gain)):
                t = jnp.concatenate([ref[...].astype(F32)] * (LANES // rows), axis=1)
                out = jnp.where((lanes == dp) & (row == n), t, out)
            return out.astype(BF16)

        def e0(i):
            name, w = gather[i]
            if name == "gain":
                pack(i, gain_block, gain_block)
            elif name == "qk":
                pack(
                    i,
                    lambda: jnp.concatenate([q_in[:, :QH], k_in[:, :QH]], axis=1),
                    lambda: jnp.concatenate([q_in[:, QH:], k_in[:, QH:]], axis=1),
                )
            elif name == "v":
                pack(i, lambda: v_in[:, :VH], lambda: v_in[:, VH:])
            elif name == "out":
                pack(i, lambda: o_in[:, :VH], lambda: o_in[:, VH:])
            else:
                at = parts[int(name[1:])][0]
                ref = {"g": g_in, "u": u_in, "d": d_in}[name[0]]
                pack(i, lambda: ff_piece(ref, at, w), lambda: ff_piece(ref, ff_half + at, w))

        def e1(i):
            r = 16 if i == 0 else rows
            got(("e0", i), W[i].at[g, p, pl.ds(pl.multiple_of(r * o, r), r)])
            for j in (1, 2, 3):
                send(("e1", i, j), W[i].at[g, p], W[i].at[g, p], dev_up[j])

        def e2(i):
            dev_a, pa, dev_b, pb = way(gather[i][0], 0)
            for j in (1, 2, 3):
                got(("e1", i, j), W[i].at[downs[j], p])
            send(("e2b", i), W[i].at[:, p], W[i].at[:, p], dev_b)
            send(("e2a", i), W[i].at[:, p], W[i].at[:, p], dev_a)

        def e3(i):
            dev_a, pa, dev_b, pb = way(gather[i][0], 0)
            got(("e2a", i), W[i].at[:, pa])
            send(("e3", i), W[i].at[:, pa], W[i].at[:, pa], dev_b)

        def e4(i):
            dev_a, pa, dev_b, pb = way(gather[i][0], 0)
            got(("e2b", i), W[i].at[:, pb])
            got(("e3", i), W[i].at[:, pab])

        iz = len(gather) - 1

        def z1():
            dev_a, pa, dev_b, pb = way(gather[iz][0], 0)
            r = rows
            got(("e0", iz), W[iz].at[g, p, pl.ds(pl.multiple_of(r * o, r), r)])
            send(("e2b", iz), W[iz].at[g, p], W[iz].at[g, p], dev_b)
            send(("e2a", iz), W[iz].at[g, p], W[iz].at[g, p], dev_a)

        def z2():
            dev_a, pa, dev_b, pb = way(gather[iz][0], 0)
            got(("e2a", iz), W[iz].at[g, pa])
            send(("e3", iz), W[iz].at[g, pa], W[iz].at[g, pa], dev_b)

        def z3():
            dev_a, pa, dev_b, pb = way(gather[iz][0], 0)
            got(("e2b", iz), W[iz].at[g, pb])
            got(("e3", iz), W[iz].at[g, pab])
            for j in (1, 2, 3):
                send(("e1", iz, j), W[iz].at[g], W[iz].at[g], dev_up[j])

        def z4():
            for j in (1, 2, 3):
                got(("e1", iz, j), W[iz].at[downs[j]])

        gathered = {1: -1, 2: -1, 3: -1, 4: -1}

        def ga(step, last):
            while gathered[step] < min(last, iz - 1):
                gathered[step] += 1
                (e1, e2, e3, e4)[step - 1](gathered[step])

        def gstep(k, l1=1, l2=1):
            ga(1, k + l1 + l2)
            ga(2, k + l2)
            ga(3, k)
            ga(4, k - 1)

        done = {1: 0, 2: 0, 3: 0, 4: 0}

        def zf1():
            w = reduce[0][1]
            for j in (1, 2, 3):
                send(("z1", j), G[0].at[ups[j]], RZ.at[j - 1, :, :, 0:w], dev_up[j])

        def zf2():
            dev_a, pa, dev_b, pb = way(reduce[0][0], 1)
            w = reduce[0][1]
            for j in (1, 2, 3):
                got(("z1", j), RZ.at[j - 1, :, :, 0:w])

            def one(k):
                total = G[0][g, k].astype(F32)
                for j in range(3):
                    total = total + RZ[j, k, :, 0:w].astype(F32)
                G[0][g, k] = total.astype(BF16)

            loop(4, one)
            for n, q in ((0, pab), (1, pb)):
                send(("z2", n), G[0].at[g, q], RY.at[n, :, 0:w], dev_b)

        def zf3():
            dev_a, pa, dev_b, pb = way(reduce[0][0], 1)
            w = reduce[0][1]
            got(("z2", 0), RY.at[0, :, 0:w])
            G[0][g, pa] = G[0][g, pa] + RY[0, :, 0:w]
            send(("z3", 0), G[0].at[g, pa], RY.at[2, :, 0:w], dev_a)
            got(("z2", 1), RY.at[1, :, 0:w])
            G[0][g, p] = G[0][g, p] + RY[1, :, 0:w]

        def zf4():
            w = reduce[0][1]
            got(("z3", 0), RY.at[2, :, 0:w])
            finish_chunk(0, G[0][g, p].astype(F32) + RY[2, :, 0:w].astype(F32))

        def f1(i):
            dev_a, pa, dev_b, pb = way(reduce[i][0], 1)
            w = reduce[i][1]
            k = i % RING
            for n, col in ((0, pab), (1, pb)):
                send(("f1", k, n), G[i].at[:, col], R1.at[k, n, :, :, 0:w], dev_b)

        def f2(i):
            dev_a, pa, dev_b, pb = way(reduce[i][0], 1)
            w = reduce[i][1]
            k = i % RING
            got(("f1", k, 0), R1.at[k, 0, :, :, 0:w])
            G[i][:, pa] = G[i][:, pa] + R1[k, 0, :, :, 0:w]
            send(("f2", k), G[i].at[:, pa], R2.at[k, :, :, 0:w], dev_a)
            got(("f1", k, 1), R1.at[k, 1, :, :, 0:w])
            G[i][:, p] = G[i][:, p] + R1[k, 1, :, :, 0:w]

        def f3(i):
            dev_a, pa, dev_b, pb = way(reduce[i][0], 1)
            w = reduce[i][1]
            k = i % RING
            got(("f2", k), R2.at[k, :, :, 0:w])
            G[i][:, p] = G[i][:, p] + R2[k, :, :, 0:w]
            for j in (1, 2, 3):
                send(("f3", k, j), G[i].at[ups[j], p], R3.at[k, j - 1, :, 0:w], dev_up[j])

        def f4(i):
            w = reduce[i][1]
            k = i % RING
            total = G[i][g, p].astype(F32)
            for j in (1, 2, 3):
                got(("f3", k, j), R3.at[k, j - 1, :, 0:w])
                total = total + R3[k, j - 1, :, 0:w].astype(F32)
            finish_chunk(i, total)

        def finish_chunk(i, total):
            w, at = reduce[i][1], offsets[i]
            FS[:, :, at : at + w] = total.reshape(2, rows, w)
            local_pending.append(local(FS.at[c, :, at : at + w], go.at[c, :, at : at + w]))
            send(("f4", i), FS.at[o, :, at : at + w], go.at[c, :, at : at + w], partner)

        stages = {1: f1, 2: f2, 3: f3, 4: f4}

        def go_to(stage, last):
            while done[stage] < last:
                i = done[stage] + 1
                if stage < 4 and i >= RING // 2:
                    go_to(stage + 1, i - RING // 2)
                if stage > 1:
                    go_to(stage - 1, i)
                stages[stage](i)
                done[stage] = i

        def loop(n, body):
            def step(i, carry):
                body(i)
                return carry

            lax.fori_loop(0, n, step, 0)

        def put_grad(i, lhs_t, rhs):
            w = reduce[i][1]

            def one(k):
                a = lhs_t[pl.ds(pl.multiple_of(k * quarter, quarter), quarter), :]
                G[i][k] = nn(a, rhs()).astype(BF16).reshape(4, rows2, w)

            loop(4, one)

        def weight(i, at, w):
            return W[i][:, :, :, at : at + w].reshape(width, w)

        def transpose_in(src, dst, b):
            def one(k):
                at = pl.multiple_of(k * quarter, quarter)
                dst[pl.ds(at, quarter), pl.ds(pl.multiple_of(b * block, block), block)] = (
                    src[b, :, pl.ds(at, quarter)].T
                )

            loop(4, one)

        step_rows = 16
        iq, iv, io = gi["qk"], gi["v"], gi["out"]

        def gains():
            for k in range(8):
                kg, kx = k // 2, k % 2
                acc = None
                for ky in range(2):
                    for kc in range(2):
                        t = W[0][kg, 2 * kx + ky, 16 * kc : 16 * kc + 16, :].astype(F32)
                        acc = t if acc is None else acc + t
                GROW[:, LANES * k : LANES * (k + 1)] = acc[:8]
            GACC[...] = jnp.zeros_like(GACC)

            GACC[...] = jnp.zeros_like(GACC)

        def norm_one(r):
            at = pl.multiple_of(r * step_rows, step_rows)
            for b in range(2):
                xs = X[b, pl.ds(at, step_rows), :].astype(F32)
                r1 = lax.rsqrt(jnp.mean(xs * xs, axis=-1, keepdims=True) + EPS)
                NB[b, pl.ds(at, step_rows), :] = (xs * r1 * GROW[0:1, :]).astype(BF16)

        def first_norm():
            loop(block // step_rows, norm_one)
            transpose_in(NB, N1T, 0)
            transpose_in(NB, N1T, 1)

        def qkv():
            both = NB[...].reshape(2 * block, width)
            t = nn(both, weight(iq, 0, 2 * QH))
            for b in range(2):
                QK[b] = t[block * b : block * (b + 1)].T
            for at, w in tiles_of(VH):
                t = nn(both, weight(iv, at, w))
                for b in range(2):
                    VT[b, at : at + w, :] = t[block * b : block * (b + 1)].T.astype(BF16)

        lane = lax.broadcasted_iota(jnp.int32, (FEATS, LANES), 1)

        def place(i):
            b = i // PAIRS
            hp = lax.rem(i, PAIRS)
            return b, hp

        def slot(hp):
            return pl.ds(pl.multiple_of(FEATS * hp, FEATS), FEATS)

        def q_rows(b, hp, e):
            return QK[b, pl.ds(pl.multiple_of(hp * 2 * FDIM + e * FDIM, FDIM), FDIM), :]

        def k_rows(b, hp, e):
            return QK[b, pl.ds(pl.multiple_of(QH + hp * 2 * FDIM + e * FDIM, FDIM), FDIM), :]

        def v_slice(hp):
            return pl.ds(pl.multiple_of(hp * 2 * VDIM, 2 * VDIM), 2 * VDIM)

        def head_slice(hp, e):
            return pl.ds(pl.multiple_of(hp * 2 * VDIM + e * VDIM, VDIM), VDIM)

        def put_state(i, f0, f1, right_side, w0, w1):
            low = nt(f0, right_side)
            high = nt(f1, right_side)
            b, hp = place(i)
            ST[b, slot(hp), :] = jnp.where(lane < VDIM, low, high).astype(BF16)
            for e, t in ((0, w0), (1, w1)):
                WACC[b, pl.ds(2 * hp + e, 1), :] = t[0:1, :LANES]
                WACC[b, pl.ds(HALF_HEADS + 2 * hp + e, 1), 0 : FEATS - LANES] = t[0:1, LANES:]

        def state_step(i):
            b, hp = place(i)
            fs = [features(k_rows(b, hp, e)) for e in range(2)]
            ws = [nt(jnp.ones((8, block), BF16), f) for f in fs]
            put_state(i, fs[0], fs[1], VT[b, v_slice(hp), :], ws[0], ws[1])

        def states():
            WACC[...] = jnp.zeros_like(WACC)
            loop(2 * PAIRS, state_step)
            ST[:, COUNTS:, :] = WACC[...].astype(BF16)

        ranks = (hi, n_hi - 1 - hi)
        firsts = (x == 0, x == 1)
        doubling = n_hi == 4

        def away(n, j):
            t = hi + j if n == 0 else hi - j
            return dev(jnp.clip(t, 0, n_hi - 1), x, y, c)

        def state_rows(body):
            def step(i, z):
                body(pl.ds(pl.multiple_of(i * 16, 16), 16))
                return z

            lax.fori_loop(0, STATE_STEPS, step, 0)

        def start_split(d, key, src, dst, to):
            i = number(key)
            for lo in range(0, STATE, SPLIT):
                rr = pl.ds(lo, min(SPLIT, STATE - lo))
                pltpu.make_async_remote_copy(
                    src_ref=src.at[rr],
                    dst_ref=dst.at[rr],
                    send_sem=ss.at[i],
                    recv_sem=rs.at[i],
                    device_id=to,
                    device_id_type=MESH,
                ).start()
            return d

        def send_split(key, src, dst, to):
            pending[key] = start_split(remote(key, src, dst, to), key, src, dst, to)

        def state_x(n):
            send_split(("sx", n), ST.at[1 - x], SA.at[n], dev_x)

        def near(n):
            return remote(("sz", n, 0), TZ, SZ.at[n, 0], away(n, 1))

        def far(n, j):
            return remote(("sz", n, j), TY, SZ.at[n, 1], away(n, j))

        def near_sends(n):
            return lax.rem(ranks[n], 2) == 0 if doubling else ranks[n] < n_hi - 1

        def near_gets(n):
            return lax.rem(ranks[n], 2) == 1 if doubling else ranks[n] > 0

        def state_z(n):
            got(("sx", n), SA.at[n])
            for j in range(3):
                number(("sz", n, j))

            @pl.when(jnp.logical_not(near_gets(n)))
            def _():
                SZ[n, 0] = jnp.zeros((STATE, LANES), BF16)

            @pl.when(ranks[n] < 2 if doubling else ranks[n] >= 0)
            def _():
                SZ[n, 1] = jnp.zeros((STATE, LANES), BF16)

            if not doubling:

                @pl.when(near_gets(n))
                def _():
                    got(("sz", n, 0), SZ.at[n, 0])

            def add(r):
                t = ST[x, r, :].astype(F32) + SA[n, r, :].astype(F32)
                if not doubling:
                    t = t + SZ[n, 0, r, :].astype(F32)
                TZ[r, :] = t.astype(BF16)

            state_rows(add)
            pl.when(near_sends(n))(
                lambda: start_split(near(n), ("sz", n, 0), TZ, SZ.at[n, 0], away(n, 1)) and None
            )

        def state_far(n):
            if not doubling:
                return

            @pl.when(ranks[n] == 1)
            def _():
                got(("sz", n, 0), SZ.at[n, 0])

                def add(r):
                    TY[r, :] = (TZ[r, :].astype(F32) + SZ[n, 0, r, :].astype(F32)).astype(BF16)

                state_rows(add)
                for j in (1, 2):
                    start_split(far(n, j), ("sz", n, j), TY, SZ.at[n, 1], away(n, j))

        def state_end(n, dst):
            if doubling:

                @pl.when(ranks[n] == 3)
                def _():
                    got(("sz", n, 0), SZ.at[n, 0])
                    got(("sz", n, 2), SZ.at[n, 1])

                @pl.when(ranks[n] == 2)
                def _():
                    got(("sz", n, 1), SZ.at[n, 1])

            def add(r):
                total = SZ[n, 0, r, :].astype(F32) + SZ[n, 1, r, :].astype(F32)
                mine = ST[x, r, :].astype(F32)
                other = SA[n, r, :].astype(F32)
                dst[x, r, :] = (total + jnp.where(firsts[n], 0.0, other)).astype(BF16)
                SB[r, :] = (total + jnp.where(firsts[n], mine, 0.0)).astype(BF16)

            state_rows(add)
            send_split(("sy", n), SB, dst.at[x], dev_x)

        def state_got(n, dst):
            got(("sy", n), dst.at[1 - x])

        def state_sent(n):
            sent(("sx", n))
            sent(("sy", n))
            pl.when(near_sends(n))(lambda: near(n).wait_send())
            if doubling:

                @pl.when(ranks[n] == 1)
                def _():
                    far(n, 1).wait_send()
                    far(n, 2).wait_send()

        def score_z(b, hp, e):
            qh, ql = split_low(q_rows(b, hp, e))
            kh, kl = split_low(k_rows(b, hp, e))
            return tn(jnp.concatenate([kh, kh, kl], axis=0), jnp.concatenate([qh, ql, qh], axis=0))

        def counts(buf, b):
            return buf[b, COUNTS:, :]

        def count_dot(t, f, at):
            r = nn(t[:HALF_HEADS], f[:LANES]) + nn(t[HALF_HEADS:, : FEATS - LANES], f[LANES:])
            spot = lax.broadcasted_iota(jnp.int32, r.shape, 0)
            return jnp.sum(jnp.where(spot == at, r, 0.0), axis=0, keepdims=True)

        def count_outer(t, row, at):
            spot = lax.broadcasted_iota(jnp.int32, (16, block), 0)
            first = jnp.where(spot == at, row, 0.0).astype(BF16)
            second = jnp.where(spot == HALF_HEADS + at, row, 0.0).astype(BF16)
            return jnp.concatenate([tn(t, first), tn(t[:, : FEATS - LANES], second)], axis=0)

        def att_step(i):
            b, hp = place(i)
            turned = PB[b, slot(hp), :].astype(F32).T.astype(BF16)
            tops = []
            for e in range(2):
                z = score_z(b, hp, e)
                st = (1.0 + z * FDIM**-0.5 + z * z * (0.5 / FDIM)).astype(BF16)
                fq = weighted(features(q_rows(b, hp, e)))
                num = nn(VT[b, head_slice(hp, e), :], st) + nn(turned[VDIM * e : VDIM * (e + 1)], fq)
                den = jnp.sum(st.astype(F32), axis=0, keepdims=True) + count_dot(counts(PB, b), fq, 2 * hp + e)
                NUM[b, head_slice(hp, e), :] = num
                DEN[i, e : e + 1, :] = den
                tops.append(num / den)
            ATT[b, :, v_slice(hp)] = jnp.concatenate(tops, axis=0).T.astype(BF16)

        def pairs(body, lo, n):
            def step(i, z):
                body(lo + i)
                return z

            lax.fori_loop(0, n, step, 0)

        def attention(lo, n):
            pairs(att_step, lo, n)

        def col(k):
            return pl.ds(pl.multiple_of(k * quarter, quarter), quarter)

        def wrow(i, k, at, w):
            return W[i][k, :, :, at : at + w].reshape(quarter, w)

        def out_proj(dst, b):
            def one(k):
                dst[:, col(k)] = nt(ATT[b], wrow(io, k, 0, VH))

            loop(4, one)

        def proj_send():
            out_proj(SND.at[0], o)
            send("x1", SND.at[0], RCV.at[0], partner)

        def norm_two(r):
            at = pl.multiple_of(r * step_rows, step_rows)
            rr = pl.ds(at, step_rows)
            x1 = X[c, rr, :].astype(F32) + (OWN[rr, :] + RCV[0, rr, :])
            X1[rr, :] = x1
            r2 = lax.rsqrt(jnp.mean(x1 * x1, axis=-1, keepdims=True) + EPS)
            NB[c, rr, :] = (x1 * r2 * GROW[1:2, :]).astype(BF16)

        def proj_own():
            out_proj(OWN, c)

        def second_norm():
            got("x1", RCV.at[0])
            loop(block // step_rows, norm_two)
            send("n2", NB.at[c], NB.at[c], partner)
            transpose_in(NB, N2T, c)

        def second_norm_in():
            got("n2", NB.at[o])
            transpose_in(NB, N2T, o)

        def ffn_in(j):
            base, w = parts[j]
            for at, tw in tiles_of(w):
                TG[:, 0:tw] = nn(NB[...].reshape(2 * block, width), weight(gi[f"g{j}"], at, tw))
                TU[:, 0:tw] = nn(NB[...].reshape(2 * block, width), weight(gi[f"u{j}"], at, tw))
                lo = base + at

                def one(r):
                    rr = pl.ds(pl.multiple_of(r * 64, 64), 64)
                    gate, up = TG[rr, 0:tw], TU[rr, 0:tw]
                    sg = 0.5 + 0.5 * jnp.tanh(0.5 * gate)
                    silu = gate * sg
                    HID[rr, lo : lo + tw] = (silu * up).astype(BF16)
                    CA[rr, lo : lo + tw] = (up * sg * (1.0 + gate * (1.0 - sg))).astype(BF16)
                    CB[rr, lo : lo + tw] = silu.astype(BF16)

                loop(2 * block // 64, one)
        def ffn_back(j):
            base, w = parts[j]
            i = gi[f"d{j}"]
            for at, tw in tiles_of(w):
                TG[:, 0:tw] = nn(DY[...].reshape(2 * block, width), weight(i, at, tw))
                lo = base + at

                def one(r):
                    rr = pl.ds(pl.multiple_of(r * 64, 64), 64)
                    dh = TG[rr, 0:tw]
                    CA[rr, lo : lo + tw] = (dh * CA[rr, lo : lo + tw].astype(F32)).astype(BF16)
                    CB[rr, lo : lo + tw] = (dh * CB[rr, lo : lo + tw].astype(F32)).astype(BF16)

                loop(2 * block // 64, one)

        def tokens_of(b):
            return pl.ds(pl.multiple_of(b * block, block), block)

        def dn2(dst, b):
            def one(k):
                acc = None
                for j, (base, w) in enumerate(parts):
                    for buf, i in ((CA, gi[f"g{j}"]), (CB, gi[f"u{j}"])):
                        t = nt(buf[tokens_of(b), base : base + w], wrow(i, k, 0, w))
                        acc = t if acc is None else acc + t
                dst[:, col(k)] = acc

            loop(4, one)

        def dn2_send():
            sent("x1")
            dn2(SND.at[0], o)
            send("dn2", SND.at[0], RCV.at[1], partner)

        def dn2_own():
            dn2(OWN, c)

        def norm_two_back(r):
            at = pl.multiple_of(r * step_rows, step_rows)
            rr = pl.ds(at, step_rows)
            d = OWN[rr, :] + RCV[1, rr, :]
            x1 = X1[rr, :]
            r2 = lax.rsqrt(jnp.mean(x1 * x1, axis=-1, keepdims=True) + EPS)
            t = d * (x1 * r2)
            GACC[8:16, :] += t[:8] + t[8:]
            a2 = d * GROW[1:2, :]
            dx = DY[c, rr, :].astype(F32) + (
                r2 * a2 - x1 * (r2 * r2 * r2) * jnp.mean(a2 * x1, axis=-1, keepdims=True)
            )
            din_ref[rr, :] = dx
            NB[c, rr, :] = dx.astype(BF16)

        def second_norm_back():
            got("dn2", RCV.at[1])
            sent("n2")
            loop(block // step_rows, norm_two_back)
            send("dx1", NB.at[c], NB.at[c], partner)
            transpose_in(NB, DYT, c)

        def datt():
            got("dx1", NB.at[o])
            transpose_in(NB, DYT, o)
            for at, tw in tiles_of(VH):
                t = nn(NB[...].reshape(2 * block, width), weight(io, at, tw))
                for b in range(2):
                    DATT[b, at : at + tw, :] = t[block * b : block * (b + 1)].T

        def back_state_step(i):
            b, hp = place(i)
            fs, ws = [], []
            for e in range(2):
                hs = head_slice(hp, e)
                datt, num, den = DATT[b, hs, :], NUM[b, hs, :], DEN[i, e : e + 1, :]
                dd = (-jnp.sum(datt * num, axis=0, keepdims=True) / (den * den)).astype(BF16)
                DNUM[b, hs, :] = (datt / den).astype(BF16)
                DDEN[i, e : e + 1, :] = dd.astype(F32)
                f = features(q_rows(b, hp, e))
                fs.append(f)
                ws.append(nt(jnp.broadcast_to(dd, (8, block)), f))
            put_state(i, fs[0], fs[1], DNUM[b, v_slice(hp), :], ws[0], ws[1])

        def back_states():
            WACC[...] = jnp.zeros_like(WACC)
            state_sent(0)
            loop(2 * PAIRS, back_state_step)
            ST[:, COUNTS:, :] = WACC[...].astype(BF16)

        zeros_head = jnp.zeros((VDIM, block), BF16)

        def masked(t, e):
            return jnp.concatenate([zeros_head, t] if e else [t, zeros_head], axis=0)

        def back_step(i):
            b, hp = place(i)
            for e in range(2):
                hs = head_slice(hp, e)
                q, kk = q_rows(b, hp, e), k_rows(b, hp, e)
                qh, ql = split_low(q)
                kh, kl = split_low(kk)
                z = tn(jnp.concatenate([kh, kh, kl], axis=0), jnp.concatenate([qh, ql, qh], axis=0))
                st = (1.0 + z * FDIM**-0.5 + z * z * (0.5 / FDIM)).astype(BF16)
                dnum, dden = DNUM[b, hs, :], DDEN[i, e : e + 1, :]
                ds = (tn(VT[b, hs, :], dnum) + dden).astype(BF16).astype(F32)
                dz = (ds * (FDIM**-0.5 + z * (1.0 / FDIM))).astype(BF16)
                t = nn(jnp.concatenate([kh, kl], axis=0), dz)
                dq = t[:FDIM] + t[FDIM:]
                t = nt(jnp.concatenate([qh, ql], axis=0), dz)
                dk = t[:FDIM] + t[FDIM:]
                DV[b, hs, :] = nt(dnum, st)
                df = nn(PB[b, slot(hp), :], masked(dnum, e)) + count_outer(counts(PB, b), dden, 2 * hp + e)
                DQK[b, pl.ds(pl.multiple_of(hp * 2 * FDIM + e * FDIM, FDIM), FDIM), :] = dq + features_back(q, df)
                DQK[b, pl.ds(pl.multiple_of(QH + hp * 2 * FDIM + e * FDIM, FDIM), FDIM), :] = dk

        def back_rows(lo, n):
            pairs(back_step, lo, n)

        def y_part(dst, b):
            def one(k):
                acc = None
                for j, (base, w) in enumerate(parts):
                    t = nt(HID[tokens_of(b), base : base + w], wrow(gi[f"d{j}"], k, 0, w))
                    acc = t if acc is None else acc + t
                dst[:, col(k)] = acc

            loop(4, one)

        def finish(r):
            rr = pl.ds(pl.multiple_of(r * step_rows, step_rows), step_rows)
            out_ref[rr, :] = (X1[rr, :] + (OWN[rr, :] + RCV[2, rr, :])).astype(BF16)

        def y_send():
            y_part(SND.at[1], o)
            send("y", SND.at[1], RCV.at[2], partner)

        def y_own():
            y_part(OWN, c)

        def y_end():
            got("y", RCV.at[2])
            loop(block // step_rows, finish)

        def key_step(i):
            b, hp = place(i)
            turned = PX[b, slot(hp), :].astype(F32).T.astype(BF16)
            for e in range(2):
                hs = head_slice(hp, e)
                kk = k_rows(b, hp, e)
                df = nn(PX[b, slot(hp), :], masked(VT[b, hs, :], e)) + count_outer(
                    counts(PX, b), jnp.ones((1, block), F32), 2 * hp + e
                )
                kr = pl.ds(pl.multiple_of(QH + hp * 2 * FDIM + e * FDIM, FDIM), FDIM)
                DQK[b, kr, :] += features_back(kk, df)
                DV[b, hs, :] += nn(turned[VDIM * e : VDIM * (e + 1)], weighted(features(kk)))

        def keys_back(lo, n):
            pairs(key_step, lo, n)

        def dqkv():
            for b in range(2):
                DQKV[b, :, 0 : 2 * QH] = DQK[b].T.astype(BF16)
                for at, tw in tiles_of(VH):
                    DQKV[b, :, 2 * QH + at : 2 * QH + at + tw] = DV[b, at : at + tw, :].T.astype(BF16)

        def dn1(dst, b):
            def one(k):
                dst[:, col(k)] = nt(DQKV[b, :, : 2 * QH], wrow(iq, k, 0, 2 * QH)) + nt(
                    DQKV[b, :, 2 * QH :], wrow(iv, k, 0, VH)
                )

            loop(4, one)

        def dn1_send():
            sent("dn2")
            dn1(SND.at[0], o)
            send("dn1", SND.at[0], RCV.at[0], partner)

        def dn1_own():
            dn1(OWN, c)

        def norm_one_back(r):
            rr = pl.ds(pl.multiple_of(r * step_rows, step_rows), step_rows)
            d = OWN[rr, :] + RCV[0, rr, :]
            xs = X[c, rr, :].astype(F32)
            r1 = lax.rsqrt(jnp.mean(xs * xs, axis=-1, keepdims=True) + EPS)
            t = d * (xs * r1)
            GACC[0:8, :] += t[:8] + t[8:]
            a1 = d * GROW[0:1, :]
            din_ref[rr, :] += r1 * a1 - xs * (r1 * r1 * r1) * jnp.mean(a1 * xs, axis=-1, keepdims=True)

        def first_norm_back():
            got("dn1", RCV.at[0])
            loop(block // step_rows, norm_one_back)
            sum_a = jnp.sum(GACC[0:8, :], axis=0, keepdims=True)
            gf = jnp.sum(GACC[8:16, :], axis=0, keepdims=True)
            last = ri["gain"]
            for k in range(4):
                row = lax.broadcasted_iota(jnp.int32, (LANES, quarter), 0)
                sl = slice(quarter * k, quarter * (k + 1))
                mat = jnp.where(row == 0, sum_a[:, sl], 0.0) + jnp.where(row == 1, gf[:, sl], 0.0)
                G[last][k] = mat.T.astype(BF16).reshape(4, rows2, LANES)
        def part_of(buf, j):
            base, w = parts[j]
            return lambda: buf[:, base : base + w]

        def grad(name):
            kind = name.rstrip("0123456789")
            if kind == "d":
                put_grad(ri[name], DYT, part_of(HID, int(name[1:])))
            elif kind == "g":
                put_grad(ri[name], N2T, part_of(CA, int(name[1:])))
            elif kind == "u":
                put_grad(ri[name], N2T, part_of(CB, int(name[1:])))
            elif name == "out":
                put_grad(ri[name], DYT, lambda: ATT[...].reshape(2 * block, VH))
            elif name == "qk":
                put_grad(ri[name], N1T, lambda: DQKV[:, :, 0 : 2 * QH].reshape(2 * block, 2 * QH))
            elif name == "v":
                put_grad(ri[name], N1T, lambda: DQKV[:, :, 2 * QH :].reshape(2 * block, VH))

        def adv(st, name):
            go_to(st, ri[name])

        def greeted():
            pl.semaphore_wait(barrier, len(greet))
            if members > 1:

                @pl.when(hi < n_hi - 1)
                def _():
                    pl.semaphore_wait(barrier, 1)

                @pl.when(hi > 0)
                def _():
                    pl.semaphore_wait(barrier, 1)

        cx = local(tok, X.at[c])
        cy = local(cot, DY.at[c])
        for i in range(len(gather)):
            e0(i)
        cx.wait()
        cy.wait()
        greeted()

        for i in range(len(gather)):
            e0_send(i)
        send("x", X.at[c], X.at[c], partner)
        send("dy", DY.at[c], DY.at[c], partner)
        ga(1, 0)
        ga(1, 1)
        ga(2, 0)
        ga(1, 2)
        ga(2, 1)
        ga(3, 0)
        transpose_in(DY, DYT, c)
        got("x", X.at[o])
        got("dy", DY.at[o])
        transpose_in(DY, DYT, o)
        ga(1, 3)
        ga(1, 4)
        ga(2, 2)
        ga(3, 1)
        ga(4, 0)
        z1()
        gains()
        first_norm()
        ga(1, 5)
        ga(2, 3)
        ga(3, 2)
        ga(2, 4)
        ga(4, 1)
        ga(4, 2)
        qkv()
        states()
        state_x(0)
        ga(1, 6)
        ga(1, 7)
        ga(1, 8)
        ga(1, 9)
        ga(1, 10)
        ga(1, 11)
        ga(2, 5)
        ga(2, 6)
        ga(3, 3)
        state_z(0)
        ga(2, 7)
        ga(3, 4)
        z2()
        state_far(0)
        ga(2, 8)
        ga(3, 5)
        state_end(0, PB)
        ga(2, 9)
        ga(3, 6)
        state_got(0, PB)
        ga(3, 7)
        z3()
        attention(0, 4)
        attention(4, 4)
        ga(2, 10)
        ga(3, 8)
        ga(4, 3)
        proj_send()
        proj_own()
        second_norm()
        second_norm_in()
        ga(2, 11)
        ga(3, 9)
        ga(4, 4)
        ga(4, 5)
        ffn_in(0)
        grad("d0")
        zf1()
        ga(3, 10)
        ga(4, 6)
        ga(4, 7)
        ffn_in(1)
        grad("d1")
        go_to(1, 1)
        ga(3, 11)
        ga(4, 8)
        ga(4, 9)
        ffn_in(2)
        grad("d2")
        go_to(1, 2)
        z4()
        ffn_back(0)
        go_to(2, 1)
        grad("g0")
        go_to(1, 3)
        ga(4, 10)
        ffn_back(1)
        go_to(2, 2)
        go_to(3, 1)
        grad("u0")
        go_to(1, 4)
        ga(4, 11)
        ffn_back(2)
        dn2_send()
        go_to(2, 3)
        dn2_own()
        go_to(3, 2)
        grad("g1")
        go_to(1, 5)
        second_norm_back()
        datt()
        go_to(2, 4)
        back_states()
        state_x(1)
        go_to(3, 3)
        go_to(4, 1)
        grad("u1")
        go_to(4, 2)
        go_to(1, 6)
        state_z(1)
        go_to(2, 5)
        go_to(3, 4)
        zf2()
        go_to(4, 3)
        back_rows(0, 4)
        grad("g2")
        go_to(1, 7)
        state_far(1)
        go_to(2, 6)
        go_to(3, 5)
        go_to(4, 4)
        back_rows(4, 4)
        grad("u2")
        go_to(1, 8)
        zf3()
        state_end(1, PX)
        go_to(2, 7)
        go_to(3, 6)
        go_to(4, 5)
        grad("out")
        go_to(1, 9)
        y_send()
        y_own()
        zf4()
        state_got(1, PX)
        keys_back(0, 4)
        keys_back(4, 4)
        dqkv()
        grad("qk")
        go_to(2, 8)
        go_to(3, 7)
        go_to(4, 6)
        go_to(1, 10)
        grad("v")
        go_to(1, 11)
        dn1_send()
        y_end()
        dn1_own()
        go_to(2, 9)
        go_to(3, 8)
        go_to(4, 7)
        first_norm_back()
        go_to(2, 10)
        go_to(3, 9)
        go_to(4, 8)
        go_to(1, 12)
        go_to(2, 11)
        go_to(3, 10)
        go_to(4, 9)
        go_to(2, 12)
        go_to(3, 11)
        go_to(4, 10)
        go_to(3, 12)
        go_to(4, 11)
        go_to(4, 12)

        n = len(reduce)
        for i in range(n):
            got(("f4", i), go.at[o, :, offsets[i] : offsets[i] + reduce[i][1]])
        for d in local_pending:
            d.wait()
        state_sent(1)
        for d in pending.values():
            d.wait_send()

    return kernel


def call_kernel(tok, cot, shards, seq_size, ff, ff_half):
    block, width = tok.shape
    gather, reduce = plan(ff_half)
    rows = width // 32
    vmem = pltpu.VMEM
    any_spec = pl.BlockSpec(memory_space=pl.ANY)
    vmem_spec = pl.BlockSpec(memory_space=vmem)
    total_width = sum(w for _, w in reduce)
    pack_width = sum(w for _, w in gather)
    state = vmem((2, STATE, LANES), BF16)
    scratch = [vmem((4, 4, 2 * (16 if name == "gain" else rows), w), BF16) for name, w in gather]
    scratch += [vmem((4, 4, 2 * rows, w), BF16) for _, w in reduce]
    scratch += [
        vmem((rows, pack_width), BF16),
        vmem((RING, 2, 4, 2 * rows, PIECE), BF16),
        vmem((RING, 4, 2 * rows, PIECE), BF16),
        vmem((RING, 3, 2 * rows, PIECE), BF16),
        vmem((3, 4, 2 * rows, PIECE), BF16),
        vmem((3, 2 * rows, PIECE), BF16),
        vmem((2, rows, total_width), F32),
        vmem((2, block, width), BF16),
        vmem((2, block, width), BF16),
        vmem((2, block, width), BF16),
        vmem((width, 2 * block), BF16),
        vmem((width, 2 * block), BF16),
        vmem((width, 2 * block), BF16),
        vmem((2 * block, ff_half), BF16),
        vmem((2 * block, ff_half), BF16),
        vmem((2 * block, ff_half), BF16),
        vmem((block, width), F32),
        vmem((2, block, width), F32),
        vmem((3, block, width), F32),
        vmem((block, width), F32),
        vmem((2, VH, block), F32),
        vmem((2, VH, block), F32),
        vmem((2, 2 * QH, block), F32),
        vmem((2, VH, block), BF16),
        vmem((2, block, VH), BF16),
        vmem((2 * PAIRS, 8, block), F32),
        vmem((2, VH, block), BF16),
        vmem((2 * PAIRS, 8, block), F32),
        vmem((2, 2 * QH, block), F32),
        vmem((2, VH, block), F32),
        vmem((2, block, 2 * QH + VH), BF16),
        state,
        vmem((2, STATE, LANES), BF16),
        vmem((2, 2, STATE, LANES), BF16),
        vmem((STATE, LANES), BF16),
        vmem((STATE, LANES), BF16),
        vmem((STATE, LANES), BF16),
        state,
        state,
        vmem((2, 16, LANES), F32),
        vmem((2 * block, 256), F32),
        vmem((2 * block, 256), F32),
        vmem((8, width), F32),
        vmem((16, width), F32),
        pltpu.SemaphoreType.DMA((n_messages(gather, reduce),)),
        pltpu.SemaphoreType.DMA((n_messages(gather, reduce),)),
        pltpu.SemaphoreType.DMA((2 + len(reduce),)),
    ]
    out_shape = [
        jax.ShapeDtypeStruct((block, width), BF16),
        jax.ShapeDtypeStruct((block, width), F32),
        jax.ShapeDtypeStruct((2, rows, total_width), F32),
    ]
    return pl.pallas_call(
        make_kernel(seq_size, block, width, ff, ff_half),
        out_shape=out_shape,
        in_specs=[any_spec] * 2 + [vmem_spec] * len(shards),
        out_specs=[vmem_spec] * 2 + [any_spec],
        scratch_shapes=scratch,
        compiler_params=pltpu.CompilerParams(
            collective_id=0, has_side_effects=True, vmem_limit_bytes=62 * 2**20
        ),
    )(tok, cot, *shards)


def n_messages(gather, reduce):
    return 7 * len(gather) + 6 * RING + len(reduce) + 24


def call_finish(output, input_grad, grads, ff, ff_half):
    block, width = output.shape
    rows = grads.shape[1]
    _, reduce = plan(ff_half)
    at = dict(zip([name for name, _ in reduce], offsets_of(reduce)))
    parts = pieces_of(ff_half)
    vmem_spec = pl.BlockSpec(memory_space=pltpu.VMEM)
    hbm_spec = pl.BlockSpec(memory_space=pltpu.HBM)

    def kernel(o_in, i_in, g_hbm, o_out, i_out, ag, qg, kg, vg, og, fg, gg, ug, dg, g_in, o_held, i_held, sems):
        c2 = pltpu.make_async_copy(g_hbm, g_in, sems.at[2])
        c2.start()
        c0 = pltpu.make_async_copy(i_in, i_held, sems.at[0])
        c1 = pltpu.make_async_copy(o_in, o_held, sems.at[1])
        c0.start()
        c1.start()
        c0.wait()
        c3 = pltpu.make_async_copy(i_held, i_out, sems.at[3])
        c3.start()
        c1.wait()
        c4 = pltpu.make_async_copy(o_held, o_out, sems.at[4])
        c4.start()
        c2.wait()
        gain = (g_in[0, :, at["gain"] : at["gain"] + LANES] + g_in[1, :, at["gain"] : at["gain"] + LANES]).T
        ag[...] = gain[0:1, :rows]
        fg[...] = gain[1:2, :rows]
        for h in range(2):
            qg[:, QH * h : QH * (h + 1)] = g_in[h, :, at["qk"] : at["qk"] + QH]
            kg[:, QH * h : QH * (h + 1)] = g_in[h, :, at["qk"] + QH : at["qk"] + 2 * QH]
            vg[:, VH * h : VH * (h + 1)] = g_in[h, :, at["v"] : at["v"] + VH]
            og[:, VH * h : VH * (h + 1)] = g_in[h, :, at["out"] : at["out"] + VH]
            for j, (base, w) in enumerate(parts):
                lo = ff_half * h + base
                have = min(w, ff - lo)
                for ref, letter in ((gg, "g"), (ug, "u"), (dg, "d")):
                    a = at[f"{letter}{j}"]
                    ref[:, lo : lo + have] = g_in[h, :, a : a + have]
        c3.wait()
        c4.wait()

    shapes = [(1, rows), (rows, 2 * QH), (rows, 2 * QH), (rows, 2 * VH), (rows, 2 * VH), (1, rows)] + [(rows, ff)] * 3
    return pl.pallas_call(
        kernel,
        out_shape=[jax.ShapeDtypeStruct(output.shape, BF16), jax.ShapeDtypeStruct(input_grad.shape, F32)]
        + [jax.ShapeDtypeStruct(n, F32) for n in shapes],
        in_specs=[hbm_spec] * 3,
        out_specs=[hbm_spec] * 2 + [vmem_spec] * len(shapes),
        scratch_shapes=[
            pltpu.VMEM(grads.shape, F32),
            pltpu.VMEM(output.shape, BF16),
            pltpu.VMEM(input_grad.shape, F32),
            pltpu.SemaphoreType.DMA((5,)),
        ],
        compiler_params=pltpu.CompilerParams(vmem_limit_bytes=60 * 2**20),
    )(output, input_grad, grads)


def body(
    tokens, attn_gain, query_weight, key_weight, value_weight, out_weight, ffn_gain, gate_weight, up_weight, down_weight, cotangent
):
    seq_size = lax.axis_size("seq")
    members = seq_size // 8
    _, block, width = tokens.shape
    ff = gate_weight.shape[1]
    ff_half = LANES * ((ff + 2 * LANES - 1) // (2 * LANES))
    few = attn_gain.shape[0]
    groups = [[(g * members + m) * 2 + x for m in range(members)] for g in range(4) for x in range(2)]

    shards = [attn_gain, query_weight, key_weight, value_weight, out_weight.T, ffn_gain, gate_weight, up_weight, down_weight.T]
    if members > 1:
        shards = [
            lax.all_gather(a, "seq", axis_index_groups=groups, axis=0, tiled=True) for a in shards
        ]
    shards = [a.reshape(1, -1) if a.ndim == 1 else a for a in shards]

    def turn(t):
        if members == 1:
            return t
        return t.reshape(block, 4, members, 2, 4, few).transpose(0, 1, 3, 4, 2, 5).reshape(block, width)

    def turn_back(t):
        if members == 1:
            return t
        return t.reshape(block, 4, 2, 4, members, few).transpose(0, 1, 4, 2, 3, 5).reshape(block, width)

    output, input_grad, grads = call_kernel(turn(tokens[0]), turn(cotangent[0]), shards, seq_size, ff, ff_half)
    if members == 1:
        o, i, ag, qg, kg, vg, og, fg, gg, ug, dg = call_finish(output, input_grad, grads, ff, ff_half)
        return o[None], i[None], ag[0], qg, kg, vg, og.T, fg[0], gg, ug, dg.T
    grads = lax.psum_scatter(grads, "seq", scatter_dimension=1, axis_index_groups=groups, tiled=True)
    _, reduce = plan(ff_half)
    by = {name: grads[:, :, a : a + w] for (name, w), a in zip(reduce, offsets_of(reduce))}
    n_parts = len(pieces_of(ff_half))

    def joined(a):
        return jnp.concatenate([a[0], a[1]], axis=1)

    def ff_joined(letter):
        return joined(jnp.concatenate([by[f"{letter}{j}"] for j in range(n_parts)], axis=2))[:, :ff]

    gain = by["gain"][0] + by["gain"][1]
    return (
        turn_back(output)[None],
        turn_back(input_grad)[None],
        gain[:, 0],
        joined(by["qk"][:, :, :QH]),
        joined(by["qk"][:, :, QH:]),
        joined(by["v"]),
        joined(by["out"]).T,
        gain[:, 1],
        ff_joined("g"),
        ff_joined("u"),
        ff_joined("d").T,
    )


def solution(mesh):
    both = ("seq", "dp")
    row, column, whole = P(both, None), P(None, both), P("dp", "seq", None)
    return jax.shard_map(
        body,
        mesh=mesh,
        in_specs=(whole, P(both), row, row, row, column, P(both), row, row, column, whole),
        out_specs=(whole, whole, P(both), row, row, row, column, P(both), row, row, column),
        check_vma=False,
    )
```

```python
import jax
import jax.numpy as jnp
from jax import lax
from jax.experimental import pallas as pl
from jax.experimental.pallas import tpu as pltpu
from jax.sharding import PartitionSpec as P

HEADS = 16
FDIM = 16
VDIM = 64
EPS = 1e-05
LIN = FDIM**-0.25
QUAD = (2.0 * FDIM) ** -0.5
SHIFTS = FDIM // 2
HALF = FDIM // 2
FEATS = FDIM * (SHIFTS + 2)
HALF_HEADS = HEADS // 2
QH = HALF_HEADS * FDIM
VH = HALF_HEADS * VDIM
PAIRS = HALF_HEADS // 2
COUNTS = PAIRS * FEATS
STATE = COUNTS + 16
STATE_STEPS = STATE // 16
SPLIT = 96
LANES = 128
ALIKE = (("g0", "u2"), ())
PIECE = 512
RING = 6
MESH = pl.DeviceIdType.MESH
F32 = jnp.float32
BF16 = jnp.bfloat16


def pieces_of(width):
    out, at = [], 0
    while at < width:
        out.append((at, min(PIECE, width - at)))
        at += PIECE
    return out


def tiles_of(width):
    out, at = [], 0
    while at < width:
        out.append((at, min(256, width - at)))
        at += 256
    return out


def nn(a, b):
    return jnp.dot(a, b, preferred_element_type=F32)


def nt(a, b):
    return lax.dot_general(a, b, (((1,), (1,)), ((), ())), preferred_element_type=F32)


def tn(a, b):
    return lax.dot_general(a, b, (((0,), (0,)), ((), ())), preferred_element_type=F32)


def ahead(t, d):
    return t if d == 0 else pltpu.roll(t, FDIM - d, 0)


def behind(t, d):
    return t if d == 0 else pltpu.roll(t, d, 0)


def features(u):
    rows = [u * ahead(u, d) * QUAD for d in range(SHIFTS)]
    spot = lax.broadcasted_iota(jnp.int32, u.shape, 0)
    last = jnp.where(spot < HALF, u * ahead(u, HALF) * QUAD, jnp.where(spot == HALF, 1.0, 0.0))
    return jnp.concatenate(rows + [last, u * LIN], axis=0).astype(BF16)


def weighted(f):
    at = FDIM * SHIFTS
    scale = jnp.where(lax.broadcasted_iota(jnp.int32, (FDIM, f.shape[1]), 0) < HALF, 2.0, 1.0).astype(BF16)
    return jnp.concatenate([f[:FDIM], f[FDIM:at] * 2, f[at : at + FDIM] * scale, f[at + FDIM :]], axis=0)


def features_back(u, df):
    at = FDIM * SHIFTS
    total = df[at + FDIM :] * LIN
    for d in range(SHIFTS + 1):
        t = df[FDIM * d : FDIM * (d + 1)] * (QUAD * (2.0 if d else 1.0))
        if d == HALF:
            t = jnp.where(lax.broadcasted_iota(jnp.int32, t.shape, 0) < HALF, t, 0.0)
        total = total + t * ahead(u, d) + behind(t * u, d)
    return total


def split_low(u):
    high = u.astype(BF16)
    return high, (u - high.astype(F32)).astype(BF16)


def plan(ff_half):
    parts = pieces_of(ff_half)
    gather = [("gain", LANES), ("qk", 2 * QH), ("v", VH), ("out", VH)]
    for j, (_, w) in enumerate(parts):
        gather += [(f"g{j}", w), (f"u{j}", w)]
    gather += [(f"d{j}", w) for j, (_, w) in enumerate(parts)][1:]
    gather += [("d0", parts[0][1])]
    reduce = [(f"d{j}", w) for j, (_, w) in enumerate(parts)]
    for j, (_, w) in enumerate(parts):
        reduce += [(f"g{j}", w), (f"u{j}", w)]
    reduce += [("out", VH), ("qk", 2 * QH), ("v", VH), ("gain", LANES)]
    return gather, reduce


def offsets_of(chunks):
    out, at = [], 0
    for _, w in chunks:
        out.append(at)
        at += w
    return out


def make_kernel(seq_size, block, width, ff, ff_half):
    gather, reduce = plan(ff_half)
    parts = pieces_of(ff_half)
    n_parts = len(parts)
    gi = {name: i for i, (name, _) in enumerate(gather)}
    ri = {name: i for i, (name, _) in enumerate(reduce)}
    members = seq_size // 8
    n_hi = seq_size // 2
    rows = width // 32
    rows2 = 2 * rows
    quarter = width // 4
    offsets = offsets_of(reduce)
    pack_at = offsets_of(gather)

    def kernel(*refs):
        it = iter(refs)
        take = lambda n: [next(it) for _ in range(n)]
        tok, cot = take(2)
        attn_in, q_in, k_in, v_in, o_in, ffn_in_gain, g_in, u_in, d_in = take(9)
        out_ref, din_ref, go = take(3)
        W = take(len(gather))
        G = take(len(reduce))
        (PK, R1, R2, R3, RZ, RY, FS, X, DY, NB, N1T, N2T, DYT, HID, CA, CB, X1, SND, RCV, OWN) = take(20)
        (NUM, DATT, QK, VT, ATT, DEN, DNUM, DDEN, DQK, DV, DQKV) = take(11)
        (ST, SA, SZ, TZ, TY, SB, PB, PX, WACC, TG, TU, GROW, GACC) = take(13)
        ss, rs, ls = take(3)

        s, dp = lax.axis_index("seq"), lax.axis_index("dp")
        hi, x = s // 2, lax.rem(s, 2)
        y, c = dp // 2, lax.rem(dp, 2)
        g, m = hi // members, lax.rem(hi, members)
        o = 1 - c
        p, pab = 2 * x + y, 2 * (1 - x) + (1 - y)

        def dev(hi_, x_, y_, c_):
            return (hi_ * 2 + x_, y_ * 2 + c_)

        partner = dev(hi, x, y, o)
        dev_x, dev_y = dev(hi, 1 - x, y, c), dev(hi, x, 1 - y, c)

        def roles(flip):
            nx, ny = x + flip * (1 - 2 * x), y + (1 - flip) * (1 - 2 * y)
            return dev(hi, nx, ny, c), 2 * nx + ny

        mixed = roles(o) + roles(c)
        alike = roles(1) + roles(0)

        def way(name, phase):
            return alike if name in ALIKE[phase] else mixed

        ups = [lax.rem(g + j, 4) for j in range(4)]
        downs = [lax.rem(g + 4 - j, 4) for j in range(4)]
        dev_up = [dev(u * members + m, x, y, c) for u in ups]
        right = dev(jnp.minimum(hi + 1, n_hi - 1), x, y, c)
        left = dev(jnp.maximum(hi - 1, 0), x, y, c)

        n_local = [0]
        local_pending = []

        def local(src, dst):
            d = pltpu.make_async_copy(src, dst, ls.at[n_local[0]])
            n_local[0] += 1
            d.start()
            return d

        barrier = pltpu.get_barrier_semaphore()
        greet = [partner, dev_x, dev_y] + dev_up[1:]
        for d in greet:
            pl.semaphore_signal(barrier, inc=1, device_id=d, device_id_type=MESH)
        if members > 1:

            @pl.when(hi < n_hi - 1)
            def _():
                pl.semaphore_signal(barrier, inc=1, device_id=right, device_id_type=MESH)

            @pl.when(hi > 0)
            def _():
                pl.semaphore_signal(barrier, inc=1, device_id=left, device_id_type=MESH)

        numbers = {}
        pending = {}

        def number(key):
            return numbers.setdefault(again(key), len(numbers))

        def again(key):
            if key[0] == "f1":
                return (("e2b", key[1]), ("e3", key[1]))[key[2]]
            return {"f2": ("e2a",), "f3": ("e1",), "f4": ("e0",)}.get(key[0], key[:1]) + key[1:]

        def remote(key, src, dst, to):
            i = number(key)
            return pltpu.make_async_remote_copy(
                src_ref=src, dst_ref=dst, send_sem=ss.at[i], recv_sem=rs.at[i], device_id=to, device_id_type=MESH
            )

        def send(key, src, dst, to):
            key = again(key)
            if key in pending:
                sent(key)
            d = remote(key, src, dst, to)
            d.start()
            pending[key] = d

        def sent(key):
            pending.pop(key).wait_send()

        def got(key, ref):
            remote(key, ref, ref, partner).wait_recv()

        def pack(i, lower, upper):
            w = gather[i][1]
            r = 16 if i == 0 else rows
            mine = W[i].at[g, p, pl.ds(pl.multiple_of(r * c, r), r)]
            stage = PK.at[0:r, pack_at[i] : pack_at[i] + w]

            @pl.when(c == 0)
            def _():
                mine[...] = lower()
                stage[...] = upper()

            @pl.when(c == 1)
            def _():
                mine[...] = upper()
                stage[...] = lower()

        def e0_send(i):
            w = gather[i][1]
            r = 16 if i == 0 else rows
            mine = W[i].at[g, p, pl.ds(pl.multiple_of(r * c, r), r)]
            send(("e0", i), PK.at[0:r, pack_at[i] : pack_at[i] + w], mine, partner)

        def ff_piece(ref, at, w):
            have = min(w, ff - at)
            if have == w:
                return ref[:, at : at + w]
            return jnp.concatenate([ref[:, at : at + have], jnp.zeros((ref.shape[0], w - have), BF16)], axis=1)

        def gain_block():
            out = jnp.zeros((16, LANES), F32)
            lanes = lax.broadcasted_iota(jnp.int32, (16, LANES), 1) // rows
            row = lax.broadcasted_iota(jnp.int32, (16, LANES), 0)
            for n, ref in enumerate((attn_in, ffn_in_gain)):
                t = jnp.concatenate([ref[...].astype(F32)] * (LANES // rows), axis=1)
                out = jnp.where((lanes == dp) & (row == n), t, out)
            return out.astype(BF16)

        def e0(i):
            name, w = gather[i]
            if name == "gain":
                pack(i, gain_block, gain_block)
            elif name == "qk":
                pack(
                    i,
                    lambda: jnp.concatenate([q_in[:, :QH], k_in[:, :QH]], axis=1),
                    lambda: jnp.concatenate([q_in[:, QH:], k_in[:, QH:]], axis=1),
                )
            elif name == "v":
                pack(i, lambda: v_in[:, :VH], lambda: v_in[:, VH:])
            elif name == "out":
                pack(i, lambda: o_in[:, :VH], lambda: o_in[:, VH:])
            else:
                at = parts[int(name[1:])][0]
                ref = {"g": g_in, "u": u_in, "d": d_in}[name[0]]
                pack(i, lambda: ff_piece(ref, at, w), lambda: ff_piece(ref, ff_half + at, w))

        def e1(i):
            r = 16 if i == 0 else rows
            got(("e0", i), W[i].at[g, p, pl.ds(pl.multiple_of(r * o, r), r)])
            for j in (1, 2, 3):
                send(("e1", i, j), W[i].at[g, p], W[i].at[g, p], dev_up[j])

        def e2(i):
            dev_a, pa, dev_b, pb = way(gather[i][0], 0)
            for j in (1, 2, 3):
                got(("e1", i, j), W[i].at[downs[j], p])
            send(("e2b", i), W[i].at[:, p], W[i].at[:, p], dev_b)
            send(("e2a", i), W[i].at[:, p], W[i].at[:, p], dev_a)

        def e3(i):
            dev_a, pa, dev_b, pb = way(gather[i][0], 0)
            got(("e2a", i), W[i].at[:, pa])
            send(("e3", i), W[i].at[:, pa], W[i].at[:, pa], dev_b)

        def e4(i):
            dev_a, pa, dev_b, pb = way(gather[i][0], 0)
            got(("e2b", i), W[i].at[:, pb])
            got(("e3", i), W[i].at[:, pab])

        iz = len(gather) - 1

        def z1():
            dev_a, pa, dev_b, pb = way(gather[iz][0], 0)
            r = rows
            got(("e0", iz), W[iz].at[g, p, pl.ds(pl.multiple_of(r * o, r), r)])
            send(("e2b", iz), W[iz].at[g, p], W[iz].at[g, p], dev_b)
            send(("e2a", iz), W[iz].at[g, p], W[iz].at[g, p], dev_a)

        def z2():
            dev_a, pa, dev_b, pb = way(gather[iz][0], 0)
            got(("e2a", iz), W[iz].at[g, pa])
            send(("e3", iz), W[iz].at[g, pa], W[iz].at[g, pa], dev_b)

        def z3():
            dev_a, pa, dev_b, pb = way(gather[iz][0], 0)
            got(("e2b", iz), W[iz].at[g, pb])
            got(("e3", iz), W[iz].at[g, pab])
            for j in (1, 2, 3):
                send(("e1", iz, j), W[iz].at[g], W[iz].at[g], dev_up[j])

        def z4():
            for j in (1, 2, 3):
                got(("e1", iz, j), W[iz].at[downs[j]])

        gathered = {1: -1, 2: -1, 3: -1, 4: -1}

        def ga(step, last):
            while gathered[step] < min(last, iz - 1):
                gathered[step] += 1
                (e1, e2, e3, e4)[step - 1](gathered[step])

        def gstep(k, l1=1, l2=1):
            ga(1, k + l1 + l2)
            ga(2, k + l2)
            ga(3, k)
            ga(4, k - 1)

        done = {1: 0, 2: 0, 3: 0, 4: 0}

        def zf1():
            w = reduce[0][1]
            for j in (1, 2, 3):
                send(("z1", j), G[0].at[ups[j]], RZ.at[j - 1, :, :, 0:w], dev_up[j])

        def zf2():
            dev_a, pa, dev_b, pb = way(reduce[0][0], 1)
            w = reduce[0][1]
            for j in (1, 2, 3):
                got(("z1", j), RZ.at[j - 1, :, :, 0:w])

            def one(k):
                total = G[0][g, k].astype(F32)
                for j in range(3):
                    total = total + RZ[j, k, :, 0:w].astype(F32)
                G[0][g, k] = total.astype(BF16)

            loop(4, one)
            for n, q in ((0, pab), (1, pb)):
                send(("z2", n), G[0].at[g, q], RY.at[n, :, 0:w], dev_b)

        def zf3():
            dev_a, pa, dev_b, pb = way(reduce[0][0], 1)
            w = reduce[0][1]
            got(("z2", 0), RY.at[0, :, 0:w])
            G[0][g, pa] = G[0][g, pa] + RY[0, :, 0:w]
            send(("z3", 0), G[0].at[g, pa], RY.at[2, :, 0:w], dev_a)
            got(("z2", 1), RY.at[1, :, 0:w])
            G[0][g, p] = G[0][g, p] + RY[1, :, 0:w]

        def zf4():
            w = reduce[0][1]
            got(("z3", 0), RY.at[2, :, 0:w])
            finish_chunk(0, G[0][g, p].astype(F32) + RY[2, :, 0:w].astype(F32))

        def f1(i):
            dev_a, pa, dev_b, pb = way(reduce[i][0], 1)
            w = reduce[i][1]
            k = i % RING
            for n, col in ((0, pab), (1, pb)):
                send(("f1", k, n), G[i].at[:, col], R1.at[k, n, :, :, 0:w], dev_b)

        def f2(i):
            dev_a, pa, dev_b, pb = way(reduce[i][0], 1)
            w = reduce[i][1]
            k = i % RING
            got(("f1", k, 0), R1.at[k, 0, :, :, 0:w])
            G[i][:, pa] = G[i][:, pa] + R1[k, 0, :, :, 0:w]
            send(("f2", k), G[i].at[:, pa], R2.at[k, :, :, 0:w], dev_a)
            got(("f1", k, 1), R1.at[k, 1, :, :, 0:w])
            G[i][:, p] = G[i][:, p] + R1[k, 1, :, :, 0:w]

        def f3(i):
            dev_a, pa, dev_b, pb = way(reduce[i][0], 1)
            w = reduce[i][1]
            k = i % RING
            got(("f2", k), R2.at[k, :, :, 0:w])
            G[i][:, p] = G[i][:, p] + R2[k, :, :, 0:w]
            for j in (1, 2, 3):
                send(("f3", k, j), G[i].at[ups[j], p], R3.at[k, j - 1, :, 0:w], dev_up[j])

        def f4(i):
            w = reduce[i][1]
            k = i % RING
            total = G[i][g, p].astype(F32)
            for j in (1, 2, 3):
                got(("f3", k, j), R3.at[k, j - 1, :, 0:w])
                total = total + R3[k, j - 1, :, 0:w].astype(F32)
            finish_chunk(i, total)

        def finish_chunk(i, total):
            w, at = reduce[i][1], offsets[i]
            FS[:, :, at : at + w] = total.reshape(2, rows, w)
            local_pending.append(local(FS.at[c, :, at : at + w], go.at[c, :, at : at + w]))
            send(("f4", i), FS.at[o, :, at : at + w], go.at[c, :, at : at + w], partner)

        stages = {1: f1, 2: f2, 3: f3, 4: f4}

        def go_to(stage, last):
            while done[stage] < last:
                i = done[stage] + 1
                if stage < 4 and i >= RING // 2:
                    go_to(stage + 1, i - RING // 2)
                if stage > 1:
                    go_to(stage - 1, i)
                stages[stage](i)
                done[stage] = i

        def loop(n, body):
            def step(i, carry):
                body(i)
                return carry

            lax.fori_loop(0, n, step, 0)

        def put_grad(i, lhs_t, rhs):
            w = reduce[i][1]

            def one(k):
                a = lhs_t[pl.ds(pl.multiple_of(k * quarter, quarter), quarter), :]
                G[i][k] = nn(a, rhs()).astype(BF16).reshape(4, rows2, w)

            loop(4, one)

        def weight(i, at, w):
            return W[i][:, :, :, at : at + w].reshape(width, w)

        def transpose_in(src, dst, b):
            def one(k):
                at = pl.multiple_of(k * quarter, quarter)
                dst[pl.ds(at, quarter), pl.ds(pl.multiple_of(b * block, block), block)] = (
                    src[b, :, pl.ds(at, quarter)].T
                )

            loop(4, one)

        step_rows = 16
        iq, iv, io = gi["qk"], gi["v"], gi["out"]

        def gains():
            for k in range(8):
                kg, kx = k // 2, k % 2
                acc = None
                for ky in range(2):
                    for kc in range(2):
                        t = W[0][kg, 2 * kx + ky, 16 * kc : 16 * kc + 16, :].astype(F32)
                        acc = t if acc is None else acc + t
                GROW[:, LANES * k : LANES * (k + 1)] = acc[:8]
            GACC[...] = jnp.zeros_like(GACC)

            GACC[...] = jnp.zeros_like(GACC)

        def norm_one(r):
            at = pl.multiple_of(r * step_rows, step_rows)
            for b in range(2):
                xs = X[b, pl.ds(at, step_rows), :].astype(F32)
                r1 = lax.rsqrt(jnp.mean(xs * xs, axis=-1, keepdims=True) + EPS)
                NB[b, pl.ds(at, step_rows), :] = (xs * r1 * GROW[0:1, :]).astype(BF16)

        def first_norm():
            loop(block // step_rows, norm_one)
            transpose_in(NB, N1T, 0)
            transpose_in(NB, N1T, 1)

        def qkv():
            both = NB[...].reshape(2 * block, width)
            t = nn(both, weight(iq, 0, 2 * QH))
            for b in range(2):
                QK[b] = t[block * b : block * (b + 1)].T
            for at, w in tiles_of(VH):
                t = nn(both, weight(iv, at, w))
                for b in range(2):
                    VT[b, at : at + w, :] = t[block * b : block * (b + 1)].T.astype(BF16)

        lane = lax.broadcasted_iota(jnp.int32, (FEATS, LANES), 1)

        def place(i):
            b = i // PAIRS
            hp = lax.rem(i, PAIRS)
            return b, hp

        def slot(hp):
            return pl.ds(pl.multiple_of(FEATS * hp, FEATS), FEATS)

        def q_rows(b, hp, e):
            return QK[b, pl.ds(pl.multiple_of(hp * 2 * FDIM + e * FDIM, FDIM), FDIM), :]

        def k_rows(b, hp, e):
            return QK[b, pl.ds(pl.multiple_of(QH + hp * 2 * FDIM + e * FDIM, FDIM), FDIM), :]

        def v_slice(hp):
            return pl.ds(pl.multiple_of(hp * 2 * VDIM, 2 * VDIM), 2 * VDIM)

        def head_slice(hp, e):
            return pl.ds(pl.multiple_of(hp * 2 * VDIM + e * VDIM, VDIM), VDIM)

        def put_state(i, f0, f1, right_side, w0, w1):
            low = nt(f0, right_side)
            high = nt(f1, right_side)
            b, hp = place(i)
            ST[b, slot(hp), :] = jnp.where(lane < VDIM, low, high).astype(BF16)
            for e, t in ((0, w0), (1, w1)):
                WACC[b, pl.ds(2 * hp + e, 1), :] = t[0:1, :LANES]
                WACC[b, pl.ds(HALF_HEADS + 2 * hp + e, 1), 0 : FEATS - LANES] = t[0:1, LANES:]

        def state_step(i):
            b, hp = place(i)
            fs = [features(k_rows(b, hp, e)) for e in range(2)]
            ws = [nt(jnp.ones((8, block), BF16), f) for f in fs]
            put_state(i, fs[0], fs[1], VT[b, v_slice(hp), :], ws[0], ws[1])

        def states():
            WACC[...] = jnp.zeros_like(WACC)
            loop(2 * PAIRS, state_step)
            ST[:, COUNTS:, :] = WACC[...].astype(BF16)

        ranks = (hi, n_hi - 1 - hi)
        firsts = (x == 0, x == 1)
        doubling = n_hi == 4

        def away(n, j):
            t = hi + j if n == 0 else hi - j
            return dev(jnp.clip(t, 0, n_hi - 1), x, y, c)

        def state_rows(body):
            def step(i, z):
                body(pl.ds(pl.multiple_of(i * 16, 16), 16))
                return z

            lax.fori_loop(0, STATE_STEPS, step, 0)

        def start_split(d, key, src, dst, to):
            i = number(key)
            for lo in range(0, STATE, SPLIT):
                rr = pl.ds(lo, min(SPLIT, STATE - lo))
                pltpu.make_async_remote_copy(
                    src_ref=src.at[rr],
                    dst_ref=dst.at[rr],
                    send_sem=ss.at[i],
                    recv_sem=rs.at[i],
                    device_id=to,
                    device_id_type=MESH,
                ).start()
            return d

        def send_split(key, src, dst, to):
            pending[key] = start_split(remote(key, src, dst, to), key, src, dst, to)

        def state_x(n):
            send_split(("sx", n), ST.at[1 - x], SA.at[n], dev_x)

        def near(n):
            return remote(("sz", n, 0), TZ, SZ.at[n, 0], away(n, 1))

        def far(n, j):
            return remote(("sz", n, j), TY, SZ.at[n, 1], away(n, j))

        def near_sends(n):
            return lax.rem(ranks[n], 2) == 0 if doubling else ranks[n] < n_hi - 1

        def near_gets(n):
            return lax.rem(ranks[n], 2) == 1 if doubling else ranks[n] > 0

        def state_z(n):
            got(("sx", n), SA.at[n])
            for j in range(3):
                number(("sz", n, j))

            @pl.when(jnp.logical_not(near_gets(n)))
            def _():
                SZ[n, 0] = jnp.zeros((STATE, LANES), BF16)

            @pl.when(ranks[n] < 2 if doubling else ranks[n] >= 0)
            def _():
                SZ[n, 1] = jnp.zeros((STATE, LANES), BF16)

            if not doubling:

                @pl.when(near_gets(n))
                def _():
                    got(("sz", n, 0), SZ.at[n, 0])

            def add(r):
                t = ST[x, r, :].astype(F32) + SA[n, r, :].astype(F32)
                if not doubling:
                    t = t + SZ[n, 0, r, :].astype(F32)
                TZ[r, :] = t.astype(BF16)

            state_rows(add)
            pl.when(near_sends(n))(
                lambda: start_split(near(n), ("sz", n, 0), TZ, SZ.at[n, 0], away(n, 1)) and None
            )

        def state_far(n):
            if not doubling:
                return

            @pl.when(ranks[n] == 1)
            def _():
                got(("sz", n, 0), SZ.at[n, 0])

                def add(r):
                    TY[r, :] = (TZ[r, :].astype(F32) + SZ[n, 0, r, :].astype(F32)).astype(BF16)

                state_rows(add)
                for j in (1, 2):
                    start_split(far(n, j), ("sz", n, j), TY, SZ.at[n, 1], away(n, j))

        def state_end(n, dst):
            if doubling:

                @pl.when(ranks[n] == 3)
                def _():
                    got(("sz", n, 0), SZ.at[n, 0])
                    got(("sz", n, 2), SZ.at[n, 1])

                @pl.when(ranks[n] == 2)
                def _():
                    got(("sz", n, 1), SZ.at[n, 1])

            def add(r):
                total = SZ[n, 0, r, :].astype(F32) + SZ[n, 1, r, :].astype(F32)
                mine = ST[x, r, :].astype(F32)
                other = SA[n, r, :].astype(F32)
                dst[x, r, :] = (total + jnp.where(firsts[n], 0.0, other)).astype(BF16)
                SB[r, :] = (total + jnp.where(firsts[n], mine, 0.0)).astype(BF16)

            state_rows(add)
            send_split(("sy", n), SB, dst.at[x], dev_x)

        def state_got(n, dst):
            got(("sy", n), dst.at[1 - x])

        def state_sent(n):
            sent(("sx", n))
            sent(("sy", n))
            pl.when(near_sends(n))(lambda: near(n).wait_send())
            if doubling:

                @pl.when(ranks[n] == 1)
                def _():
                    far(n, 1).wait_send()
                    far(n, 2).wait_send()

        def score_z(b, hp, e):
            qh, ql = split_low(q_rows(b, hp, e))
            kh, kl = split_low(k_rows(b, hp, e))
            return tn(jnp.concatenate([kh, kh, kl], axis=0), jnp.concatenate([qh, ql, qh], axis=0))

        def counts(buf, b):
            return buf[b, COUNTS:, :]

        def count_dot(t, f, at):
            r = nn(t[:HALF_HEADS], f[:LANES]) + nn(t[HALF_HEADS:, : FEATS - LANES], f[LANES:])
            spot = lax.broadcasted_iota(jnp.int32, r.shape, 0)
            return jnp.sum(jnp.where(spot == at, r, 0.0), axis=0, keepdims=True)

        def count_outer(t, row, at):
            spot = lax.broadcasted_iota(jnp.int32, (16, block), 0)
            first = jnp.where(spot == at, row, 0.0).astype(BF16)
            second = jnp.where(spot == HALF_HEADS + at, row, 0.0).astype(BF16)
            return jnp.concatenate([tn(t, first), tn(t[:, : FEATS - LANES], second)], axis=0)

        def att_step(i):
            b, hp = place(i)
            turned = PB[b, slot(hp), :].astype(F32).T.astype(BF16)
            tops = []
            for e in range(2):
                z = score_z(b, hp, e)
                st = (1.0 + z * FDIM**-0.5 + z * z * (0.5 / FDIM)).astype(BF16)
                fq = weighted(features(q_rows(b, hp, e)))
                num = nn(VT[b, head_slice(hp, e), :], st) + nn(turned[VDIM * e : VDIM * (e + 1)], fq)
                den = jnp.sum(st.astype(F32), axis=0, keepdims=True) + count_dot(counts(PB, b), fq, 2 * hp + e)
                NUM[b, head_slice(hp, e), :] = num
                DEN[i, e : e + 1, :] = den
                tops.append(num / den)
            ATT[b, :, v_slice(hp)] = jnp.concatenate(tops, axis=0).T.astype(BF16)

        def pairs(body, lo, n):
            def step(i, z):
                body(lo + i)
                return z

            lax.fori_loop(0, n, step, 0)

        def attention(lo, n):
            pairs(att_step, lo, n)

        def col(k):
            return pl.ds(pl.multiple_of(k * quarter, quarter), quarter)

        def wrow(i, k, at, w):
            return W[i][k, :, :, at : at + w].reshape(quarter, w)

        def out_proj(dst, b):
            def one(k):
                dst[:, col(k)] = nt(ATT[b], wrow(io, k, 0, VH))

            loop(4, one)

        def proj_send():
            out_proj(SND.at[0], o)
            send("x1", SND.at[0], RCV.at[0], partner)

        def norm_two(r):
            at = pl.multiple_of(r * step_rows, step_rows)
            rr = pl.ds(at, step_rows)
            x1 = X[c, rr, :].astype(F32) + (OWN[rr, :] + RCV[0, rr, :])
            X1[rr, :] = x1
            r2 = lax.rsqrt(jnp.mean(x1 * x1, axis=-1, keepdims=True) + EPS)
            NB[c, rr, :] = (x1 * r2 * GROW[1:2, :]).astype(BF16)

        def proj_own():
            out_proj(OWN, c)

        def second_norm():
            got("x1", RCV.at[0])
            loop(block // step_rows, norm_two)
            send("n2", NB.at[c], NB.at[c], partner)
            transpose_in(NB, N2T, c)

        def second_norm_in():
            got("n2", NB.at[o])
            transpose_in(NB, N2T, o)

        def ffn_in(j):
            base, w = parts[j]
            for at, tw in tiles_of(w):
                TG[:, 0:tw] = nn(NB[...].reshape(2 * block, width), weight(gi[f"g{j}"], at, tw))
                TU[:, 0:tw] = nn(NB[...].reshape(2 * block, width), weight(gi[f"u{j}"], at, tw))
                lo = base + at

                def one(r):
                    rr = pl.ds(pl.multiple_of(r * 64, 64), 64)
                    gate, up = TG[rr, 0:tw], TU[rr, 0:tw]
                    sg = 0.5 + 0.5 * jnp.tanh(0.5 * gate)
                    silu = gate * sg
                    HID[rr, lo : lo + tw] = (silu * up).astype(BF16)
                    CA[rr, lo : lo + tw] = (up * sg * (1.0 + gate * (1.0 - sg))).astype(BF16)
                    CB[rr, lo : lo + tw] = silu.astype(BF16)

                loop(2 * block // 64, one)
        def ffn_back(j):
            base, w = parts[j]
            i = gi[f"d{j}"]
            for at, tw in tiles_of(w):
                TG[:, 0:tw] = nn(DY[...].reshape(2 * block, width), weight(i, at, tw))
                lo = base + at

                def one(r):
                    rr = pl.ds(pl.multiple_of(r * 64, 64), 64)
                    dh = TG[rr, 0:tw]
                    CA[rr, lo : lo + tw] = (dh * CA[rr, lo : lo + tw].astype(F32)).astype(BF16)
                    CB[rr, lo : lo + tw] = (dh * CB[rr, lo : lo + tw].astype(F32)).astype(BF16)

                loop(2 * block // 64, one)

        def tokens_of(b):
            return pl.ds(pl.multiple_of(b * block, block), block)

        def dn2(dst, b):
            def one(k):
                acc = None
                for j, (base, w) in enumerate(parts):
                    for buf, i in ((CA, gi[f"g{j}"]), (CB, gi[f"u{j}"])):
                        t = nt(buf[tokens_of(b), base : base + w], wrow(i, k, 0, w))
                        acc = t if acc is None else acc + t
                dst[:, col(k)] = acc

            loop(4, one)

        def dn2_send():
            sent("x1")
            dn2(SND.at[0], o)
            send("dn2", SND.at[0], RCV.at[1], partner)

        def dn2_own():
            dn2(OWN, c)

        def norm_two_back(r):
            at = pl.multiple_of(r * step_rows, step_rows)
            rr = pl.ds(at, step_rows)
            d = OWN[rr, :] + RCV[1, rr, :]
            x1 = X1[rr, :]
            r2 = lax.rsqrt(jnp.mean(x1 * x1, axis=-1, keepdims=True) + EPS)
            t = d * (x1 * r2)
            GACC[8:16, :] += t[:8] + t[8:]
            a2 = d * GROW[1:2, :]
            dx = DY[c, rr, :].astype(F32) + (
                r2 * a2 - x1 * (r2 * r2 * r2) * jnp.mean(a2 * x1, axis=-1, keepdims=True)
            )
            din_ref[rr, :] = dx
            NB[c, rr, :] = dx.astype(BF16)

        def second_norm_back():
            got("dn2", RCV.at[1])
            sent("n2")
            loop(block // step_rows, norm_two_back)
            send("dx1", NB.at[c], NB.at[c], partner)
            transpose_in(NB, DYT, c)

        def datt():
            got("dx1", NB.at[o])
            transpose_in(NB, DYT, o)
            for at, tw in tiles_of(VH):
                t = nn(NB[...].reshape(2 * block, width), weight(io, at, tw))
                for b in range(2):
                    DATT[b, at : at + tw, :] = t[block * b : block * (b + 1)].T

        def back_state_step(i):
            b, hp = place(i)
            fs, ws = [], []
            for e in range(2):
                hs = head_slice(hp, e)
                datt, num, den = DATT[b, hs, :], NUM[b, hs, :], DEN[i, e : e + 1, :]
                dd = (-jnp.sum(datt * num, axis=0, keepdims=True) / (den * den)).astype(BF16)
                DNUM[b, hs, :] = (datt / den).astype(BF16)
                DDEN[i, e : e + 1, :] = dd.astype(F32)
                f = features(q_rows(b, hp, e))
                fs.append(f)
                ws.append(nt(jnp.broadcast_to(dd, (8, block)), f))
            put_state(i, fs[0], fs[1], DNUM[b, v_slice(hp), :], ws[0], ws[1])

        def back_states():
            WACC[...] = jnp.zeros_like(WACC)
            state_sent(0)
            loop(2 * PAIRS, back_state_step)
            ST[:, COUNTS:, :] = WACC[...].astype(BF16)

        zeros_head = jnp.zeros((VDIM, block), BF16)

        def masked(t, e):
            return jnp.concatenate([zeros_head, t] if e else [t, zeros_head], axis=0)

        def back_step(i):
            b, hp = place(i)
            for e in range(2):
                hs = head_slice(hp, e)
                q, kk = q_rows(b, hp, e), k_rows(b, hp, e)
                qh, ql = split_low(q)
                kh, kl = split_low(kk)
                z = tn(jnp.concatenate([kh, kh, kl], axis=0), jnp.concatenate([qh, ql, qh], axis=0))
                st = (1.0 + z * FDIM**-0.5 + z * z * (0.5 / FDIM)).astype(BF16)
                dnum, dden = DNUM[b, hs, :], DDEN[i, e : e + 1, :]
                ds = (tn(VT[b, hs, :], dnum) + dden).astype(BF16).astype(F32)
                dz = (ds * (FDIM**-0.5 + z * (1.0 / FDIM))).astype(BF16)
                t = nn(jnp.concatenate([kh, kl], axis=0), dz)
                dq = t[:FDIM] + t[FDIM:]
                t = nt(jnp.concatenate([qh, ql], axis=0), dz)
                dk = t[:FDIM] + t[FDIM:]
                DV[b, hs, :] = nt(dnum, st)
                df = nn(PB[b, slot(hp), :], masked(dnum, e)) + count_outer(counts(PB, b), dden, 2 * hp + e)
                DQK[b, pl.ds(pl.multiple_of(hp * 2 * FDIM + e * FDIM, FDIM), FDIM), :] = dq + features_back(q, df)
                DQK[b, pl.ds(pl.multiple_of(QH + hp * 2 * FDIM + e * FDIM, FDIM), FDIM), :] = dk

        def back_rows(lo, n):
            pairs(back_step, lo, n)

        def y_part(dst, b):
            def one(k):
                acc = None
                for j, (base, w) in enumerate(parts):
                    t = nt(HID[tokens_of(b), base : base + w], wrow(gi[f"d{j}"], k, 0, w))
                    acc = t if acc is None else acc + t
                dst[:, col(k)] = acc

            loop(4, one)

        def finish(r):
            rr = pl.ds(pl.multiple_of(r * step_rows, step_rows), step_rows)
            out_ref[rr, :] = (X1[rr, :] + (OWN[rr, :] + RCV[2, rr, :])).astype(BF16)

        def y_send():
            y_part(SND.at[1], o)
            send("y", SND.at[1], RCV.at[2], partner)

        def y_own():
            y_part(OWN, c)

        def y_end():
            got("y", RCV.at[2])
            loop(block // step_rows, finish)

        def key_step(i):
            b, hp = place(i)
            turned = PX[b, slot(hp), :].astype(F32).T.astype(BF16)
            for e in range(2):
                hs = head_slice(hp, e)
                kk = k_rows(b, hp, e)
                df = nn(PX[b, slot(hp), :], masked(VT[b, hs, :], e)) + count_outer(
                    counts(PX, b), jnp.ones((1, block), F32), 2 * hp + e
                )
                kr = pl.ds(pl.multiple_of(QH + hp * 2 * FDIM + e * FDIM, FDIM), FDIM)
                DQK[b, kr, :] += features_back(kk, df)
                DV[b, hs, :] += nn(turned[VDIM * e : VDIM * (e + 1)], weighted(features(kk)))

        def keys_back(lo, n):
            pairs(key_step, lo, n)

        def dqkv():
            for b in range(2):
                DQKV[b, :, 0 : 2 * QH] = DQK[b].T.astype(BF16)
                for at, tw in tiles_of(VH):
                    DQKV[b, :, 2 * QH + at : 2 * QH + at + tw] = DV[b, at : at + tw, :].T.astype(BF16)

        def dn1(dst, b):
            def one(k):
                dst[:, col(k)] = nt(DQKV[b, :, : 2 * QH], wrow(iq, k, 0, 2 * QH)) + nt(
                    DQKV[b, :, 2 * QH :], wrow(iv, k, 0, VH)
                )

            loop(4, one)

        def dn1_send():
            sent("dn2")
            dn1(SND.at[0], o)
            send("dn1", SND.at[0], RCV.at[0], partner)

        def dn1_own():
            dn1(OWN, c)

        def norm_one_back(r):
            rr = pl.ds(pl.multiple_of(r * step_rows, step_rows), step_rows)
            d = OWN[rr, :] + RCV[0, rr, :]
            xs = X[c, rr, :].astype(F32)
            r1 = lax.rsqrt(jnp.mean(xs * xs, axis=-1, keepdims=True) + EPS)
            t = d * (xs * r1)
            GACC[0:8, :] += t[:8] + t[8:]
            a1 = d * GROW[0:1, :]
            din_ref[rr, :] += r1 * a1 - xs * (r1 * r1 * r1) * jnp.mean(a1 * xs, axis=-1, keepdims=True)

        def first_norm_back():
            got("dn1", RCV.at[0])
            loop(block // step_rows, norm_one_back)
            sum_a = jnp.sum(GACC[0:8, :], axis=0, keepdims=True)
            gf = jnp.sum(GACC[8:16, :], axis=0, keepdims=True)
            last = ri["gain"]
            for k in range(4):
                row = lax.broadcasted_iota(jnp.int32, (LANES, quarter), 0)
                sl = slice(quarter * k, quarter * (k + 1))
                mat = jnp.where(row == 0, sum_a[:, sl], 0.0) + jnp.where(row == 1, gf[:, sl], 0.0)
                G[last][k] = mat.T.astype(BF16).reshape(4, rows2, LANES)
        def part_of(buf, j):
            base, w = parts[j]
            return lambda: buf[:, base : base + w]

        def grad(name):
            kind = name.rstrip("0123456789")
            if kind == "d":
                put_grad(ri[name], DYT, part_of(HID, int(name[1:])))
            elif kind == "g":
                put_grad(ri[name], N2T, part_of(CA, int(name[1:])))
            elif kind == "u":
                put_grad(ri[name], N2T, part_of(CB, int(name[1:])))
            elif name == "out":
                put_grad(ri[name], DYT, lambda: ATT[...].reshape(2 * block, VH))
            elif name == "qk":
                put_grad(ri[name], N1T, lambda: DQKV[:, :, 0 : 2 * QH].reshape(2 * block, 2 * QH))
            elif name == "v":
                put_grad(ri[name], N1T, lambda: DQKV[:, :, 2 * QH :].reshape(2 * block, VH))

        def adv(st, name):
            go_to(st, ri[name])

        def greeted():
            pl.semaphore_wait(barrier, len(greet))
            if members > 1:

                @pl.when(hi < n_hi - 1)
                def _():
                    pl.semaphore_wait(barrier, 1)

                @pl.when(hi > 0)
                def _():
                    pl.semaphore_wait(barrier, 1)

        cx = local(tok, X.at[c])
        cy = local(cot, DY.at[c])
        for i in range(len(gather)):
            e0(i)
        cx.wait()
        cy.wait()
        greeted()

        for i in range(len(gather)):
            e0_send(i)
        send("x", X.at[c], X.at[c], partner)
        send("dy", DY.at[c], DY.at[c], partner)
        z1()
        ga(1, 0)
        ga(1, 1)
        ga(2, 0)
        ga(1, 2)
        ga(2, 1)
        ga(3, 0)
        z2()
        transpose_in(DY, DYT, c)
        got("x", X.at[o])
        got("dy", DY.at[o])
        transpose_in(DY, DYT, o)
        ga(1, 3)
        ga(1, 4)
        ga(2, 2)
        ga(3, 1)
        ga(4, 0)
        ga(1, 5)
        gains()
        first_norm()
        ga(2, 3)
        ga(3, 2)
        ga(2, 4)
        ga(4, 1)
        ga(4, 2)
        qkv()
        states()
        state_x(0)
        ga(1, 6)
        ga(1, 7)
        ga(1, 8)
        ga(1, 9)
        ga(1, 10)
        ga(1, 11)
        ga(2, 5)
        ga(2, 6)
        ga(3, 3)
        state_z(0)
        ga(2, 7)
        ga(3, 4)
        state_far(0)
        ga(2, 8)
        ga(3, 5)
        state_end(0, PB)
        ga(2, 9)
        ga(3, 6)
        state_got(0, PB)
        ga(3, 7)
        z3()
        attention(0, 4)
        attention(4, 4)
        ga(2, 10)
        ga(3, 8)
        ga(4, 3)
        proj_send()
        proj_own()
        second_norm()
        second_norm_in()
        ga(2, 11)
        ga(3, 9)
        ga(4, 4)
        ga(4, 5)
        ffn_in(0)
        grad("d0")
        zf1()
        ga(3, 10)
        ga(4, 6)
        ga(4, 7)
        ffn_in(1)
        grad("d1")
        go_to(1, 1)
        ga(3, 11)
        ga(4, 8)
        ga(4, 9)
        ffn_in(2)
        grad("d2")
        go_to(1, 2)
        z4()
        ffn_back(0)
        go_to(2, 1)
        grad("g0")
        go_to(1, 3)
        ga(4, 10)
        ffn_back(1)
        go_to(2, 2)
        go_to(3, 1)
        grad("u0")
        go_to(1, 4)
        ga(4, 11)
        ffn_back(2)
        dn2_send()
        go_to(2, 3)
        dn2_own()
        go_to(3, 2)
        grad("g1")
        go_to(1, 5)
        second_norm_back()
        datt()
        go_to(2, 4)
        back_states()
        state_x(1)
        go_to(3, 3)
        go_to(4, 1)
        grad("u1")
        go_to(4, 2)
        go_to(1, 6)
        state_z(1)
        go_to(2, 5)
        go_to(3, 4)
        zf2()
        go_to(4, 3)
        back_rows(0, 4)
        grad("g2")
        go_to(1, 7)
        state_far(1)
        go_to(2, 6)
        go_to(3, 5)
        go_to(4, 4)
        back_rows(4, 4)
        grad("u2")
        go_to(1, 8)
        zf3()
        state_end(1, PX)
        go_to(2, 7)
        go_to(3, 6)
        go_to(4, 5)
        grad("out")
        go_to(1, 9)
        y_send()
        y_own()
        zf4()
        state_got(1, PX)
        keys_back(0, 4)
        keys_back(4, 4)
        dqkv()
        grad("qk")
        go_to(2, 8)
        go_to(3, 7)
        go_to(4, 6)
        go_to(1, 10)
        grad("v")
        go_to(1, 11)
        dn1_send()
        y_end()
        dn1_own()
        go_to(2, 9)
        go_to(3, 8)
        go_to(4, 7)
        first_norm_back()
        go_to(2, 10)
        go_to(3, 9)
        go_to(4, 8)
        go_to(1, 12)
        go_to(2, 11)
        go_to(3, 10)
        go_to(4, 9)
        go_to(2, 12)
        go_to(3, 11)
        go_to(4, 10)
        go_to(3, 12)
        go_to(4, 11)
        go_to(4, 12)

        n = len(reduce)
        for i in range(n):
            got(("f4", i), go.at[o, :, offsets[i] : offsets[i] + reduce[i][1]])
        for d in local_pending:
            d.wait()
        state_sent(1)
        for d in pending.values():
            d.wait_send()

    return kernel


def call_kernel(tok, cot, shards, seq_size, ff, ff_half):
    block, width = tok.shape
    gather, reduce = plan(ff_half)
    rows = width // 32
    vmem = pltpu.VMEM
    any_spec = pl.BlockSpec(memory_space=pl.ANY)
    vmem_spec = pl.BlockSpec(memory_space=vmem)
    total_width = sum(w for _, w in reduce)
    pack_width = sum(w for _, w in gather)
    state = vmem((2, STATE, LANES), BF16)
    scratch = [vmem((4, 4, 2 * (16 if name == "gain" else rows), w), BF16) for name, w in gather]
    scratch += [vmem((4, 4, 2 * rows, w), BF16) for _, w in reduce]
    scratch += [
        vmem((rows, pack_width), BF16),
        vmem((RING, 2, 4, 2 * rows, PIECE), BF16),
        vmem((RING, 4, 2 * rows, PIECE), BF16),
        vmem((RING, 3, 2 * rows, PIECE), BF16),
        vmem((3, 4, 2 * rows, PIECE), BF16),
        vmem((3, 2 * rows, PIECE), BF16),
        vmem((2, rows, total_width), F32),
        vmem((2, block, width), BF16),
        vmem((2, block, width), BF16),
        vmem((2, block, width), BF16),
        vmem((width, 2 * block), BF16),
        vmem((width, 2 * block), BF16),
        vmem((width, 2 * block), BF16),
        vmem((2 * block, ff_half), BF16),
        vmem((2 * block, ff_half), BF16),
        vmem((2 * block, ff_half), BF16),
        vmem((block, width), F32),
        vmem((2, block, width), F32),
        vmem((3, block, width), F32),
        vmem((block, width), F32),
        vmem((2, VH, block), F32),
        vmem((2, VH, block), F32),
        vmem((2, 2 * QH, block), F32),
        vmem((2, VH, block), BF16),
        vmem((2, block, VH), BF16),
        vmem((2 * PAIRS, 8, block), F32),
        vmem((2, VH, block), BF16),
        vmem((2 * PAIRS, 8, block), F32),
        vmem((2, 2 * QH, block), F32),
        vmem((2, VH, block), F32),
        vmem((2, block, 2 * QH + VH), BF16),
        state,
        vmem((2, STATE, LANES), BF16),
        vmem((2, 2, STATE, LANES), BF16),
        vmem((STATE, LANES), BF16),
        vmem((STATE, LANES), BF16),
        vmem((STATE, LANES), BF16),
        state,
        state,
        vmem((2, 16, LANES), F32),
        vmem((2 * block, 256), F32),
        vmem((2 * block, 256), F32),
        vmem((8, width), F32),
        vmem((16, width), F32),
        pltpu.SemaphoreType.DMA((n_messages(gather, reduce),)),
        pltpu.SemaphoreType.DMA((n_messages(gather, reduce),)),
        pltpu.SemaphoreType.DMA((2 + len(reduce),)),
    ]
    out_shape = [
        jax.ShapeDtypeStruct((block, width), BF16),
        jax.ShapeDtypeStruct((block, width), F32),
        jax.ShapeDtypeStruct((2, rows, total_width), F32),
    ]
    return pl.pallas_call(
        make_kernel(seq_size, block, width, ff, ff_half),
        out_shape=out_shape,
        in_specs=[any_spec] * 2 + [vmem_spec] * len(shards),
        out_specs=[vmem_spec] * 2 + [any_spec],
        scratch_shapes=scratch,
        compiler_params=pltpu.CompilerParams(
            collective_id=0, has_side_effects=True, vmem_limit_bytes=62 * 2**20
        ),
    )(tok, cot, *shards)


def n_messages(gather, reduce):
    return 7 * len(gather) + 24


def call_finish(output, input_grad, grads, ff, ff_half):
    block, width = output.shape
    rows = grads.shape[1]
    _, reduce = plan(ff_half)
    at = dict(zip([name for name, _ in reduce], offsets_of(reduce)))
    parts = pieces_of(ff_half)
    vmem_spec = pl.BlockSpec(memory_space=pltpu.VMEM)
    hbm_spec = pl.BlockSpec(memory_space=pltpu.HBM)

    def kernel(o_in, i_in, g_hbm, o_out, i_out, ag, qg, kg, vg, og, fg, gg, ug, dg, g_in, o_held, i_held, sems):
        c2 = pltpu.make_async_copy(g_hbm, g_in, sems.at[2])
        c2.start()
        c0 = pltpu.make_async_copy(i_in, i_held, sems.at[0])
        c1 = pltpu.make_async_copy(o_in, o_held, sems.at[1])
        c0.start()
        c1.start()
        c0.wait()
        c3 = pltpu.make_async_copy(i_held, i_out, sems.at[3])
        c3.start()
        c1.wait()
        c4 = pltpu.make_async_copy(o_held, o_out, sems.at[4])
        c4.start()
        c2.wait()
        gain = (g_in[0, :, at["gain"] : at["gain"] + LANES] + g_in[1, :, at["gain"] : at["gain"] + LANES]).T
        ag[...] = gain[0:1, :rows]
        fg[...] = gain[1:2, :rows]
        for h in range(2):
            qg[:, QH * h : QH * (h + 1)] = g_in[h, :, at["qk"] : at["qk"] + QH]
            kg[:, QH * h : QH * (h + 1)] = g_in[h, :, at["qk"] + QH : at["qk"] + 2 * QH]
            vg[:, VH * h : VH * (h + 1)] = g_in[h, :, at["v"] : at["v"] + VH]
            og[:, VH * h : VH * (h + 1)] = g_in[h, :, at["out"] : at["out"] + VH]
            for j, (base, w) in enumerate(parts):
                lo = ff_half * h + base
                have = min(w, ff - lo)
                for ref, letter in ((gg, "g"), (ug, "u"), (dg, "d")):
                    a = at[f"{letter}{j}"]
                    ref[:, lo : lo + have] = g_in[h, :, a : a + have]
        c3.wait()
        c4.wait()

    shapes = [(1, rows), (rows, 2 * QH), (rows, 2 * QH), (rows, 2 * VH), (rows, 2 * VH), (1, rows)] + [(rows, ff)] * 3
    return pl.pallas_call(
        kernel,
        out_shape=[jax.ShapeDtypeStruct(output.shape, BF16), jax.ShapeDtypeStruct(input_grad.shape, F32)]
        + [jax.ShapeDtypeStruct(n, F32) for n in shapes],
        in_specs=[hbm_spec] * 3,
        out_specs=[hbm_spec] * 2 + [vmem_spec] * len(shapes),
        scratch_shapes=[
            pltpu.VMEM(grads.shape, F32),
            pltpu.VMEM(output.shape, BF16),
            pltpu.VMEM(input_grad.shape, F32),
            pltpu.SemaphoreType.DMA((5,)),
        ],
        compiler_params=pltpu.CompilerParams(vmem_limit_bytes=60 * 2**20),
    )(output, input_grad, grads)


def body(
    tokens, attn_gain, query_weight, key_weight, value_weight, out_weight, ffn_gain, gate_weight, up_weight, down_weight, cotangent
):
    seq_size = lax.axis_size("seq")
    members = seq_size // 8
    _, block, width = tokens.shape
    ff = gate_weight.shape[1]
    ff_half = LANES * ((ff + 2 * LANES - 1) // (2 * LANES))
    few = attn_gain.shape[0]
    groups = [[(g * members + m) * 2 + x for m in range(members)] for g in range(4) for x in range(2)]

    shards = [attn_gain, query_weight, key_weight, value_weight, out_weight.T, ffn_gain, gate_weight, up_weight, down_weight.T]
    if members > 1:
        shards = [
            lax.all_gather(a, "seq", axis_index_groups=groups, axis=0, tiled=True) for a in shards
        ]
    shards = [a.reshape(1, -1) if a.ndim == 1 else a for a in shards]

    def turn(t):
        if members == 1:
            return t
        return t.reshape(block, 4, members, 2, 4, few).transpose(0, 1, 3, 4, 2, 5).reshape(block, width)

    def turn_back(t):
        if members == 1:
            return t
        return t.reshape(block, 4, 2, 4, members, few).transpose(0, 1, 4, 2, 3, 5).reshape(block, width)

    output, input_grad, grads = call_kernel(turn(tokens[0]), turn(cotangent[0]), shards, seq_size, ff, ff_half)
    if members == 1:
        o, i, ag, qg, kg, vg, og, fg, gg, ug, dg = call_finish(output, input_grad, grads, ff, ff_half)
        return o[None], i[None], ag[0], qg, kg, vg, og.T, fg[0], gg, ug, dg.T
    grads = lax.psum_scatter(grads, "seq", scatter_dimension=1, axis_index_groups=groups, tiled=True)
    _, reduce = plan(ff_half)
    by = {name: grads[:, :, a : a + w] for (name, w), a in zip(reduce, offsets_of(reduce))}
    n_parts = len(pieces_of(ff_half))

    def joined(a):
        return jnp.concatenate([a[0], a[1]], axis=1)

    def ff_joined(letter):
        return joined(jnp.concatenate([by[f"{letter}{j}"] for j in range(n_parts)], axis=2))[:, :ff]

    gain = by["gain"][0] + by["gain"][1]
    return (
        turn_back(output)[None],
        turn_back(input_grad)[None],
        gain[:, 0],
        joined(by["qk"][:, :, :QH]),
        joined(by["qk"][:, :, QH:]),
        joined(by["v"]),
        joined(by["out"]).T,
        gain[:, 1],
        ff_joined("g"),
        ff_joined("u"),
        ff_joined("d").T,
    )


def solution(mesh):
    both = ("seq", "dp")
    row, column, whole = P(both, None), P(None, both), P("dp", "seq", None)
    return jax.shard_map(
        body,
        mesh=mesh,
        in_specs=(whole, P(both), row, row, row, column, P(both), row, row, column, whole),
        out_specs=(whole, whole, P(both), row, row, row, column, P(both), row, row, column),
        check_vma=False,
    )
```

```python
import jax
import jax.numpy as jnp
from jax import lax
from jax.experimental import pallas as pl
from jax.experimental.pallas import tpu as pltpu
from jax.sharding import PartitionSpec as P

HEADS = 16
FDIM = 16
VDIM = 64
EPS = 1e-05
LIN = FDIM**-0.25
QUAD = (2.0 * FDIM) ** -0.5
SHIFTS = FDIM // 2
HALF = FDIM // 2
FEATS = FDIM * (SHIFTS + 2)
HALF_HEADS = HEADS // 2
QH = HALF_HEADS * FDIM
VH = HALF_HEADS * VDIM
PAIRS = HALF_HEADS // 2
COUNTS = PAIRS * FEATS
STATE = COUNTS + 16
STATE_STEPS = STATE // 16
SPLIT = 96
LANES = 128
ALIKE = (("g0", "u2"), ())
PIECE = 512
RING = 6
MESH = pl.DeviceIdType.MESH
F32 = jnp.float32
BF16 = jnp.bfloat16


def pieces_of(width):
    out, at = [], 0
    while at < width:
        out.append((at, min(PIECE, width - at)))
        at += PIECE
    return out


def tiles_of(width):
    out, at = [], 0
    while at < width:
        out.append((at, min(256, width - at)))
        at += 256
    return out


def nn(a, b):
    return jnp.dot(a, b, preferred_element_type=F32)


def nt(a, b):
    return lax.dot_general(a, b, (((1,), (1,)), ((), ())), preferred_element_type=F32)


def tn(a, b):
    return lax.dot_general(a, b, (((0,), (0,)), ((), ())), preferred_element_type=F32)


def ahead(t, d):
    return t if d == 0 else pltpu.roll(t, FDIM - d, 0)


def behind(t, d):
    return t if d == 0 else pltpu.roll(t, d, 0)


def features(u):
    rows = [u * ahead(u, d) * QUAD for d in range(SHIFTS)]
    spot = lax.broadcasted_iota(jnp.int32, u.shape, 0)
    last = jnp.where(spot < HALF, u * ahead(u, HALF) * QUAD, jnp.where(spot == HALF, 1.0, 0.0))
    return jnp.concatenate(rows + [last, u * LIN], axis=0).astype(BF16)


def weighted(f):
    at = FDIM * SHIFTS
    scale = jnp.where(lax.broadcasted_iota(jnp.int32, (FDIM, f.shape[1]), 0) < HALF, 2.0, 1.0).astype(BF16)
    return jnp.concatenate([f[:FDIM], f[FDIM:at] * 2, f[at : at + FDIM] * scale, f[at + FDIM :]], axis=0)


def features_back(u, df):
    at = FDIM * SHIFTS
    total = df[at + FDIM :] * LIN
    for d in range(SHIFTS + 1):
        t = df[FDIM * d : FDIM * (d + 1)] * (QUAD * (2.0 if d else 1.0))
        if d == HALF:
            t = jnp.where(lax.broadcasted_iota(jnp.int32, t.shape, 0) < HALF, t, 0.0)
        total = total + t * ahead(u, d) + behind(t * u, d)
    return total


def split_low(u):
    high = u.astype(BF16)
    return high, (u - high.astype(F32)).astype(BF16)


def plan(ff_half):
    parts = pieces_of(ff_half)
    gather = [("gain", LANES), ("qk", 2 * QH), ("v", VH), ("out", VH)]
    for j, (_, w) in enumerate(parts):
        gather += [(f"g{j}", w), (f"u{j}", w)]
    gather += [(f"d{j}", w) for j, (_, w) in enumerate(parts)][1:]
    gather += [("d0", parts[0][1])]
    reduce = [(f"d{j}", w) for j, (_, w) in enumerate(parts)]
    for j, (_, w) in enumerate(parts):
        reduce += [(f"g{j}", w), (f"u{j}", w)]
    reduce += [("out", VH), ("qk", 2 * QH), ("v", VH), ("gain", LANES)]
    return gather, reduce


def offsets_of(chunks):
    out, at = [], 0
    for _, w in chunks:
        out.append(at)
        at += w
    return out


def make_kernel(seq_size, block, width, ff, ff_half):
    gather, reduce = plan(ff_half)
    parts = pieces_of(ff_half)
    n_parts = len(parts)
    gi = {name: i for i, (name, _) in enumerate(gather)}
    ri = {name: i for i, (name, _) in enumerate(reduce)}
    members = seq_size // 8
    n_hi = seq_size // 2
    rows = width // 32
    rows2 = 2 * rows
    quarter = width // 4
    offsets = offsets_of(reduce)
    pack_at = offsets_of(gather)

    def kernel(*refs):
        it = iter(refs)
        take = lambda n: [next(it) for _ in range(n)]
        tok, cot = take(2)
        attn_in, q_in, k_in, v_in, o_in, ffn_in_gain, g_in, u_in, d_in = take(9)
        out_ref, din_ref, go = take(3)
        W = take(len(gather))
        G = take(len(reduce))
        (PK, R1, R2, R3, RZ, RY, FS, X, DY, NB, N1T, N2T, DYT, HID, CA, CB, X1, SND, RCV, OWN) = take(20)
        (NUM, DATT, QK, VT, ATT, DEN, DNUM, DDEN, DQK, DV, DQKV) = take(11)
        (ST, SA, SZ, TZ, TY, SB, PB, PX, WACC, TG, TU, GROW, GACC) = take(13)
        ss, rs, ls = take(3)

        s, dp = lax.axis_index("seq"), lax.axis_index("dp")
        hi, x = s // 2, lax.rem(s, 2)
        y, c = dp // 2, lax.rem(dp, 2)
        g, m = hi // members, lax.rem(hi, members)
        o = 1 - c
        p, pab = 2 * x + y, 2 * (1 - x) + (1 - y)

        def dev(hi_, x_, y_, c_):
            return (hi_ * 2 + x_, y_ * 2 + c_)

        partner = dev(hi, x, y, o)
        dev_x, dev_y = dev(hi, 1 - x, y, c), dev(hi, x, 1 - y, c)

        def roles(flip):
            nx, ny = x + flip * (1 - 2 * x), y + (1 - flip) * (1 - 2 * y)
            return dev(hi, nx, ny, c), 2 * nx + ny

        mixed = roles(o) + roles(c)
        alike = roles(1) + roles(0)

        def way(name, phase):
            return alike if name in ALIKE[phase] else mixed

        ups = [lax.rem(g + j, 4) for j in range(4)]
        downs = [lax.rem(g + 4 - j, 4) for j in range(4)]
        dev_up = [dev(u * members + m, x, y, c) for u in ups]
        right = dev(jnp.minimum(hi + 1, n_hi - 1), x, y, c)
        left = dev(jnp.maximum(hi - 1, 0), x, y, c)

        n_local = [0]
        local_pending = []

        def local(src, dst):
            d = pltpu.make_async_copy(src, dst, ls.at[n_local[0]])
            n_local[0] += 1
            d.start()
            return d

        barrier = pltpu.get_barrier_semaphore()
        greet = [partner, dev_x, dev_y] + dev_up[1:]
        for d in greet:
            pl.semaphore_signal(barrier, inc=1, device_id=d, device_id_type=MESH)
        if members > 1:

            @pl.when(hi < n_hi - 1)
            def _():
                pl.semaphore_signal(barrier, inc=1, device_id=right, device_id_type=MESH)

            @pl.when(hi > 0)
            def _():
                pl.semaphore_signal(barrier, inc=1, device_id=left, device_id_type=MESH)

        numbers = {}
        pending = {}

        def number(key):
            return numbers.setdefault(again(key), len(numbers))

        def again(key):
            if key[0] == "f1":
                return (("e2b", key[1]), ("e3", key[1]))[key[2]]
            return {"f2": ("e2a",), "f3": ("e1",), "f4": ("e0",)}.get(key[0], key[:1]) + key[1:]

        def remote(key, src, dst, to):
            i = number(key)
            return pltpu.make_async_remote_copy(
                src_ref=src, dst_ref=dst, send_sem=ss.at[i], recv_sem=rs.at[i], device_id=to, device_id_type=MESH
            )

        def send(key, src, dst, to):
            key = again(key)
            if key in pending:
                sent(key)
            d = remote(key, src, dst, to)
            d.start()
            pending[key] = d

        def sent(key):
            pending.pop(key).wait_send()

        def got(key, ref):
            remote(key, ref, ref, partner).wait_recv()

        def pack(i, lower, upper):
            w = gather[i][1]
            r = 16 if i == 0 else rows
            mine = W[i].at[g, p, pl.ds(pl.multiple_of(r * c, r), r)]
            stage = PK.at[0:r, pack_at[i] : pack_at[i] + w]

            @pl.when(c == 0)
            def _():
                mine[...] = lower()
                stage[...] = upper()

            @pl.when(c == 1)
            def _():
                mine[...] = upper()
                stage[...] = lower()

        def e0_send(i):
            w = gather[i][1]
            r = 16 if i == 0 else rows
            mine = W[i].at[g, p, pl.ds(pl.multiple_of(r * c, r), r)]
            send(("e0", i), PK.at[0:r, pack_at[i] : pack_at[i] + w], mine, partner)

        def ff_piece(ref, at, w):
            have = min(w, ff - at)
            if have == w:
                return ref[:, at : at + w]
            return jnp.concatenate([ref[:, at : at + have], jnp.zeros((ref.shape[0], w - have), BF16)], axis=1)

        def gain_block():
            out = jnp.zeros((16, LANES), F32)
            lanes = lax.broadcasted_iota(jnp.int32, (16, LANES), 1) // rows
            row = lax.broadcasted_iota(jnp.int32, (16, LANES), 0)
            for n, ref in enumerate((attn_in, ffn_in_gain)):
                t = jnp.concatenate([ref[...].astype(F32)] * (LANES // rows), axis=1)
                out = jnp.where((lanes == dp) & (row == n), t, out)
            return out.astype(BF16)

        def e0(i):
            name, w = gather[i]
            if name == "gain":
                pack(i, gain_block, gain_block)
            elif name == "qk":
                pack(
                    i,
                    lambda: jnp.concatenate([q_in[:, :QH], k_in[:, :QH]], axis=1),
                    lambda: jnp.concatenate([q_in[:, QH:], k_in[:, QH:]], axis=1),
                )
            elif name == "v":
                pack(i, lambda: v_in[:, :VH], lambda: v_in[:, VH:])
            elif name == "out":
                pack(i, lambda: o_in[:, :VH], lambda: o_in[:, VH:])
            else:
                at = parts[int(name[1:])][0]
                ref = {"g": g_in, "u": u_in, "d": d_in}[name[0]]
                pack(i, lambda: ff_piece(ref, at, w), lambda: ff_piece(ref, ff_half + at, w))

        def e1(i):
            r = 16 if i == 0 else rows
            got(("e0", i), W[i].at[g, p, pl.ds(pl.multiple_of(r * o, r), r)])
            for j in (1, 2, 3):
                send(("e1", i, j), W[i].at[g, p], W[i].at[g, p], dev_up[j])

        def e2(i):
            dev_a, pa, dev_b, pb = way(gather[i][0], 0)
            for j in (1, 2, 3):
                got(("e1", i, j), W[i].at[downs[j], p])
            send(("e2b", i), W[i].at[:, p], W[i].at[:, p], dev_b)
            send(("e2a", i), W[i].at[:, p], W[i].at[:, p], dev_a)

        def e3(i):
            dev_a, pa, dev_b, pb = way(gather[i][0], 0)
            got(("e2a", i), W[i].at[:, pa])
            send(("e3", i), W[i].at[:, pa], W[i].at[:, pa], dev_b)

        def e4(i):
            dev_a, pa, dev_b, pb = way(gather[i][0], 0)
            got(("e2b", i), W[i].at[:, pb])
            got(("e3", i), W[i].at[:, pab])

        iz = len(gather) - 1

        def z1():
            dev_a, pa, dev_b, pb = way(gather[iz][0], 0)
            r = rows
            got(("e0", iz), W[iz].at[g, p, pl.ds(pl.multiple_of(r * o, r), r)])
            send(("e2b", iz), W[iz].at[g, p], W[iz].at[g, p], dev_b)
            send(("e2a", iz), W[iz].at[g, p], W[iz].at[g, p], dev_a)

        def z2():
            dev_a, pa, dev_b, pb = way(gather[iz][0], 0)
            got(("e2a", iz), W[iz].at[g, pa])
            send(("e3", iz), W[iz].at[g, pa], W[iz].at[g, pa], dev_b)

        def z3():
            dev_a, pa, dev_b, pb = way(gather[iz][0], 0)
            got(("e2b", iz), W[iz].at[g, pb])
            got(("e3", iz), W[iz].at[g, pab])
            for j in (1, 2, 3):
                send(("e1", iz, j), W[iz].at[g], W[iz].at[g], dev_up[j])

        def z4():
            for j in (1, 2, 3):
                got(("e1", iz, j), W[iz].at[downs[j]])

        gathered = {1: -1, 2: -1, 3: -1, 4: -1}

        def ga(step, last):
            while gathered[step] < min(last, iz - 1):
                gathered[step] += 1
                (e1, e2, e3, e4)[step - 1](gathered[step])

        def gstep(k, l1=1, l2=1):
            ga(1, k + l1 + l2)
            ga(2, k + l2)
            ga(3, k)
            ga(4, k - 1)

        done = {1: 0, 2: 0, 3: 0, 4: 0}

        def zf1():
            w = reduce[0][1]
            for j in (1, 2, 3):
                send(("z1", j), G[0].at[ups[j]], RZ.at[j - 1, :, :, 0:w], dev_up[j])

        def zf2():
            dev_a, pa, dev_b, pb = way(reduce[0][0], 1)
            w = reduce[0][1]
            for j in (1, 2, 3):
                got(("z1", j), RZ.at[j - 1, :, :, 0:w])

            def one(k):
                total = G[0][g, k].astype(F32)
                for j in range(3):
                    total = total + RZ[j, k, :, 0:w].astype(F32)
                G[0][g, k] = total.astype(BF16)

            loop(4, one)
            for n, q in ((0, pab), (1, pb)):
                send(("z2", n), G[0].at[g, q], RY.at[n, :, 0:w], dev_b)

        def zf3():
            dev_a, pa, dev_b, pb = way(reduce[0][0], 1)
            w = reduce[0][1]
            got(("z2", 0), RY.at[0, :, 0:w])
            G[0][g, pa] = G[0][g, pa] + RY[0, :, 0:w]
            send(("z3", 0), G[0].at[g, pa], RY.at[2, :, 0:w], dev_a)
            got(("z2", 1), RY.at[1, :, 0:w])
            G[0][g, p] = G[0][g, p] + RY[1, :, 0:w]

        def zf4():
            w = reduce[0][1]
            got(("z3", 0), RY.at[2, :, 0:w])
            finish_chunk(0, G[0][g, p].astype(F32) + RY[2, :, 0:w].astype(F32))

        def f1(i):
            dev_a, pa, dev_b, pb = way(reduce[i][0], 1)
            w = reduce[i][1]
            k = i % RING
            for n, col in ((0, pab), (1, pb)):
                send(("f1", k, n), G[i].at[:, col], R1.at[k, n, :, :, 0:w], dev_b)

        def f2(i):
            dev_a, pa, dev_b, pb = way(reduce[i][0], 1)
            w = reduce[i][1]
            k = i % RING
            got(("f1", k, 0), R1.at[k, 0, :, :, 0:w])
            G[i][:, pa] = G[i][:, pa] + R1[k, 0, :, :, 0:w]
            send(("f2", k), G[i].at[:, pa], R2.at[k, :, :, 0:w], dev_a)
            got(("f1", k, 1), R1.at[k, 1, :, :, 0:w])
            G[i][:, p] = G[i][:, p] + R1[k, 1, :, :, 0:w]

        def f3(i):
            dev_a, pa, dev_b, pb = way(reduce[i][0], 1)
            w = reduce[i][1]
            k = i % RING
            got(("f2", k), R2.at[k, :, :, 0:w])
            G[i][:, p] = G[i][:, p] + R2[k, :, :, 0:w]
            for j in (1, 2, 3):
                send(("f3", k, j), G[i].at[ups[j], p], R3.at[k, j - 1, :, 0:w], dev_up[j])

        def f4(i):
            w = reduce[i][1]
            k = i % RING
            total = G[i][g, p].astype(F32)
            for j in (1, 2, 3):
                got(("f3", k, j), R3.at[k, j - 1, :, 0:w])
                total = total + R3[k, j - 1, :, 0:w].astype(F32)
            finish_chunk(i, total)

        def finish_chunk(i, total):
            w, at = reduce[i][1], offsets[i]
            FS[:, :, at : at + w] = total.reshape(2, rows, w)
            local_pending.append(local(FS.at[c, :, at : at + w], go.at[c, :, at : at + w]))
            send(("f4", i), FS.at[o, :, at : at + w], go.at[c, :, at : at + w], partner)

        stages = {1: f1, 2: f2, 3: f3, 4: f4}

        def go_to(stage, last):
            while done[stage] < last:
                i = done[stage] + 1
                if stage < 4 and i >= RING // 2:
                    go_to(stage + 1, i - RING // 2)
                if stage > 1:
                    go_to(stage - 1, i)
                stages[stage](i)
                done[stage] = i

        def loop(n, body):
            def step(i, carry):
                body(i)
                return carry

            lax.fori_loop(0, n, step, 0)

        def put_grad(i, lhs_t, rhs):
            w = reduce[i][1]

            def one(k):
                a = lhs_t[pl.ds(pl.multiple_of(k * quarter, quarter), quarter), :]
                G[i][k] = nn(a, rhs()).astype(BF16).reshape(4, rows2, w)

            loop(4, one)

        def weight(i, at, w):
            return W[i][:, :, :, at : at + w].reshape(width, w)

        def transpose_in(src, dst, b):
            def one(k):
                at = pl.multiple_of(k * quarter, quarter)
                dst[pl.ds(at, quarter), pl.ds(pl.multiple_of(b * block, block), block)] = (
                    src[b, :, pl.ds(at, quarter)].T
                )

            loop(4, one)

        step_rows = 16
        iq, iv, io = gi["qk"], gi["v"], gi["out"]

        def gains():
            for k in range(8):
                kg, kx = k // 2, k % 2
                acc = None
                for ky in range(2):
                    for kc in range(2):
                        t = W[0][kg, 2 * kx + ky, 16 * kc : 16 * kc + 16, :].astype(F32)
                        acc = t if acc is None else acc + t
                GROW[:, LANES * k : LANES * (k + 1)] = acc[:8]
            GACC[...] = jnp.zeros_like(GACC)

            GACC[...] = jnp.zeros_like(GACC)

        def norm_one(r):
            at = pl.multiple_of(r * step_rows, step_rows)
            for b in range(2):
                xs = X[b, pl.ds(at, step_rows), :].astype(F32)
                r1 = lax.rsqrt(jnp.mean(xs * xs, axis=-1, keepdims=True) + EPS)
                NB[b, pl.ds(at, step_rows), :] = (xs * r1 * GROW[0:1, :]).astype(BF16)

        def first_norm():
            loop(block // step_rows, norm_one)
            transpose_in(NB, N1T, 0)
            transpose_in(NB, N1T, 1)

        def qkv():
            both = NB[...].reshape(2 * block, width)
            t = nn(both, weight(iq, 0, 2 * QH))
            for b in range(2):
                QK[b] = t[block * b : block * (b + 1)].T
            for at, w in tiles_of(VH):
                t = nn(both, weight(iv, at, w))
                for b in range(2):
                    VT[b, at : at + w, :] = t[block * b : block * (b + 1)].T.astype(BF16)

        lane = lax.broadcasted_iota(jnp.int32, (FEATS, LANES), 1)

        def place(i):
            b = i // PAIRS
            hp = lax.rem(i, PAIRS)
            return b, hp

        def slot(hp):
            return pl.ds(pl.multiple_of(FEATS * hp, FEATS), FEATS)

        def q_rows(b, hp, e):
            return QK[b, pl.ds(pl.multiple_of(hp * 2 * FDIM + e * FDIM, FDIM), FDIM), :]

        def k_rows(b, hp, e):
            return QK[b, pl.ds(pl.multiple_of(QH + hp * 2 * FDIM + e * FDIM, FDIM), FDIM), :]

        def v_slice(hp):
            return pl.ds(pl.multiple_of(hp * 2 * VDIM, 2 * VDIM), 2 * VDIM)

        def head_slice(hp, e):
            return pl.ds(pl.multiple_of(hp * 2 * VDIM + e * VDIM, VDIM), VDIM)

        def put_state(i, f0, f1, right_side, w0, w1):
            low = nt(f0, right_side)
            high = nt(f1, right_side)
            b, hp = place(i)
            ST[b, slot(hp), :] = jnp.where(lane < VDIM, low, high).astype(BF16)
            for e, t in ((0, w0), (1, w1)):
                WACC[b, pl.ds(2 * hp + e, 1), :] = t[0:1, :LANES]
                WACC[b, pl.ds(HALF_HEADS + 2 * hp + e, 1), 0 : FEATS - LANES] = t[0:1, LANES:]

        def state_step(i):
            b, hp = place(i)
            fs = [features(k_rows(b, hp, e)) for e in range(2)]
            ws = [nt(jnp.ones((8, block), BF16), f) for f in fs]
            put_state(i, fs[0], fs[1], VT[b, v_slice(hp), :], ws[0], ws[1])

        def states():
            WACC[...] = jnp.zeros_like(WACC)
            loop(2 * PAIRS, state_step)
            ST[:, COUNTS:, :] = WACC[...].astype(BF16)

        ranks = (hi, n_hi - 1 - hi)
        firsts = (x == 0, x == 1)
        doubling = n_hi == 4

        def away(n, j):
            t = hi + j if n == 0 else hi - j
            return dev(jnp.clip(t, 0, n_hi - 1), x, y, c)

        def state_rows(body):
            def step(i, z):
                body(pl.ds(pl.multiple_of(i * 16, 16), 16))
                return z

            lax.fori_loop(0, STATE_STEPS, step, 0)

        def start_split(d, key, src, dst, to):
            i = number(key)
            for lo in range(0, STATE, SPLIT):
                rr = pl.ds(lo, min(SPLIT, STATE - lo))
                pltpu.make_async_remote_copy(
                    src_ref=src.at[rr],
                    dst_ref=dst.at[rr],
                    send_sem=ss.at[i],
                    recv_sem=rs.at[i],
                    device_id=to,
                    device_id_type=MESH,
                ).start()
            return d

        def send_split(key, src, dst, to):
            pending[key] = start_split(remote(key, src, dst, to), key, src, dst, to)

        def state_x(n):
            send_split(("sx", n), ST.at[1 - x], SA.at[n], dev_x)

        def near(n):
            return remote(("sz", n, 0), TZ, SZ.at[n, 0], away(n, 1))

        def far(n, j):
            return remote(("sz", n, j), TY, SZ.at[n, 1], away(n, j))

        def near_sends(n):
            return lax.rem(ranks[n], 2) == 0 if doubling else ranks[n] < n_hi - 1

        def near_gets(n):
            return lax.rem(ranks[n], 2) == 1 if doubling else ranks[n] > 0

        def state_z(n):
            got(("sx", n), SA.at[n])
            for j in range(3):
                number(("sz", n, j))

            @pl.when(jnp.logical_not(near_gets(n)))
            def _():
                SZ[n, 0] = jnp.zeros((STATE, LANES), BF16)

            @pl.when(ranks[n] < 2 if doubling else ranks[n] >= 0)
            def _():
                SZ[n, 1] = jnp.zeros((STATE, LANES), BF16)

            if not doubling:

                @pl.when(near_gets(n))
                def _():
                    got(("sz", n, 0), SZ.at[n, 0])

            def add(r):
                t = ST[x, r, :].astype(F32) + SA[n, r, :].astype(F32)
                if not doubling:
                    t = t + SZ[n, 0, r, :].astype(F32)
                TZ[r, :] = t.astype(BF16)

            state_rows(add)
            pl.when(near_sends(n))(
                lambda: start_split(near(n), ("sz", n, 0), TZ, SZ.at[n, 0], away(n, 1)) and None
            )

        def state_far(n):
            if not doubling:
                return

            @pl.when(ranks[n] == 1)
            def _():
                got(("sz", n, 0), SZ.at[n, 0])

                def add(r):
                    TY[r, :] = (TZ[r, :].astype(F32) + SZ[n, 0, r, :].astype(F32)).astype(BF16)

                state_rows(add)
                for j in (1, 2):
                    start_split(far(n, j), ("sz", n, j), TY, SZ.at[n, 1], away(n, j))

        def state_end(n, dst):
            if doubling:

                @pl.when(ranks[n] == 3)
                def _():
                    got(("sz", n, 0), SZ.at[n, 0])
                    got(("sz", n, 2), SZ.at[n, 1])

                @pl.when(ranks[n] == 2)
                def _():
                    got(("sz", n, 1), SZ.at[n, 1])

            def add(r):
                total = SZ[n, 0, r, :].astype(F32) + SZ[n, 1, r, :].astype(F32)
                mine = ST[x, r, :].astype(F32)
                other = SA[n, r, :].astype(F32)
                dst[x, r, :] = (total + jnp.where(firsts[n], 0.0, other)).astype(BF16)
                SB[r, :] = (total + jnp.where(firsts[n], mine, 0.0)).astype(BF16)

            state_rows(add)
            send_split(("sy", n), SB, dst.at[x], dev_x)

        def state_got(n, dst):
            got(("sy", n), dst.at[1 - x])

        def state_sent(n):
            sent(("sx", n))
            sent(("sy", n))
            pl.when(near_sends(n))(lambda: near(n).wait_send())
            if doubling:

                @pl.when(ranks[n] == 1)
                def _():
                    far(n, 1).wait_send()
                    far(n, 2).wait_send()

        def score_z(b, hp, e):
            qh, ql = split_low(q_rows(b, hp, e))
            kh, kl = split_low(k_rows(b, hp, e))
            return tn(jnp.concatenate([kh, kh, kl], axis=0), jnp.concatenate([qh, ql, qh], axis=0))

        def counts(buf, b):
            return buf[b, COUNTS:, :]

        def count_dot(t, f, at):
            r = nn(t[:HALF_HEADS], f[:LANES]) + nn(t[HALF_HEADS:, : FEATS - LANES], f[LANES:])
            spot = lax.broadcasted_iota(jnp.int32, r.shape, 0)
            return jnp.sum(jnp.where(spot == at, r, 0.0), axis=0, keepdims=True)

        def count_outer(t, row, at):
            spot = lax.broadcasted_iota(jnp.int32, (16, block), 0)
            first = jnp.where(spot == at, row, 0.0).astype(BF16)
            second = jnp.where(spot == HALF_HEADS + at, row, 0.0).astype(BF16)
            return jnp.concatenate([tn(t, first), tn(t[:, : FEATS - LANES], second)], axis=0)

        def att_step(i):
            b, hp = place(i)
            turned = PB[b, slot(hp), :].astype(F32).T.astype(BF16)
            tops = []
            for e in range(2):
                z = score_z(b, hp, e)
                st = (1.0 + z * FDIM**-0.5 + z * z * (0.5 / FDIM)).astype(BF16)
                fq = weighted(features(q_rows(b, hp, e)))
                num = nn(VT[b, head_slice(hp, e), :], st) + nn(turned[VDIM * e : VDIM * (e + 1)], fq)
                den = jnp.sum(st.astype(F32), axis=0, keepdims=True) + count_dot(counts(PB, b), fq, 2 * hp + e)
                NUM[b, head_slice(hp, e), :] = num
                DEN[i, e : e + 1, :] = den
                tops.append(num / den)
            ATT[b, :, v_slice(hp)] = jnp.concatenate(tops, axis=0).T.astype(BF16)

        def pairs(body, lo, n):
            def step(i, z):
                body(lo + i)
                return z

            lax.fori_loop(0, n, step, 0)

        def attention(lo, n):
            pairs(att_step, lo, n)

        def col(k):
            return pl.ds(pl.multiple_of(k * quarter, quarter), quarter)

        def wrow(i, k, at, w):
            return W[i][k, :, :, at : at + w].reshape(quarter, w)

        def out_proj(dst, b):
            def one(k):
                dst[:, col(k)] = nt(ATT[b], wrow(io, k, 0, VH))

            loop(4, one)

        def proj_send():
            out_proj(SND.at[0], o)
            send("x1", SND.at[0], RCV.at[0], partner)

        def norm_two(r):
            at = pl.multiple_of(r * step_rows, step_rows)
            rr = pl.ds(at, step_rows)
            x1 = X[c, rr, :].astype(F32) + (OWN[rr, :] + RCV[0, rr, :])
            X1[rr, :] = x1
            r2 = lax.rsqrt(jnp.mean(x1 * x1, axis=-1, keepdims=True) + EPS)
            NB[c, rr, :] = (x1 * r2 * GROW[1:2, :]).astype(BF16)

        def proj_own():
            out_proj(OWN, c)

        def second_norm():
            got("x1", RCV.at[0])
            loop(block // step_rows, norm_two)
            send("n2", NB.at[c], NB.at[c], partner)
            transpose_in(NB, N2T, c)

        def second_norm_in():
            got("n2", NB.at[o])
            transpose_in(NB, N2T, o)

        def ffn_in(j):
            base, w = parts[j]
            for at, tw in tiles_of(w):
                TG[:, 0:tw] = nn(NB[...].reshape(2 * block, width), weight(gi[f"g{j}"], at, tw))
                TU[:, 0:tw] = nn(NB[...].reshape(2 * block, width), weight(gi[f"u{j}"], at, tw))
                lo = base + at

                def one(r):
                    rr = pl.ds(pl.multiple_of(r * 64, 64), 64)
                    gate, up = TG[rr, 0:tw], TU[rr, 0:tw]
                    sg = 0.5 + 0.5 * jnp.tanh(0.5 * gate)
                    silu = gate * sg
                    HID[rr, lo : lo + tw] = (silu * up).astype(BF16)
                    CA[rr, lo : lo + tw] = (up * sg * (1.0 + gate * (1.0 - sg))).astype(BF16)
                    CB[rr, lo : lo + tw] = silu.astype(BF16)

                loop(2 * block // 64, one)
        def ffn_back(j):
            base, w = parts[j]
            i = gi[f"d{j}"]
            for at, tw in tiles_of(w):
                TG[:, 0:tw] = nn(DY[...].reshape(2 * block, width), weight(i, at, tw))
                lo = base + at

                def one(r):
                    rr = pl.ds(pl.multiple_of(r * 64, 64), 64)
                    dh = TG[rr, 0:tw]
                    CA[rr, lo : lo + tw] = (dh * CA[rr, lo : lo + tw].astype(F32)).astype(BF16)
                    CB[rr, lo : lo + tw] = (dh * CB[rr, lo : lo + tw].astype(F32)).astype(BF16)

                loop(2 * block // 64, one)

        def tokens_of(b):
            return pl.ds(pl.multiple_of(b * block, block), block)

        def dn2(dst, b):
            def one(k):
                acc = None
                for j, (base, w) in enumerate(parts):
                    for buf, i in ((CA, gi[f"g{j}"]), (CB, gi[f"u{j}"])):
                        t = nt(buf[tokens_of(b), base : base + w], wrow(i, k, 0, w))
                        acc = t if acc is None else acc + t
                dst[:, col(k)] = acc

            loop(4, one)

        def dn2_send():
            sent("x1")
            dn2(SND.at[0], o)
            send("dn2", SND.at[0], RCV.at[1], partner)

        def dn2_own():
            dn2(OWN, c)

        def norm_two_back(r):
            at = pl.multiple_of(r * step_rows, step_rows)
            rr = pl.ds(at, step_rows)
            d = OWN[rr, :] + RCV[1, rr, :]
            x1 = X1[rr, :]
            r2 = lax.rsqrt(jnp.mean(x1 * x1, axis=-1, keepdims=True) + EPS)
            t = d * (x1 * r2)
            GACC[8:16, :] += t[:8] + t[8:]
            a2 = d * GROW[1:2, :]
            dx = DY[c, rr, :].astype(F32) + (
                r2 * a2 - x1 * (r2 * r2 * r2) * jnp.mean(a2 * x1, axis=-1, keepdims=True)
            )
            din_ref[rr, :] = dx
            NB[c, rr, :] = dx.astype(BF16)

        def second_norm_back():
            got("dn2", RCV.at[1])
            sent("n2")
            loop(block // step_rows, norm_two_back)
            send("dx1", NB.at[c], NB.at[c], partner)
            transpose_in(NB, DYT, c)

        def datt():
            got("dx1", NB.at[o])
            transpose_in(NB, DYT, o)
            for at, tw in tiles_of(VH):
                t = nn(NB[...].reshape(2 * block, width), weight(io, at, tw))
                for b in range(2):
                    DATT[b, at : at + tw, :] = t[block * b : block * (b + 1)].T

        def back_state_step(i):
            b, hp = place(i)
            fs, ws = [], []
            for e in range(2):
                hs = head_slice(hp, e)
                datt, num, den = DATT[b, hs, :], NUM[b, hs, :], DEN[i, e : e + 1, :]
                dd = (-jnp.sum(datt * num, axis=0, keepdims=True) / (den * den)).astype(BF16)
                DNUM[b, hs, :] = (datt / den).astype(BF16)
                DDEN[i, e : e + 1, :] = dd.astype(F32)
                f = features(q_rows(b, hp, e))
                fs.append(f)
                ws.append(nt(jnp.broadcast_to(dd, (8, block)), f))
            put_state(i, fs[0], fs[1], DNUM[b, v_slice(hp), :], ws[0], ws[1])

        def back_states():
            WACC[...] = jnp.zeros_like(WACC)
            state_sent(0)
            loop(2 * PAIRS, back_state_step)
            ST[:, COUNTS:, :] = WACC[...].astype(BF16)

        zeros_head = jnp.zeros((VDIM, block), BF16)

        def masked(t, e):
            return jnp.concatenate([zeros_head, t] if e else [t, zeros_head], axis=0)

        def back_step(i):
            b, hp = place(i)
            for e in range(2):
                hs = head_slice(hp, e)
                q, kk = q_rows(b, hp, e), k_rows(b, hp, e)
                qh, ql = split_low(q)
                kh, kl = split_low(kk)
                z = tn(jnp.concatenate([kh, kh, kl], axis=0), jnp.concatenate([qh, ql, qh], axis=0))
                st = (1.0 + z * FDIM**-0.5 + z * z * (0.5 / FDIM)).astype(BF16)
                dnum, dden = DNUM[b, hs, :], DDEN[i, e : e + 1, :]
                ds = (tn(VT[b, hs, :], dnum) + dden).astype(BF16).astype(F32)
                dz = (ds * (FDIM**-0.5 + z * (1.0 / FDIM))).astype(BF16)
                t = nn(jnp.concatenate([kh, kl], axis=0), dz)
                dq = t[:FDIM] + t[FDIM:]
                t = nt(jnp.concatenate([qh, ql], axis=0), dz)
                dk = t[:FDIM] + t[FDIM:]
                DV[b, hs, :] = nt(dnum, st)
                df = nn(PB[b, slot(hp), :], masked(dnum, e)) + count_outer(counts(PB, b), dden, 2 * hp + e)
                DQK[b, pl.ds(pl.multiple_of(hp * 2 * FDIM + e * FDIM, FDIM), FDIM), :] = dq + features_back(q, df)
                DQK[b, pl.ds(pl.multiple_of(QH + hp * 2 * FDIM + e * FDIM, FDIM), FDIM), :] = dk

        def back_rows(lo, n):
            pairs(back_step, lo, n)

        def y_part(dst, b):
            def one(k):
                acc = None
                for j, (base, w) in enumerate(parts):
                    t = nt(HID[tokens_of(b), base : base + w], wrow(gi[f"d{j}"], k, 0, w))
                    acc = t if acc is None else acc + t
                dst[:, col(k)] = acc

            loop(4, one)

        def finish(r):
            rr = pl.ds(pl.multiple_of(r * step_rows, step_rows), step_rows)
            out_ref[rr, :] = (X1[rr, :] + (OWN[rr, :] + RCV[2, rr, :])).astype(BF16)

        def y_send():
            y_part(SND.at[1], o)
            send("y", SND.at[1], RCV.at[2], partner)

        def y_own():
            y_part(OWN, c)

        def y_end():
            got("y", RCV.at[2])
            loop(block // step_rows, finish)

        def key_step(i):
            b, hp = place(i)
            turned = PX[b, slot(hp), :].astype(F32).T.astype(BF16)
            for e in range(2):
                hs = head_slice(hp, e)
                kk = k_rows(b, hp, e)
                df = nn(PX[b, slot(hp), :], masked(VT[b, hs, :], e)) + count_outer(
                    counts(PX, b), jnp.ones((1, block), F32), 2 * hp + e
                )
                kr = pl.ds(pl.multiple_of(QH + hp * 2 * FDIM + e * FDIM, FDIM), FDIM)
                DQK[b, kr, :] += features_back(kk, df)
                DV[b, hs, :] += nn(turned[VDIM * e : VDIM * (e + 1)], weighted(features(kk)))

        def keys_back(lo, n):
            pairs(key_step, lo, n)

        def dqkv():
            for b in range(2):
                DQKV[b, :, 0 : 2 * QH] = DQK[b].T.astype(BF16)
                for at, tw in tiles_of(VH):
                    DQKV[b, :, 2 * QH + at : 2 * QH + at + tw] = DV[b, at : at + tw, :].T.astype(BF16)

        def dn1(dst, b):
            def one(k):
                dst[:, col(k)] = nt(DQKV[b, :, : 2 * QH], wrow(iq, k, 0, 2 * QH)) + nt(
                    DQKV[b, :, 2 * QH :], wrow(iv, k, 0, VH)
                )

            loop(4, one)

        def dn1_send():
            sent("dn2")
            dn1(SND.at[0], o)
            send("dn1", SND.at[0], RCV.at[0], partner)

        def dn1_own():
            dn1(OWN, c)

        def norm_one_back(r):
            rr = pl.ds(pl.multiple_of(r * step_rows, step_rows), step_rows)
            d = OWN[rr, :] + RCV[0, rr, :]
            xs = X[c, rr, :].astype(F32)
            r1 = lax.rsqrt(jnp.mean(xs * xs, axis=-1, keepdims=True) + EPS)
            t = d * (xs * r1)
            GACC[0:8, :] += t[:8] + t[8:]
            a1 = d * GROW[0:1, :]
            din_ref[rr, :] += r1 * a1 - xs * (r1 * r1 * r1) * jnp.mean(a1 * xs, axis=-1, keepdims=True)

        def first_norm_back():
            got("dn1", RCV.at[0])
            loop(block // step_rows, norm_one_back)
            sum_a = jnp.sum(GACC[0:8, :], axis=0, keepdims=True)
            gf = jnp.sum(GACC[8:16, :], axis=0, keepdims=True)
            last = ri["gain"]
            for k in range(4):
                row = lax.broadcasted_iota(jnp.int32, (LANES, quarter), 0)
                sl = slice(quarter * k, quarter * (k + 1))
                mat = jnp.where(row == 0, sum_a[:, sl], 0.0) + jnp.where(row == 1, gf[:, sl], 0.0)
                G[last][k] = mat.T.astype(BF16).reshape(4, rows2, LANES)
        def part_of(buf, j):
            base, w = parts[j]
            return lambda: buf[:, base : base + w]

        def grad(name):
            kind = name.rstrip("0123456789")
            if kind == "d":
                put_grad(ri[name], DYT, part_of(HID, int(name[1:])))
            elif kind == "g":
                put_grad(ri[name], N2T, part_of(CA, int(name[1:])))
            elif kind == "u":
                put_grad(ri[name], N2T, part_of(CB, int(name[1:])))
            elif name == "out":
                put_grad(ri[name], DYT, lambda: ATT[...].reshape(2 * block, VH))
            elif name == "qk":
                put_grad(ri[name], N1T, lambda: DQKV[:, :, 0 : 2 * QH].reshape(2 * block, 2 * QH))
            elif name == "v":
                put_grad(ri[name], N1T, lambda: DQKV[:, :, 2 * QH :].reshape(2 * block, VH))

        def adv(st, name):
            go_to(st, ri[name])

        def greeted():
            pl.semaphore_wait(barrier, len(greet))
            if members > 1:

                @pl.when(hi < n_hi - 1)
                def _():
                    pl.semaphore_wait(barrier, 1)

                @pl.when(hi > 0)
                def _():
                    pl.semaphore_wait(barrier, 1)

        cx = local(tok, X.at[c])
        cy = local(cot, DY.at[c])
        for i in range(len(gather)):
            e0(i)
        cx.wait()
        cy.wait()
        greeted()

        for i in range(len(gather)):
            e0_send(i)
        send("x", X.at[c], X.at[c], partner)
        send("dy", DY.at[c], DY.at[c], partner)
        z1()
        ga(1, 0)
        ga(1, 1)
        ga(2, 0)
        ga(1, 2)
        ga(2, 1)
        ga(3, 0)
        z2()
        transpose_in(DY, DYT, c)
        got("x", X.at[o])
        got("dy", DY.at[o])
        transpose_in(DY, DYT, o)
        ga(1, 3)
        ga(1, 4)
        ga(2, 2)
        ga(3, 1)
        ga(4, 0)
        ga(1, 5)
        ga(1, 6)
        gains()
        first_norm()
        ga(2, 3)
        ga(3, 2)
        ga(2, 4)
        ga(4, 1)
        ga(4, 2)
        qkv()
        states()
        state_x(0)
        ga(1, 7)
        ga(1, 8)
        ga(1, 9)
        ga(1, 10)
        ga(1, 11)
        ga(2, 5)
        ga(2, 6)
        ga(3, 3)
        state_z(0)
        ga(2, 7)
        ga(3, 4)
        state_far(0)
        ga(2, 8)
        ga(3, 5)
        state_end(0, PB)
        ga(2, 9)
        ga(3, 6)
        state_got(0, PB)
        ga(3, 7)
        z3()
        attention(0, 4)
        attention(4, 4)
        ga(2, 10)
        ga(3, 8)
        ga(4, 3)
        proj_send()
        proj_own()
        second_norm()
        second_norm_in()
        ga(2, 11)
        ga(3, 9)
        ga(4, 4)
        ga(4, 5)
        ffn_in(0)
        grad("d0")
        zf1()
        ga(3, 10)
        ga(4, 6)
        ga(4, 7)
        ffn_in(1)
        grad("d1")
        go_to(1, 1)
        ga(3, 11)
        ga(4, 8)
        ga(4, 9)
        ffn_in(2)
        grad("d2")
        go_to(1, 2)
        z4()
        ffn_back(0)
        go_to(2, 1)
        grad("g0")
        go_to(1, 3)
        ga(4, 10)
        ffn_back(1)
        go_to(2, 2)
        go_to(3, 1)
        grad("u0")
        go_to(1, 4)
        ga(4, 11)
        ffn_back(2)
        dn2_send()
        go_to(2, 3)
        dn2_own()
        go_to(3, 2)
        grad("g1")
        go_to(1, 5)
        second_norm_back()
        datt()
        go_to(2, 4)
        back_states()
        state_x(1)
        go_to(3, 3)
        go_to(4, 1)
        grad("u1")
        go_to(4, 2)
        go_to(1, 6)
        state_z(1)
        go_to(2, 5)
        go_to(3, 4)
        zf2()
        go_to(4, 3)
        back_rows(0, 4)
        grad("g2")
        go_to(1, 7)
        state_far(1)
        go_to(2, 6)
        go_to(3, 5)
        go_to(4, 4)
        back_rows(4, 4)
        grad("u2")
        go_to(1, 8)
        zf3()
        state_end(1, PX)
        go_to(2, 7)
        go_to(3, 6)
        go_to(4, 5)
        grad("out")
        go_to(1, 9)
        y_send()
        y_own()
        zf4()
        state_got(1, PX)
        keys_back(0, 4)
        keys_back(4, 4)
        dqkv()
        grad("qk")
        go_to(2, 8)
        go_to(3, 7)
        go_to(4, 6)
        go_to(1, 10)
        y_end()
        dn1_send()
        grad("v")
        go_to(1, 11)
        dn1_own()
        go_to(2, 9)
        go_to(3, 8)
        go_to(4, 7)
        first_norm_back()
        go_to(1, 12)
        go_to(2, 10)
        go_to(3, 9)
        go_to(4, 8)
        go_to(2, 11)
        go_to(3, 10)
        go_to(4, 9)
        go_to(2, 12)
        go_to(3, 11)
        go_to(4, 10)
        go_to(3, 12)
        go_to(4, 11)
        go_to(4, 12)

        n = len(reduce)
        for i in range(n):
            got(("f4", i), go.at[o, :, offsets[i] : offsets[i] + reduce[i][1]])
        for d in local_pending:
            d.wait()
        state_sent(1)
        for d in pending.values():
            d.wait_send()

    return kernel


def call_kernel(tok, cot, shards, seq_size, ff, ff_half):
    block, width = tok.shape
    gather, reduce = plan(ff_half)
    rows = width // 32
    vmem = pltpu.VMEM
    any_spec = pl.BlockSpec(memory_space=pl.ANY)
    vmem_spec = pl.BlockSpec(memory_space=vmem)
    total_width = sum(w for _, w in reduce)
    pack_width = sum(w for _, w in gather)
    state = vmem((2, STATE, LANES), BF16)
    scratch = [vmem((4, 4, 2 * (16 if name == "gain" else rows), w), BF16) for name, w in gather]
    scratch += [vmem((4, 4, 2 * rows, w), BF16) for _, w in reduce]
    scratch += [
        vmem((rows, pack_width), BF16),
        vmem((RING, 2, 4, 2 * rows, PIECE), BF16),
        vmem((RING, 4, 2 * rows, PIECE), BF16),
        vmem((RING, 3, 2 * rows, PIECE), BF16),
        vmem((3, 4, 2 * rows, PIECE), BF16),
        vmem((3, 2 * rows, PIECE), BF16),
        vmem((2, rows, total_width), F32),
        vmem((2, block, width), BF16),
        vmem((2, block, width), BF16),
        vmem((2, block, width), BF16),
        vmem((width, 2 * block), BF16),
        vmem((width, 2 * block), BF16),
        vmem((width, 2 * block), BF16),
        vmem((2 * block, ff_half), BF16),
        vmem((2 * block, ff_half), BF16),
        vmem((2 * block, ff_half), BF16),
        vmem((block, width), F32),
        vmem((2, block, width), F32),
        vmem((3, block, width), F32),
        vmem((block, width), F32),
        vmem((2, VH, block), F32),
        vmem((2, VH, block), F32),
        vmem((2, 2 * QH, block), F32),
        vmem((2, VH, block), BF16),
        vmem((2, block, VH), BF16),
        vmem((2 * PAIRS, 8, block), F32),
        vmem((2, VH, block), BF16),
        vmem((2 * PAIRS, 8, block), F32),
        vmem((2, 2 * QH, block), F32),
        vmem((2, VH, block), F32),
        vmem((2, block, 2 * QH + VH), BF16),
        state,
        vmem((2, STATE, LANES), BF16),
        vmem((2, 2, STATE, LANES), BF16),
        vmem((STATE, LANES), BF16),
        vmem((STATE, LANES), BF16),
        vmem((STATE, LANES), BF16),
        state,
        state,
        vmem((2, 16, LANES), F32),
        vmem((2 * block, 256), F32),
        vmem((2 * block, 256), F32),
        vmem((8, width), F32),
        vmem((16, width), F32),
        pltpu.SemaphoreType.DMA((n_messages(gather, reduce),)),
        pltpu.SemaphoreType.DMA((n_messages(gather, reduce),)),
        pltpu.SemaphoreType.DMA((2 + len(reduce),)),
    ]
    out_shape = [
        jax.ShapeDtypeStruct((block, width), BF16),
        jax.ShapeDtypeStruct((block, width), F32),
        jax.ShapeDtypeStruct((2, rows, total_width), F32),
    ]
    return pl.pallas_call(
        make_kernel(seq_size, block, width, ff, ff_half),
        out_shape=out_shape,
        in_specs=[any_spec] * 2 + [vmem_spec] * len(shards),
        out_specs=[vmem_spec] * 2 + [any_spec],
        scratch_shapes=scratch,
        compiler_params=pltpu.CompilerParams(
            collective_id=0, has_side_effects=True, vmem_limit_bytes=62 * 2**20
        ),
    )(tok, cot, *shards)


def n_messages(gather, reduce):
    return 7 * len(gather) + 24


def call_finish(output, input_grad, grads, ff, ff_half):
    block, width = output.shape
    rows = grads.shape[1]
    _, reduce = plan(ff_half)
    at = dict(zip([name for name, _ in reduce], offsets_of(reduce)))
    parts = pieces_of(ff_half)
    vmem_spec = pl.BlockSpec(memory_space=pltpu.VMEM)
    hbm_spec = pl.BlockSpec(memory_space=pltpu.HBM)

    def kernel(o_in, i_in, g_hbm, o_out, i_out, ag, qg, kg, vg, og, fg, gg, ug, dg, g_in, o_held, i_held, sems):
        c2 = pltpu.make_async_copy(g_hbm, g_in, sems.at[2])
        c2.start()
        c0 = pltpu.make_async_copy(i_in, i_held, sems.at[0])
        c1 = pltpu.make_async_copy(o_in, o_held, sems.at[1])
        c0.start()
        c1.start()
        c0.wait()
        c3 = pltpu.make_async_copy(i_held, i_out, sems.at[3])
        c3.start()
        c1.wait()
        c4 = pltpu.make_async_copy(o_held, o_out, sems.at[4])
        c4.start()
        c2.wait()
        gain = (g_in[0, :, at["gain"] : at["gain"] + LANES] + g_in[1, :, at["gain"] : at["gain"] + LANES]).T
        ag[...] = gain[0:1, :rows]
        fg[...] = gain[1:2, :rows]
        for h in range(2):
            qg[:, QH * h : QH * (h + 1)] = g_in[h, :, at["qk"] : at["qk"] + QH]
            kg[:, QH * h : QH * (h + 1)] = g_in[h, :, at["qk"] + QH : at["qk"] + 2 * QH]
            vg[:, VH * h : VH * (h + 1)] = g_in[h, :, at["v"] : at["v"] + VH]
            og[:, VH * h : VH * (h + 1)] = g_in[h, :, at["out"] : at["out"] + VH]
            for j, (base, w) in enumerate(parts):
                lo = ff_half * h + base
                have = min(w, ff - lo)
                for ref, letter in ((gg, "g"), (ug, "u"), (dg, "d")):
                    a = at[f"{letter}{j}"]
                    ref[:, lo : lo + have] = g_in[h, :, a : a + have]
        c3.wait()
        c4.wait()

    shapes = [(1, rows), (rows, 2 * QH), (rows, 2 * QH), (rows, 2 * VH), (rows, 2 * VH), (1, rows)] + [(rows, ff)] * 3
    return pl.pallas_call(
        kernel,
        out_shape=[jax.ShapeDtypeStruct(output.shape, BF16), jax.ShapeDtypeStruct(input_grad.shape, F32)]
        + [jax.ShapeDtypeStruct(n, F32) for n in shapes],
        in_specs=[hbm_spec] * 3,
        out_specs=[hbm_spec] * 2 + [vmem_spec] * len(shapes),
        scratch_shapes=[
            pltpu.VMEM(grads.shape, F32),
            pltpu.VMEM(output.shape, BF16),
            pltpu.VMEM(input_grad.shape, F32),
            pltpu.SemaphoreType.DMA((5,)),
        ],
        compiler_params=pltpu.CompilerParams(vmem_limit_bytes=60 * 2**20),
    )(output, input_grad, grads)


def body(
    tokens, attn_gain, query_weight, key_weight, value_weight, out_weight, ffn_gain, gate_weight, up_weight, down_weight, cotangent
):
    seq_size = lax.axis_size("seq")
    members = seq_size // 8
    _, block, width = tokens.shape
    ff = gate_weight.shape[1]
    ff_half = LANES * ((ff + 2 * LANES - 1) // (2 * LANES))
    few = attn_gain.shape[0]
    groups = [[(g * members + m) * 2 + x for m in range(members)] for g in range(4) for x in range(2)]

    shards = [attn_gain, query_weight, key_weight, value_weight, out_weight.T, ffn_gain, gate_weight, up_weight, down_weight.T]
    if members > 1:
        shards = [
            lax.all_gather(a, "seq", axis_index_groups=groups, axis=0, tiled=True) for a in shards
        ]
    shards = [a.reshape(1, -1) if a.ndim == 1 else a for a in shards]

    def turn(t):
        if members == 1:
            return t
        return t.reshape(block, 4, members, 2, 4, few).transpose(0, 1, 3, 4, 2, 5).reshape(block, width)

    def turn_back(t):
        if members == 1:
            return t
        return t.reshape(block, 4, 2, 4, members, few).transpose(0, 1, 4, 2, 3, 5).reshape(block, width)

    output, input_grad, grads = call_kernel(turn(tokens[0]), turn(cotangent[0]), shards, seq_size, ff, ff_half)
    if members == 1:
        o, i, ag, qg, kg, vg, og, fg, gg, ug, dg = call_finish(output, input_grad, grads, ff, ff_half)
        return o[None], i[None], ag[0], qg, kg, vg, og.T, fg[0], gg, ug, dg.T
    grads = lax.psum_scatter(grads, "seq", scatter_dimension=1, axis_index_groups=groups, tiled=True)
    _, reduce = plan(ff_half)
    by = {name: grads[:, :, a : a + w] for (name, w), a in zip(reduce, offsets_of(reduce))}
    n_parts = len(pieces_of(ff_half))

    def joined(a):
        return jnp.concatenate([a[0], a[1]], axis=1)

    def ff_joined(letter):
        return joined(jnp.concatenate([by[f"{letter}{j}"] for j in range(n_parts)], axis=2))[:, :ff]

    gain = by["gain"][0] + by["gain"][1]
    return (
        turn_back(output)[None],
        turn_back(input_grad)[None],
        gain[:, 0],
        joined(by["qk"][:, :, :QH]),
        joined(by["qk"][:, :, QH:]),
        joined(by["v"]),
        joined(by["out"]).T,
        gain[:, 1],
        ff_joined("g"),
        ff_joined("u"),
        ff_joined("d").T,
    )


def solution(mesh):
    both = ("seq", "dp")
    row, column, whole = P(both, None), P(None, both), P("dp", "seq", None)
    return jax.shard_map(
        body,
        mesh=mesh,
        in_specs=(whole, P(both), row, row, row, column, P(both), row, row, column, whole),
        out_specs=(whole, whole, P(both), row, row, row, column, P(both), row, row, column),
        check_vma=False,
    )
```
